32 devices in a mesh: ctx: 16 (over z, y, x), head: 2 (over core).
Axes of the slice: x: 2, y: 2, z: 4, core: 2. Of those that a mesh axis runs over, the one named last changes fastest.
Arguments:
- tokens: bfloat16 [2048, 4096], P('ctx'), may hold values from -6 to 6
- norm_gain: float32 [4096], replicated, may hold values from 0.1 to 1.9
- w_query: bfloat16 [4096, 4096], P('ctx', 'head')
- w_key: bfloat16 [4096, 1024], P('ctx', 'head'), may hold values from -0.09375 to 0.09375
- w_value: bfloat16 [4096, 1024], P('ctx', 'head'), may hold values from -0.09375 to 0.09375
- w_out: bfloat16 [4096, 4096], P('head', 'ctx'), may hold values from -0.5 to 0.5
- doc_starts: int32 [16], replicated, may hold values from 0 to 2047, as said below
Outputs:
- block_out: bfloat16 [2048, 4096], P('ctx', 'head')
The draws below stay inside these ranges and needn't reach their ends.
Inputs may be any that keep to these rules, and one draw needn't show every extreme that they name: doc_starts[0] is 0, the entries rise strictly, and the first document holds at least 1024 tokens.
All inputs are finite; a program needn't handle non-finite values.
Results may differ from the reference program's by a relative error of at most 0.02.
The reference program's roundings to bfloat16 on the way count: a program that leaves them out, or rounds other values in their place, can miss the bound.
Values may be sent and summed in bfloat16 or wider, within the bound.
No kernel may reach another device: no remote copies, remote signals or barrier semaphores. Data moves between devices by JAX's collectives and lax.ppermute only.
A program may use at most 128 MiB of HBM per device.

```python
import math
import jax
import jax.numpy as jnp
from jax import lax

D = 4096
KVH = 8
HD = 128
QH = 32
NDOCS = 16
TOKENS = 2048
N_HEAD = 2


def draw_w_query(key, part):
    values = jax.random.normal(jax.random.fold_in(key, 11), (D, QH * HD), jnp.float32) * D ** (-0.5)
    return values.astype(jnp.bfloat16)


def draw_doc_starts(key, part):
    second = jax.random.randint(jax.random.fold_in(key, 21), (1,), TOKENS // 2, 3 * TOKENS // 4)
    others = jnp.sort(jax.random.permutation(jax.random.fold_in(key, 22), TOKENS // 4)[:NDOCS - 2])
    return jnp.concatenate([jnp.zeros((1,), jnp.int32), second.astype(jnp.int32), (others + 3 * TOKENS // 4).astype(jnp.int32)])


def shard_levels(key, dims, shards, smallest, high):
    factor_of = 1.0
    for dim, parts in shards:
        draws = jax.random.uniform(jax.random.fold_in(jax.random.fold_in(key, 6), dim), (parts,), jnp.float32, smallest / len(shards), high / len(shards))
        factor_of = factor_of * jnp.repeat(jnp.exp(draws), dims[dim] // parts).reshape((-1,) + (1,) * (len(dims) - 1 - dim))
    return factor_of


def centred(own_key, shape, deviation, limit, cuts=(), kind=jnp.bfloat16):
    entries = deviation * jax.random.normal(own_key, shape, jnp.float32)
    if cuts:
        entries = entries * shard_levels(own_key, shape, cuts, -0.22, 0.18)
    return jnp.clip(entries, -limit, limit).astype(kind)


def setup_inputs(seed: int = 0) -> dict:
    arg_keys = jax.random.split(jax.random.key(seed), 8)
    return {
        "tokens": centred(arg_keys[0], (TOKENS, D), 1.0, 6.0, ((0, 16),)),
        "norm_gain": jnp.clip(1.0 + 0.18 * jax.random.normal(arg_keys[1], (D,), jnp.float32), 0.1, 1.9),
        "w_query": draw_w_query(jax.random.fold_in(arg_keys[7], 71), 0),
        "w_key": centred(arg_keys[3], (D, KVH * HD), D ** -0.5, 0.09375, ((0, 16), (1, 2))),
        "w_value": centred(arg_keys[4], (D, KVH * HD), D ** -0.5, 0.09375, ((0, 16), (1, 2))),
        "w_out": centred(arg_keys[5], (QH * HD, D), HD ** -0.5, 0.5, ((0, 2), (1, 16))),
        "doc_starts": draw_doc_starts(jax.random.fold_in(arg_keys[7], 71), 0),
    }


def rotate_heads(values, positions):
    half = values.shape[-1] // 2
    freqs = 500000.0 ** (-(jnp.arange(half, dtype=jnp.float32) * 2.0 / values.shape[-1]))
    angles = positions.astype(jnp.float32)[:, None] * freqs[None, :]
    cosine = jnp.cos(angles)[:, None, :]
    sine = jnp.sin(angles)[:, None, :]
    lower = values[..., :half]
    upper = values[..., half:]
    return jnp.concatenate([lower * cosine - upper * sine, upper * cosine + lower * sine], axis=-1)

def reference(tokens, norm_gain, w_query, w_key, w_value, w_out, doc_starts):
    source = tokens.astype(jnp.float32)
    normed = (source * lax.rsqrt(lax.optimization_barrier(jnp.mean(source * source, axis=1, keepdims=True)) + 1e-05) * norm_gain).astype(jnp.bfloat16)
    positions = jnp.arange(TOKENS, dtype=jnp.int32)
    query = jnp.dot(normed, w_query, preferred_element_type=jnp.float32).reshape(TOKENS, QH, HD)
    query = rotate_heads(query, positions).astype(jnp.bfloat16)
    key_proj = jnp.dot(normed, w_key, preferred_element_type=jnp.float32).reshape(TOKENS, KVH, HD)
    key_proj = rotate_heads(key_proj, positions).astype(jnp.bfloat16)
    value_proj = jnp.dot(normed, w_value, preferred_element_type=jnp.float32).astype(jnp.bfloat16).reshape(TOKENS, KVH, HD)
    doc_ids = lax.optimization_barrier(jnp.sum((doc_starts[None, :] <= positions[:, None]).astype(jnp.int32), axis=1)) - 1
    groups = QH // KVH
    qblock = math.gcd(TOKENS, 256)
    query_grouped = query.reshape(TOKENS, KVH, groups, HD)
    keys_wide = key_proj.astype(jnp.float32)
    values_wide = value_proj.astype(jnp.float32)
    score_scale = HD ** (-0.5)

    def one_block(block_index):
        first_row = (block_index * qblock).astype(jnp.int32)
        query_rows = lax.dynamic_slice_in_dim(query_grouped, first_row, qblock, 0).astype(jnp.float32)
        query_pos = first_row + jnp.arange(qblock, dtype=jnp.int32)
        query_doc = lax.dynamic_slice_in_dim(doc_ids, first_row, qblock, 0)
        scores = jnp.einsum('qhgd,khd->hgqk', query_rows, keys_wide) * score_scale
        visible = (doc_ids[None, :] == query_doc[:, None]) & (positions[None, :] <= query_pos[:, None])
        scores = jnp.where(visible[None, None], scores, -1e+30)
        highest = lax.optimization_barrier(jnp.max(scores, axis=-1))
        probs = jnp.where(visible[None, None], jnp.exp(scores - highest[..., None]), 0.0)
        denominator = lax.optimization_barrier(jnp.sum(probs, axis=-1))
        weights = lax.optimization_barrier(probs.astype(jnp.bfloat16)).astype(jnp.float32)
        mixed = jnp.einsum('hgqk,khd->hgqd', weights, values_wide) / denominator[..., None]
        mixed = jnp.transpose(mixed, (2, 0, 1, 3)).reshape(qblock, QH * HD)
        return mixed.astype(jnp.bfloat16)
    attended = lax.map(one_block, jnp.arange(TOKENS // qblock, dtype=jnp.int32)).reshape(TOKENS, QH * HD)
    group_width = QH * HD // N_HEAD
    summed = jnp.zeros((TOKENS, D), jnp.float32)
    for group in range(N_HEAD):
        partial_out = jnp.dot(attended[:, group * group_width:(group + 1) * group_width], w_out[group * group_width:(group + 1) * group_width], preferred_element_type=jnp.float32)
        summed = summed + lax.optimization_barrier(partial_out.astype(jnp.bfloat16)).astype(jnp.float32)
    return summed.astype(jnp.bfloat16)
```

```python
import functools

import jax
import jax.numpy as jnp
from jax import lax
from jax.experimental import pallas as pl
from jax.experimental.pallas import tpu as pltpu
from jax.sharding import Mesh
from jax.sharding import PartitionSpec as P

HD = 128
HALF = HD // 2


def rotary_tables(positions):
    freqs = 500000.0 ** (-(jnp.arange(HALF, dtype=jnp.float32) * 2.0 / HD))
    angles = positions.astype(jnp.float32)[:, None] * freqs[None, :]
    cosine = jnp.cos(angles)
    sine = jnp.sin(angles)
    return (
        jnp.concatenate([cosine, cosine], axis=1),
        jnp.concatenate([-sine, sine], axis=1),
    )


def rotate(values, cosine, sine):
    swapped = jnp.concatenate([values[:, HALF:], values[:, :HALF]], axis=1)
    return values * cosine + swapped * sine


def attention_kernel(blocks, n_query, n_kv, *refs):
    query_refs = refs[:n_query]
    cos_ref, sin_ref, qpos_ref, qstart_ref, kpos_ref = refs[n_query : n_query + 5]
    kv_refs = refs[n_query + 5 : n_query + 5 + n_kv]
    out_ref, rotated, bias = refs[n_query + 5 + n_kv :]
    heads, tokens, _ = rotated.shape
    cosine = cos_ref[...]
    sine = sin_ref[...]
    for h in range(heads):
        lanes = pl.ds(h * HD, HD)
        total = query_refs[0][:, lanes].astype(jnp.float32)
        for ref in query_refs[1:]:
            total = total + ref[:, lanes].astype(jnp.float32)
        turned = total * cosine + pltpu.roll(total, HALF, 1) * sine
        rotated[h] = turned.astype(jnp.bfloat16)
    rows = tokens // blocks
    kv_rows = kv_refs[0].shape[0]
    scale = HD**-0.5
    for j in range(blocks):
        first = j * rows
        length = kv_rows * (j + 1) // blocks
        qpos = qpos_ref[pl.ds(first, rows), :]
        qstart = qstart_ref[pl.ds(first, rows), :]
        for d in range(n_kv):
            kpos = kpos_ref[pl.ds(d, 1), pl.ds(0, length)]
            visible = (kpos <= qpos) & (kpos >= qstart)
            bias[:, pl.ds(d * length, length)] = jnp.where(visible, 0.0, -jnp.inf)

        def one_head(h, unused):
            query = rotated[h, pl.ds(first, rows), :]
            scores = []
            for d in range(n_kv):
                part = lax.dot_general(
                    query,
                    kv_refs[d][pl.ds(0, length), pl.ds(0, HD)],
                    (((1,), (1,)), ((), ())),
                    preferred_element_type=jnp.float32,
                )
                scores.append(part + bias[:, pl.ds(d * length, length)])
            highest = functools.reduce(
                jnp.maximum, [jnp.max(s, axis=1, keepdims=True) for s in scores]
            )
            denominator = 0.0
            mixed = 0.0
            for d in range(n_kv):
                probs = jnp.exp((scores[d] - highest) * scale)
                denominator = denominator + jnp.sum(probs, axis=1, keepdims=True)
                mixed = mixed + jnp.dot(
                    probs.astype(jnp.bfloat16),
                    kv_refs[d][pl.ds(0, length), pl.ds(HD, HD)],
                    preferred_element_type=jnp.float32,
                )
            lanes = pl.ds(pl.multiple_of(h * HD, HD), HD)
            out_ref[pl.ds(first, rows), lanes] = (mixed / denominator).astype(jnp.bfloat16)
            return unused

        lax.fori_loop(0, heads, one_head, 0)


def attention(query_parts, cosine, sine, qpos, qstart, kpos, kv_parts, blocks):
    tokens, width = query_parts[0].shape
    heads = width // HD
    keys = sum(part.shape[0] for part in kv_parts)
    return pl.pallas_call(
        functools.partial(attention_kernel, blocks, len(query_parts), len(kv_parts)),
        out_shape=jax.ShapeDtypeStruct((tokens, width), jnp.bfloat16),
        scratch_shapes=[
            pltpu.VMEM((heads, tokens, HD), jnp.bfloat16),
            pltpu.VMEM((tokens // blocks, keys), jnp.float32),
        ],
        compiler_params=pltpu.CompilerParams(vmem_limit_bytes=48 * 1024 * 1024),
        cost_estimate=pl.CostEstimate(
            flops=4 * tokens * width * keys,
            bytes_accessed=keys * 4 * HD + 4 * tokens * width,
            transcendentals=tokens * heads * keys,
        ),
    )(*query_parts, cosine, sine, qpos, qstart, kpos, *kv_parts)


def project_kernel(attended_ref, weight_ref, out_ref):
    parts, _, depth = attended_ref.shape
    total = 0.0
    for part in range(parts):
        total = total + jnp.dot(
            attended_ref[part],
            weight_ref[0, pl.ds(part * depth, depth), :],
            preferred_element_type=jnp.float32,
        )
    out_ref[...] = total.astype(jnp.bfloat16)


def project(attended, weight):
    parts, tokens, depth = attended.shape
    blocks, rows, width = weight.shape
    return pl.pallas_call(
        project_kernel,
        grid=(blocks,),
        out_shape=jax.ShapeDtypeStruct((tokens, blocks * width), jnp.bfloat16),
        in_specs=[
            pl.BlockSpec((parts, tokens, depth), lambda i: (0, 0, 0)),
            pl.BlockSpec((1, rows, width), lambda i: (i, 0, 0)),
        ],
        out_specs=pl.BlockSpec((tokens, width), lambda i: (0, i)),
        compiler_params=pltpu.CompilerParams(vmem_limit_bytes=48 * 1024 * 1024),
        cost_estimate=pl.CostEstimate(
            flops=2 * tokens * rows * blocks * width,
            bytes_accessed=2 * (rows * blocks * width + tokens * (rows + blocks * width)),
            transcendentals=0,
        ),
    )(attended, weight)


def cyclic(count, distance):
    return [(i, (i + distance) % count) for i in range(count)]


def per_device(tokens, norm_gain, w_query, w_key, w_value, w_out, doc_starts):
    rows, features = tokens.shape
    n_hi = lax.axis_size("hi")
    n_lo = lax.axis_size("lo")
    hi = lax.axis_index("hi")
    lo = lax.axis_index("lo")
    depth = features // n_hi
    kv_local = w_key.shape[1] // HD

    w_pair = jnp.concatenate(
        [
            w_key.reshape(w_key.shape[0], kv_local, HD),
            w_value.reshape(w_value.shape[0], kv_local, HD),
        ],
        axis=2,
    ).reshape(w_key.shape[0], 2 * w_key.shape[1])
    pair_rows = lax.all_gather(w_pair, "lo", axis=0, tiled=True)
    query_rows = lax.all_gather(w_query, "lo", axis=0, tiled=True)
    out_columns = lax.all_gather(w_out, "lo", axis=0) if n_hi > 1 else None

    source = tokens.astype(jnp.float32)
    normed = (
        source * lax.rsqrt(jnp.mean(source * source, axis=1, keepdims=True) + 1e-05) * norm_gain
    ).astype(jnp.bfloat16)

    own = lax.dynamic_slice_in_dim(normed, hi * depth, depth, 1)
    group_rows = n_hi * rows
    gathered = jnp.zeros((group_rows, depth), jnp.bfloat16)
    gathered = lax.dynamic_update_slice_in_dim(gathered, own, hi * rows, 0)
    for d in range(1, n_hi):
        there = lax.rem(hi + d, n_hi)
        piece = lax.dynamic_slice_in_dim(normed, there * depth, depth, 1)
        piece = lax.ppermute(piece, "hi", cyclic(n_hi, d))
        came_from = lax.rem(hi - d + n_hi, n_hi)
        gathered = lax.dynamic_update_slice_in_dim(gathered, piece, came_from * rows, 0)

    def split_sum(weight):
        product = jnp.dot(gathered, weight, preferred_element_type=jnp.float32).astype(
            jnp.bfloat16
        )
        width = weight.shape[1] // n_hi
        parts = [lax.dynamic_slice_in_dim(product, hi * width, width, 1)]
        for d in range(1, n_hi):
            there = lax.rem(hi + d, n_hi)
            piece = lax.dynamic_slice_in_dim(product, there * width, width, 1)
            parts.append(lax.ppermute(piece, "hi", cyclic(n_hi, d)))
        return parts

    row_index = jnp.arange(group_rows, dtype=jnp.int32)

    def positions_of(lo_index):
        return (row_index // rows * n_lo + lo_index) * rows + row_index % rows

    qpos = positions_of(lo)
    qstart = jnp.max(jnp.where(doc_starts[None, :] <= qpos[:, None], doc_starts[None, :], 0), axis=1)
    cosine, sine = rotary_tables(qpos)

    pair_sum = functools.reduce(
        jnp.add, [part.astype(jnp.float32) for part in split_sum(pair_rows)]
    )
    key_proj = rotate(pair_sum[:, :HD], cosine, sine).astype(jnp.bfloat16)
    kv_own = jnp.concatenate([key_proj, pair_sum[:, HD:].astype(jnp.bfloat16)], axis=1)
    if n_hi > 1:
        kv_parts = [kv_own]
        kpos = [qpos]
        for d in range(1, n_lo):
            kv_parts.append(lax.ppermute(kv_own, "lo", cyclic(n_lo, d)))
            kpos.append(positions_of(lax.rem(lo - d + n_lo, n_lo)))
        kpos = jnp.stack(kpos)
    else:
        kv_parts = [lax.all_gather(kv_own, "lo", axis=0, tiled=True)]
        kpos = jnp.arange(n_lo * rows, dtype=jnp.int32)[None, :]

    query_parts = split_sum(query_rows)
    attended = attention(
        query_parts, cosine, sine, qpos[:, None], qstart[:, None], kpos, kv_parts, n_hi
    )
    if n_hi == 1:
        wide = lax.all_gather(w_out, "lo", axis=1, tiled=True)
        partial_out = jnp.dot(attended, wide, preferred_element_type=jnp.float32)
        return lax.psum_scatter(
            partial_out.astype(jnp.bfloat16), "head", scatter_dimension=1, tiled=True
        )
    partial_out = project(lax.all_gather(attended, "hi", axis=0), out_columns)

    head = lax.axis_index("head")
    kept = group_rows // 2
    mine = lax.dynamic_slice_in_dim(partial_out, head * kept, kept, 0)
    theirs = lax.dynamic_slice_in_dim(partial_out, (1 - head) * kept, kept, 0)
    theirs = lax.ppermute(theirs, "head", [(0, 1), (1, 0)])
    summed = (mine.astype(jnp.float32) + theirs.astype(jnp.float32)).astype(jnp.bfloat16)
    arrived = []
    for e in range(2):
        block = lax.rem(hi + e, 2)
        piece = lax.dynamic_slice_in_dim(summed, block * rows, rows, 0)
        route = [
            (z * 2 + g, (2 * g + (z + e) % 2) * 2 + z // 2) for z in range(n_hi) for g in range(2)
        ]
        arrived.append(lax.ppermute(piece, ("hi", "head"), route))
    even = lax.rem(hi, 2) == 0
    return jnp.concatenate(
        [jnp.where(even, arrived[0], arrived[1]), jnp.where(even, arrived[1], arrived[0])], axis=1
    )


def solution(mesh):
    ctx = mesh.shape["ctx"]
    heads = mesh.shape["head"]
    both = ("hi", "lo")
    placed = (
        P(both, None),
        P(),
        P(both, "head"),
        P(both, "head"),
        P(both, "head"),
        P("head", both),
        P(),
    )

    def run(tokens, norm_gain, w_query, w_key, w_value, w_out, doc_starts):
        n_hi = w_key.shape[1] // HD // heads
        grid = Mesh(mesh.devices.reshape(n_hi, ctx // n_hi, heads), ("hi", "lo", "head"))
        return jax.shard_map(
            per_device, mesh=grid, in_specs=placed, out_specs=P(both, "head"), check_vma=False
        )(tokens, norm_gain, w_query, w_key, w_value, w_out, doc_starts)

    return run
```

```python
import functools

import jax
import jax.numpy as jnp
from jax import lax
from jax.experimental import pallas as pl
from jax.experimental.pallas import tpu as pltpu
from jax.sharding import Mesh
from jax.sharding import PartitionSpec as P

HD = 128
HALF = HD // 2


def rotary_tables(positions):
    freqs = 500000.0 ** (-(jnp.arange(HALF, dtype=jnp.float32) * 2.0 / HD))
    angles = positions.astype(jnp.float32)[:, None] * freqs[None, :]
    cosine = jnp.cos(angles)
    sine = jnp.sin(angles)
    return (
        jnp.concatenate([cosine, cosine], axis=1),
        jnp.concatenate([-sine, sine], axis=1),
    )


def rotate(values, cosine, sine):
    swapped = jnp.concatenate([values[:, HALF:], values[:, :HALF]], axis=1)
    return values * cosine + swapped * sine


def attention_kernel(blocks, n_query, n_kv, *refs):
    query_refs = refs[:n_query]
    cos_ref, sin_ref, qpos_ref, qstart_ref, kpos_ref = refs[n_query : n_query + 5]
    kv_refs = refs[n_query + 5 : n_query + 5 + n_kv]
    out_ref, rotated, bias = refs[n_query + 5 + n_kv :]
    heads, tokens, _ = rotated.shape
    cosine = cos_ref[...]
    sine = sin_ref[...]
    for h in range(heads):
        lanes = pl.ds(h * HD, HD)
        total = query_refs[0][:, lanes].astype(jnp.float32)
        for ref in query_refs[1:]:
            total = total + ref[:, lanes].astype(jnp.float32)
        turned = total * cosine + pltpu.roll(total, HALF, 1) * sine
        rotated[h] = turned.astype(jnp.bfloat16)
    rows = tokens // blocks
    kv_rows = kv_refs[0].shape[0]
    scale = HD**-0.5
    for j in range(blocks):
        first = j * rows
        length = kv_rows * (j + 1) // blocks
        qpos = qpos_ref[pl.ds(first, rows), :]
        qstart = qstart_ref[pl.ds(first, rows), :]
        for d in range(n_kv):
            kpos = kpos_ref[pl.ds(d, 1), pl.ds(0, length)]
            visible = (kpos <= qpos) & (kpos >= qstart)
            bias[:, pl.ds(d * length, length)] = jnp.where(visible, 0.0, -jnp.inf)

        def one_head(h, unused):
            query = rotated[h, pl.ds(first, rows), :]
            scores = []
            for d in range(n_kv):
                part = lax.dot_general(
                    query,
                    kv_refs[d][pl.ds(0, length), pl.ds(0, HD)],
                    (((1,), (1,)), ((), ())),
                    preferred_element_type=jnp.float32,
                )
                scores.append(part + bias[:, pl.ds(d * length, length)])
            highest = functools.reduce(
                jnp.maximum, [jnp.max(s, axis=1, keepdims=True) for s in scores]
            )
            denominator = 0.0
            mixed = 0.0
            for d in range(n_kv):
                probs = jnp.exp((scores[d] - highest) * scale)
                denominator = denominator + jnp.sum(probs, axis=1, keepdims=True)
                mixed = mixed + jnp.dot(
                    probs.astype(jnp.bfloat16),
                    kv_refs[d][pl.ds(0, length), pl.ds(HD, HD)],
                    preferred_element_type=jnp.float32,
                )
            lanes = pl.ds(pl.multiple_of(h * HD, HD), HD)
            out_ref[pl.ds(first, rows), lanes] = (mixed / denominator).astype(jnp.bfloat16)
            return unused

        lax.fori_loop(0, heads, one_head, 0)


def attention(query_parts, cosine, sine, qpos, qstart, kpos, kv_parts, blocks):
    tokens, width = query_parts[0].shape
    heads = width // HD
    keys = sum(part.shape[0] for part in kv_parts)
    return pl.pallas_call(
        functools.partial(attention_kernel, blocks, len(query_parts), len(kv_parts)),
        out_shape=jax.ShapeDtypeStruct((tokens, width), jnp.bfloat16),
        scratch_shapes=[
            pltpu.VMEM((heads, tokens, HD), jnp.bfloat16),
            pltpu.VMEM((tokens // blocks, keys), jnp.float32),
        ],
        compiler_params=pltpu.CompilerParams(vmem_limit_bytes=20 * 1024 * 1024),
        cost_estimate=pl.CostEstimate(
            flops=4 * tokens * width * keys,
            bytes_accessed=keys * 4 * HD + 4 * tokens * width,
            transcendentals=tokens * heads * keys,
        ),
    )(*query_parts, cosine, sine, qpos, qstart, kpos, *kv_parts)


def project_kernel(place_ref, *refs):
    attended_refs = refs[:4]
    weight_refs = refs[4:8]
    total_refs = refs[8:-2]
    hi = place_ref[0]
    lo = place_ref[1]
    core = place_ref[2]
    depth = attended_refs[0].shape[1]
    width = weight_refs[0].shape[1]
    span = weight_refs[0].shape[0] // 4
    offset = place_ref[3]
    for side, out_ref in enumerate(refs[-2:]):
        kept = out_ref.shape[0]
        rows = pl.ds(pl.multiple_of(lax.rem(core + side, 2) * kept, kept), kept)
        for r, weight_ref in enumerate(weight_refs):
            columns = pl.ds(pl.multiple_of((lo ^ r) * width, width), width)
            total = total_refs[side][:, columns] if total_refs else 0.0
            for k, attended_ref in enumerate(attended_refs):
                first = lax.rem(hi - k + 4, 4) * span + offset
                total = total + jnp.dot(
                    attended_ref[rows, :],
                    weight_ref[pl.ds(pl.multiple_of(first, depth), depth), :],
                    preferred_element_type=jnp.float32,
                )
            out_ref[:, columns] = total.astype(out_ref.dtype)


def project(place, attended_parts, weights, totals, kind):
    tokens, depth = attended_parts[0].shape
    width = weights[0].shape[1]
    shape = jax.ShapeDtypeStruct((tokens // 2, 4 * width), kind)
    operands = (*attended_parts, *weights, *totals)
    return pl.pallas_call(
        project_kernel,
        in_specs=[pl.BlockSpec(memory_space=pltpu.SMEM)]
        + [pl.BlockSpec(memory_space=pltpu.VMEM)] * len(operands),
        out_shape=(shape, shape),
        compiler_params=pltpu.CompilerParams(vmem_limit_bytes=20 * 1024 * 1024),
        cost_estimate=pl.CostEstimate(
            flops=2 * tokens * 4 * depth * 4 * width,
            bytes_accessed=sum(x.size * x.dtype.itemsize for x in operands),
            transcendentals=0,
        ),
    )(place, *operands)


def cyclic(count, distance):
    return [(i, (i + distance) % count) for i in range(count)]


def normalised(tokens, norm_gain):
    source = tokens.astype(jnp.float32)
    return (
        source * lax.rsqrt(jnp.mean(source * source, axis=1, keepdims=True) + 1e-05) * norm_gain
    ).astype(jnp.bfloat16)


def document_start(positions, doc_starts):
    begun = doc_starts[None, :] <= positions[:, None]
    return jnp.max(jnp.where(begun, doc_starts[None, :], 0), axis=1)


def plain_device(tokens, norm_gain, w_query, w_key, w_value, w_out, doc_starts):
    rows = tokens.shape[0]
    count = lax.axis_size("ctx")
    normed = normalised(tokens, norm_gain)

    def project_with(weight):
        gathered = lax.all_gather(weight, "ctx", axis=0, tiled=True)
        return jnp.dot(normed, gathered, preferred_element_type=jnp.float32)

    qpos = lax.axis_index("ctx") * rows + jnp.arange(rows, dtype=jnp.int32)
    qstart = document_start(qpos, doc_starts)
    cosine, sine = rotary_tables(qpos)
    kpos = jnp.arange(count * rows, dtype=jnp.int32)[None, :]
    query = project_with(w_query)
    key = project_with(w_key)
    value = project_with(w_value).astype(jnp.bfloat16)
    kv_local = w_key.shape[1] // HD
    group = w_query.shape[1] // kv_local
    mixed = []
    for h in range(kv_local):
        lanes = slice(h * HD, (h + 1) * HD)
        turned = rotate(key[:, lanes], cosine, sine).astype(jnp.bfloat16)
        pair = jnp.concatenate([turned, value[:, lanes]], axis=1)
        pair = lax.all_gather(pair, "ctx", axis=0, tiled=True)
        part = query[:, h * group : (h + 1) * group]
        mixed.append(
            attention([part], cosine, sine, qpos[:, None], qstart[:, None], kpos, [pair], 1)
        )
    attended = jnp.concatenate(mixed, axis=1)
    wide = lax.all_gather(w_out, "ctx", axis=1, tiled=True)
    partial_out = jnp.dot(attended, wide, preferred_element_type=jnp.float32)
    return lax.psum_scatter(
        partial_out.astype(jnp.bfloat16), "head", scatter_dimension=1, tiled=True
    )


def after(value, *earlier):
    return lax.optimization_barrier((value, *earlier))[0]


def beside(value, bit):
    return lax.ppermute(value, "lo", [(i, i ^ bit) for i in range(4)])


def across(from_one, from_two):
    half = from_one.shape[0] // 2
    return beside(from_two[:half], 1), beside(from_one[half:], 2)


def line_device(tokens, norm_gain, w_query, w_key, w_value, w_out, doc_starts):
    rows, features = tokens.shape
    hi = lax.axis_index("hi")
    lo = lax.axis_index("lo")
    core = lax.axis_index("head")
    depth = features // 4
    share = depth // 4
    group_rows = 4 * rows
    heads = w_query.shape[1] // 4

    w_pair = jnp.concatenate([w_key, w_value], axis=1)
    half = heads // 2
    w_halves = [
        jnp.concatenate(
            [w_query[:, z * heads + c * half : z * heads + (c + 1) * half] for z in range(4)],
            axis=1,
        )
        for c in range(2)
    ]

    def spread(pieces):
        return [pieces[0]] + [lax.ppermute(pieces[d], "hi", cyclic(4, d)) for d in range(1, 4)]

    pair_one, pair_two = beside(w_pair, 1), beside(w_pair, 2)
    w_a = after(w_halves[0], pair_one, pair_two)
    pair_cross = across(pair_one, pair_two)
    a_one, a_two = beside(w_a, 1), beside(w_a, 2)
    w_b = after(w_halves[1], a_one, a_two)
    a_cross = across(a_one, a_two)
    b_one, b_two = beside(w_b, 1), beside(w_b, 2)
    b_cross = across(b_one, b_two)
    w_o = after(w_out, *b_cross)
    o_one, o_two = beside(w_o, 1), beside(w_o, 2)
    o_cross = jnp.concatenate(across(o_one, o_two), axis=0)

    normed = normalised(tokens, norm_gain)
    pieces = []
    for d in range(4):
        first = lax.rem(hi + d, 4) * depth
        pieces.append(
            jnp.concatenate(
                [
                    lax.dynamic_slice_in_dim(normed, first + (lo ^ r) * share, share, 1)
                    for r in range(4)
                ],
                axis=1,
            )
        )
    gathered = jnp.zeros((group_rows, depth), jnp.bfloat16)
    for d, piece in enumerate(spread(pieces)):
        gathered = lax.dynamic_update_slice_in_dim(
            gathered, piece, lax.rem(hi - d + 4, 4) * rows, 0
        )

    def product(own, one, two, cross):
        total = jnp.dot(gathered[:, :share], own, preferred_element_type=jnp.float32)
        place = share
        for weight in (one, two, *cross):
            depth_here = weight.shape[0]
            total = total + jnp.dot(
                gathered[:, place : place + depth_here],
                weight,
                preferred_element_type=jnp.float32,
            )
            place += depth_here
        return total.astype(jnp.bfloat16)

    row_index = jnp.arange(group_rows, dtype=jnp.int32)

    def positions_of(lo_index):
        return (row_index // rows * 4 + lo_index) * rows + row_index % rows

    qpos = positions_of(lo)
    qstart = document_start(qpos, doc_starts)
    cosine, sine = rotary_tables(qpos)
    kpos = jnp.stack([positions_of(lo ^ r) for r in range(4)])

    pair_product = product(w_pair, pair_one, pair_two, pair_cross)
    kv_width = w_key.shape[1]
    pieces = []
    for d in range(4):
        first = lax.rem(hi + d, 4) * HD
        pieces.append(
            jnp.concatenate(
                [
                    lax.dynamic_slice_in_dim(pair_product, first, HD, 1),
                    lax.dynamic_slice_in_dim(pair_product, first + kv_width, HD, 1),
                ],
                axis=1,
            )
        )
    pair_sum = functools.reduce(jnp.add, [part.astype(jnp.float32) for part in spread(pieces)])
    key_proj = rotate(pair_sum[:, :HD], cosine, sine).astype(jnp.bfloat16)
    kv_own = jnp.concatenate([key_proj, pair_sum[:, HD:].astype(jnp.bfloat16)], axis=1)
    kv_parts = [kv_own] + [
        lax.ppermute(kv_own, "lo", [(i, i ^ r) for i in range(4)]) for r in range(1, 4)
    ]

    place = jnp.stack([hi, lo, core])
    totals = ()
    kinds = (jnp.float32, jnp.bfloat16)
    chunks = [(w_a, a_one, a_two, a_cross), (w_b, b_one, b_two, b_cross)]
    for c, chunk in enumerate(chunks):
        query = product(*chunk)
        query_parts = spread(
            [lax.dynamic_slice_in_dim(query, lax.rem(hi + d, 4) * half, half, 1) for d in range(4)]
        )
        attended = attention(
            query_parts, cosine, sine, qpos[:, None], qstart[:, None], kpos, kv_parts, 4
        )
        attended_parts = [attended] + [
            lax.ppermute(attended, "hi", cyclic(4, d)) for d in range(1, 4)
        ]
        where = jnp.concatenate([place, jnp.full((1,), c * half, jnp.int32)])
        totals = project(where, attended_parts, (w_o, o_one, o_two, o_cross), totals, kinds[c])

    mine, theirs = totals
    theirs = lax.ppermute(theirs, "head", [(0, 1), (1, 0)])
    summed = (mine.astype(jnp.float32) + theirs.astype(jnp.float32)).astype(jnp.bfloat16)
    arrived = []
    for e in range(2):
        block = lax.rem(hi + e, 2)
        piece = lax.dynamic_slice_in_dim(summed, block * rows, rows, 0)
        route = [(z * 2 + g, (2 * g + (z + e) % 2) * 2 + z // 2) for z in range(4) for g in range(2)]
        arrived.append(lax.ppermute(piece, ("hi", "head"), route))
    even = lax.rem(hi, 2) == 0
    return jnp.concatenate(
        [jnp.where(even, arrived[0], arrived[1]), jnp.where(even, arrived[1], arrived[0])], axis=1
    )


def solution(mesh):
    ctx = mesh.shape["ctx"]
    heads = mesh.shape["head"]

    def run(tokens, norm_gain, w_query, w_key, w_value, w_out, doc_starts):
        lines = w_key.shape[1] // HD // heads
        if (ctx, heads, lines) == (16, 2, 4):
            both = ("hi", "lo")
            grid = Mesh(mesh.devices.reshape(4, 4, 2), ("hi", "lo", "head"))
            body = line_device
        else:
            both, grid, body = "ctx", mesh, plain_device
        placed = (
            P(both, None),
            P(),
            P(both, "head"),
            P(both, "head"),
            P(both, "head"),
            P("head", both),
            P(),
        )
        return jax.shard_map(
            body, mesh=grid, in_specs=placed, out_specs=P(both, "head"), check_vma=False
        )(tokens, norm_gain, w_query, w_key, w_value, w_out, doc_starts)

    return run
```

```python
import functools

import jax
import jax.numpy as jnp
from jax import lax
from jax.experimental import pallas as pl
from jax.experimental.pallas import tpu as pltpu
from jax.sharding import Mesh
from jax.sharding import PartitionSpec as P

HD = 128
HALF = HD // 2
MIB = 1024 * 1024


def local_kernel(body, out_shape, operands, flops, scratch=(), exps=0):
    size = sum(x.size * x.dtype.itemsize for x in operands)
    return pl.pallas_call(
        body,
        in_specs=[pl.BlockSpec(memory_space=pltpu.SMEM)]
        + [pl.BlockSpec(memory_space=pltpu.VMEM)] * (len(operands) - 1),
        out_shape=out_shape,
        scratch_shapes=scratch,
        compiler_params=pltpu.CompilerParams(vmem_limit_bytes=20 * MIB),
        cost_estimate=pl.CostEstimate(flops=flops, bytes_accessed=size, transcendentals=exps),
    )(*operands)


def rotary_tables(positions):
    freqs = 500000.0 ** (-(jnp.arange(HALF, dtype=jnp.float32) * 2.0 / HD))
    angles = positions.astype(jnp.float32)[:, None] * freqs[None, :]
    cosine = jnp.cos(angles)
    sine = jnp.sin(angles)
    return (
        jnp.concatenate([cosine, cosine], axis=1),
        jnp.concatenate([-sine, sine], axis=1),
    )


def summed_lanes(parts_ref, lanes):
    total = parts_ref[0, :, lanes].astype(jnp.float32)
    for part in range(1, parts_ref.shape[0]):
        total = total + parts_ref[part, :, lanes].astype(jnp.float32)
    return total


def rotated(values, cos_ref, sin_ref):
    return values * cos_ref[...] + pltpu.roll(values, HALF, 1) * sin_ref[...]


def pair_kernel(unused_ref, cos_ref, sin_ref, parts, out_ref):
    key = rotated(summed_lanes(parts, pl.ds(0, HD)), cos_ref, sin_ref)
    out_ref[:, pl.ds(0, HD)] = key.astype(jnp.bfloat16)
    out_ref[:, pl.ds(HD, HD)] = summed_lanes(parts, pl.ds(HD, HD)).astype(jnp.bfloat16)


def finish_pair(cosine, sine, parts):
    operands = (jnp.zeros((1,), jnp.int32), cosine, sine, parts)
    shape = jax.ShapeDtypeStruct(parts.shape[1:], jnp.bfloat16)
    return local_kernel(pair_kernel, shape, operands, 8 * parts.size)


def attention_kernel(blocks, stride, n_kv, place_ref, cos_ref, sin_ref, query_ref, *refs):
    kv_refs = refs[:n_kv]
    out_ref, turned, bias = refs[n_kv:]
    heads, tokens, _ = turned.shape
    for h in range(heads):
        total = summed_lanes(query_ref, pl.ds(h * HD, HD))
        turned[h] = rotated(total, cos_ref, sin_ref).astype(jnp.bfloat16)
    rows = tokens // blocks
    kv_rows = kv_refs[0].shape[0] // blocks
    documents = place_ref.shape[0] - 1 - n_kv
    scale = HD**-0.5
    for j in range(blocks):
        first = j * rows
        length = kv_rows * (j + 1)
        qpos = lax.broadcasted_iota(jnp.int32, (rows, HD), 0) + (place_ref[0] + j * stride)
        qstart = jnp.zeros_like(qpos)
        for i in range(documents):
            start = place_ref[1 + n_kv + i]
            qstart = jnp.where(qpos >= start, start, qstart)
        span = qpos - qstart
        for d in range(n_kv):
            for b in range(j + 1):
                for c in range(0, kv_rows, HD):
                    kpos = lax.broadcasted_iota(jnp.int32, (rows, HD), 1) + (
                        place_ref[1 + d] + (b * stride + c)
                    )
                    back = qpos - kpos
                    visible = (back >= 0) & (back <= span)
                    bias[:, pl.ds(d * length + b * kv_rows + c, HD)] = jnp.where(
                        visible, 0.0, -jnp.inf
                    )

        def one_head(h, unused):
            query = turned[h, pl.ds(first, rows), :]
            scores = []
            for d in range(n_kv):
                part = lax.dot_general(
                    query,
                    kv_refs[d][pl.ds(0, length), pl.ds(0, HD)],
                    (((1,), (1,)), ((), ())),
                    preferred_element_type=jnp.float32,
                )
                scores.append(part + bias[:, pl.ds(d * length, length)])
            highest = functools.reduce(
                jnp.maximum, [jnp.max(s, axis=1, keepdims=True) for s in scores]
            )
            denominator = 0.0
            mixed = 0.0
            for d in range(n_kv):
                probs = jnp.exp((scores[d] - highest) * scale)
                denominator = denominator + jnp.sum(probs, axis=1, keepdims=True)
                mixed = mixed + jnp.dot(
                    probs.astype(jnp.bfloat16),
                    kv_refs[d][pl.ds(0, length), pl.ds(HD, HD)],
                    preferred_element_type=jnp.float32,
                )
            lanes = pl.ds(pl.multiple_of(h * HD, HD), HD)
            out_ref[pl.ds(first, rows), lanes] = (mixed / denominator).astype(jnp.bfloat16)
            return unused

        lax.fori_loop(0, heads, one_head, 0)


def attention(place, cosine, sine, query_parts, kv_parts, blocks, stride):
    _, tokens, width = query_parts.shape
    heads = width // HD
    keys = sum(part.shape[0] for part in kv_parts)
    return local_kernel(
        functools.partial(attention_kernel, blocks, stride, len(kv_parts)),
        jax.ShapeDtypeStruct((tokens, width), jnp.bfloat16),
        (place, cosine, sine, query_parts, *kv_parts),
        4 * tokens * width * keys,
        [
            pltpu.VMEM((heads, tokens, HD), jnp.bfloat16),
            pltpu.VMEM((tokens // blocks, keys), jnp.float32),
        ],
        tokens * heads * keys,
    )


def product_kernel(groups, place_ref, token_ref, *refs):
    weight_refs = refs[:4]
    out_ref = refs[-1]
    lo = place_ref[1]
    share = weight_refs[0].shape[0] // groups
    width = weight_refs[0].shape[1] // 4
    for d in range(4):
        columns = pl.ds(d * width, width)
        for g in range(groups):
            total = 0.0
            for r in range(4):
                features = pl.ds(pl.multiple_of((lo ^ r) * share, share), share)
                total = total + jnp.dot(
                    token_ref[:, features],
                    weight_refs[r][pl.ds(g * share, share), columns],
                    preferred_element_type=jnp.float32,
                )
            out_ref[d, :, pl.ds(g * width, width)] = total.astype(jnp.bfloat16)


def product(place, line_tokens, weights, groups):
    count, depth = line_tokens.shape
    width = groups * weights[0].shape[1] // 4
    return local_kernel(
        functools.partial(product_kernel, groups),
        jax.ShapeDtypeStruct((4, count, width), jnp.bfloat16),
        (place, line_tokens, *weights),
        2 * count * depth * 4 * width,
    )


def project_kernel(place_ref, *refs):
    attended_refs = refs[:4]
    weight_refs = refs[4:8]
    total_refs = refs[8:-2]
    hi = place_ref[0]
    lo = place_ref[1]
    core = place_ref[2]
    offset = place_ref[3]
    depth = attended_refs[0].shape[1]
    width = weight_refs[0].shape[1]
    span = weight_refs[0].shape[0] // 4
    for side, out_ref in enumerate(refs[-2:]):
        kept = out_ref.shape[0]
        rows = pl.ds(pl.multiple_of(lax.rem(core + side, 2) * kept, kept), kept)
        for r, weight_ref in enumerate(weight_refs):
            columns = pl.ds(pl.multiple_of((lo ^ r) * width, width), width)
            total = total_refs[side][:, columns] if total_refs else 0.0
            for k, attended_ref in enumerate(attended_refs):
                first = lax.rem(hi - k + 4, 4) * span + offset
                total = total + jnp.dot(
                    attended_ref[rows, :],
                    weight_ref[pl.ds(pl.multiple_of(first, depth), depth), :],
                    preferred_element_type=jnp.float32,
                )
            out_ref[:, columns] = total.astype(out_ref.dtype)


def project(place, attended_parts, weights, totals, kind):
    tokens, depth = attended_parts[0].shape
    width = weights[0].shape[1]
    shape = jax.ShapeDtypeStruct((tokens // 2, 4 * width), kind)
    return local_kernel(
        project_kernel,
        (shape, shape),
        (place, *attended_parts, *weights, *totals),
        2 * tokens * 4 * depth * 4 * width,
    )


def normalised(tokens, norm_gain):
    source = tokens.astype(jnp.float32)
    return (
        source * lax.rsqrt(jnp.mean(source * source, axis=1, keepdims=True) + 1e-05) * norm_gain
    ).astype(jnp.bfloat16)


def plain_device(tokens, norm_gain, w_query, w_key, w_value, w_out, doc_starts):
    rows = tokens.shape[0]
    first = lax.axis_index("ctx") * rows
    normed = normalised(tokens, norm_gain)

    def project_with(weight):
        gathered = lax.all_gather(weight, "ctx", axis=0, tiled=True)
        total = jnp.dot(normed, gathered, preferred_element_type=jnp.float32)
        return total.astype(jnp.bfloat16)

    cosine, sine = rotary_tables(first + jnp.arange(rows, dtype=jnp.int32))
    place = jnp.concatenate([jnp.stack([first, jnp.zeros_like(first)]), doc_starts])
    query = project_with(w_query)
    key = project_with(w_key)
    value = project_with(w_value)
    kv_local = w_key.shape[1] // HD
    group = w_query.shape[1] // kv_local
    mixed = []
    for h in range(kv_local):
        lanes = slice(h * HD, (h + 1) * HD)
        pair = jnp.concatenate([key[:, lanes], value[:, lanes]], axis=1)
        pair = lax.all_gather(finish_pair(cosine, sine, pair[None]), "ctx", axis=0, tiled=True)
        part = query[:, h * group : (h + 1) * group]
        mixed.append(attention(place, cosine, sine, part[None], [pair], 1, 0))
    attended = jnp.concatenate(mixed, axis=1)
    wide = lax.all_gather(w_out, "ctx", axis=1, tiled=True)
    partial_out = jnp.dot(attended, wide, preferred_element_type=jnp.float32)
    return lax.psum_scatter(
        partial_out.astype(jnp.bfloat16), "head", scatter_dimension=1, tiled=True
    )


def after(value, *earlier):
    return lax.optimization_barrier((value, *earlier))[0]


def square(block):
    return [block] + [
        lax.ppermute(block, "lo", [(i, i ^ r) for i in range(4)]) for r in range(1, 4)
    ]


def along_line(pieces):
    return lax.all_to_all(pieces, "hi", 0, 0, tiled=True)


def round_line(block):
    return [block] + [
        lax.ppermute(block, "hi", [(i, (i + d) % 4) for i in range(4)]) for d in range(1, 4)
    ]


def line_device(tokens, norm_gain, w_query, w_key, w_value, w_out, doc_starts):
    rows, features = tokens.shape
    hi = lax.axis_index("hi")
    lo = lax.axis_index("lo")
    core = lax.axis_index("head")
    depth = features // 4
    heads = w_query.shape[1] // 4
    half = heads // 2
    place = jnp.stack([hi, lo, core])

    pair_blocks = square(jnp.concatenate([w_key, w_value], axis=0))
    stage = pair_blocks[1:]
    query_blocks = []
    for c in range(2):
        columns = [
            w_query[:, z * heads + c * half : z * heads + (c + 1) * half] for z in range(4)
        ]
        query_blocks.append(square(after(jnp.concatenate(columns, axis=1), *stage)))
        stage = query_blocks[-1][1:]
    out_blocks = square(after(w_out, *stage))

    normed = normalised(tokens, norm_gain)
    pieces = jnp.stack([normed[:, d * depth : (d + 1) * depth] for d in range(4)])
    line_tokens = along_line(pieces).reshape(4 * rows, depth)

    row_index = jnp.arange(4 * rows, dtype=jnp.int32)
    cosine, sine = rotary_tables((row_index // rows * 4 + lo) * rows + row_index % rows)
    kv_parts = square(
        finish_pair(
            cosine, sine, along_line(product(place, line_tokens, pair_blocks, 2))
        )
    )

    firsts = jnp.stack([lo, lo, lo ^ 1, lo ^ 2, lo ^ 3]) * rows
    seen = jnp.concatenate([firsts, doc_starts])
    totals = ()
    kinds = (jnp.float32, jnp.bfloat16)
    for c in range(2):
        query_parts = along_line(product(place, line_tokens, query_blocks[c], 1))
        attended = attention(seen, cosine, sine, query_parts, kv_parts, 4, 4 * rows)
        where = jnp.concatenate([place, jnp.full((1,), c * half, jnp.int32)])
        totals = project(where, round_line(attended), out_blocks, totals, kinds[c])

    mine, theirs = totals
    theirs = lax.ppermute(theirs, "head", [(0, 1), (1, 0)])
    summed = (mine.astype(jnp.float32) + theirs.astype(jnp.float32)).astype(jnp.bfloat16)
    arrived = []
    for e in range(2):
        block = lax.rem(hi + e, 2)
        piece = lax.dynamic_slice_in_dim(summed, block * rows, rows, 0)
        route = [(z * 2 + g, (2 * g + (z + e) % 2) * 2 + z // 2) for z in range(4) for g in range(2)]
        arrived.append(lax.ppermute(piece, ("hi", "head"), route))
    even = lax.rem(hi, 2) == 0
    return jnp.concatenate(
        [jnp.where(even, arrived[0], arrived[1]), jnp.where(even, arrived[1], arrived[0])], axis=1
    )


def solution(mesh):
    ctx = mesh.shape["ctx"]
    heads = mesh.shape["head"]

    def run(tokens, norm_gain, w_query, w_key, w_value, w_out, doc_starts):
        lines = w_key.shape[1] // HD // heads
        if (ctx, heads, lines) == (16, 2, 4):
            both = ("hi", "lo")
            grid = Mesh(mesh.devices.reshape(4, 4, 2), ("hi", "lo", "head"))
            body = line_device
        else:
            both, grid, body = "ctx", mesh, plain_device
        placed = (
            P(both, None),
            P(),
            P(both, "head"),
            P(both, "head"),
            P(both, "head"),
            P("head", both),
            P(),
        )
        return jax.shard_map(
            body, mesh=grid, in_specs=placed, out_specs=P(both, "head"), check_vma=False
        )(tokens, norm_gain, w_query, w_key, w_value, w_out, doc_starts)

    return run
```

```python
import functools

import jax
import jax.numpy as jnp
from jax import lax
from jax.experimental import pallas as pl
from jax.experimental.pallas import tpu as pltpu
from jax.sharding import Mesh
from jax.sharding import PartitionSpec as P

HD = 128
HALF = HD // 2
MIB = 1024 * 1024


def local_kernel(body, out_shape, operands, flops, scratch=(), exps=0):
    size = sum(x.size * x.dtype.itemsize for x in operands)
    return pl.pallas_call(
        body,
        in_specs=[pl.BlockSpec(memory_space=pltpu.SMEM)]
        + [pl.BlockSpec(memory_space=pltpu.VMEM)] * (len(operands) - 1),
        out_shape=out_shape,
        scratch_shapes=scratch,
        compiler_params=pltpu.CompilerParams(vmem_limit_bytes=12 * MIB),
        cost_estimate=pl.CostEstimate(flops=flops, bytes_accessed=size, transcendentals=exps),
    )(*operands)


def rotary_tables(positions):
    freqs = 500000.0 ** (-(jnp.arange(HALF, dtype=jnp.float32) * 2.0 / HD))
    angles = positions.astype(jnp.float32)[:, None] * freqs[None, :]
    cosine = jnp.cos(angles)
    sine = jnp.sin(angles)
    return (
        jnp.concatenate([cosine, cosine], axis=1),
        jnp.concatenate([-sine, sine], axis=1),
    )


def summed_lanes(parts_ref, lanes):
    total = parts_ref[0, :, lanes].astype(jnp.float32)
    for part in range(1, parts_ref.shape[0]):
        total = total + parts_ref[part, :, lanes].astype(jnp.float32)
    return total


def rotated(values, cos_ref, sin_ref):
    return values * cos_ref[...] + pltpu.roll(values, HALF, 1) * sin_ref[...]


def pair_kernel(unused_ref, cos_ref, sin_ref, parts, out_ref):
    key = rotated(summed_lanes(parts, pl.ds(0, HD)), cos_ref, sin_ref)
    out_ref[:, pl.ds(0, HD)] = key.astype(jnp.bfloat16)
    out_ref[:, pl.ds(HD, HD)] = summed_lanes(parts, pl.ds(HD, HD)).astype(jnp.bfloat16)


def finish_pair(cosine, sine, parts):
    operands = (jnp.zeros((1,), jnp.int32), cosine, sine, parts)
    shape = jax.ShapeDtypeStruct(parts.shape[1:], jnp.bfloat16)
    return local_kernel(pair_kernel, shape, operands, 8 * parts.size)


def attention_kernel(blocks, stride, n_kv, place_ref, cos_ref, sin_ref, query_ref, *refs):
    kv_refs = refs[:n_kv]
    out_ref, turned, bias = refs[n_kv:]
    heads, tokens, _ = turned.shape
    for h in range(heads):
        total = summed_lanes(query_ref, pl.ds(h * HD, HD))
        turned[h] = rotated(total, cos_ref, sin_ref).astype(jnp.bfloat16)
    rows = tokens // blocks
    kv_rows = kv_refs[0].shape[0] // blocks
    documents = place_ref.shape[0] - 1 - n_kv
    scale = HD**-0.5
    for j in range(blocks):
        first = j * rows
        length = kv_rows * (j + 1)
        qpos = lax.broadcasted_iota(jnp.int32, (rows, HD), 0) + (place_ref[0] + j * stride)
        qstart = jnp.zeros_like(qpos)
        for i in range(documents):
            start = place_ref[1 + n_kv + i]
            qstart = jnp.where(qpos >= start, start, qstart)
        span = qpos - qstart
        for d in range(n_kv):
            for b in range(j + 1):
                for c in range(0, kv_rows, HD):
                    kpos = lax.broadcasted_iota(jnp.int32, (rows, HD), 1) + (
                        place_ref[1 + d] + (b * stride + c)
                    )
                    back = qpos - kpos
                    visible = (back >= 0) & (back <= span)
                    bias[:, pl.ds(d * length + b * kv_rows + c, HD)] = jnp.where(
                        visible, 0.0, -jnp.inf
                    )

        def one_head(h, unused):
            query = turned[h, pl.ds(first, rows), :]
            scores = []
            for d in range(n_kv):
                part = lax.dot_general(
                    query,
                    kv_refs[d][pl.ds(0, length), pl.ds(0, HD)],
                    (((1,), (1,)), ((), ())),
                    preferred_element_type=jnp.float32,
                )
                scores.append(part + bias[:, pl.ds(d * length, length)])
            highest = functools.reduce(
                jnp.maximum, [jnp.max(s, axis=1, keepdims=True) for s in scores]
            )
            denominator = 0.0
            mixed = 0.0
            for d in range(n_kv):
                probs = jnp.exp((scores[d] - highest) * scale)
                denominator = denominator + jnp.sum(probs, axis=1, keepdims=True)
                mixed = mixed + jnp.dot(
                    probs.astype(jnp.bfloat16),
                    kv_refs[d][pl.ds(0, length), pl.ds(HD, HD)],
                    preferred_element_type=jnp.float32,
                )
            lanes = pl.ds(pl.multiple_of(h * HD, HD), HD)
            out_ref[pl.ds(first, rows), lanes] = (mixed / denominator).astype(jnp.bfloat16)
            return unused

        lax.fori_loop(0, heads, one_head, 0)


def attention(place, cosine, sine, query_parts, kv_parts, blocks, stride):
    _, tokens, width = query_parts.shape
    heads = width // HD
    keys = sum(part.shape[0] for part in kv_parts)
    return local_kernel(
        functools.partial(attention_kernel, blocks, stride, len(kv_parts)),
        jax.ShapeDtypeStruct((tokens, width), jnp.bfloat16),
        (place, cosine, sine, query_parts, *kv_parts),
        4 * tokens * width * keys,
        [
            pltpu.VMEM((heads, tokens, HD), jnp.bfloat16),
            pltpu.VMEM((tokens // blocks, keys), jnp.float32),
        ],
        tokens * heads * keys,
    )


def product_kernel(groups, place_ref, token_ref, *refs):
    weight_refs = refs[:5]
    out_ref = refs[-1]
    lo = place_ref[1]
    share = weight_refs[0].shape[0] // groups
    width = weight_refs[0].shape[1] // 4
    for d in range(4):
        columns = pl.ds(d * width, width)
        for g in range(groups):
            total = 0.0
            for r in range(4):
                features = pl.ds(pl.multiple_of((lo ^ r) * share, share), share)
                if r < 3:
                    weight = weight_refs[r][pl.ds(g * share, share), columns]
                elif groups == 2:
                    weight = weight_refs[3 + g][:, columns]
                else:
                    weight = jnp.concatenate([ref[:, columns] for ref in weight_refs[3:]], axis=0)
                total = total + jnp.dot(
                    token_ref[:, features], weight, preferred_element_type=jnp.float32
                )
            out_ref[d, :, pl.ds(g * width, width)] = total.astype(jnp.bfloat16)


def product(place, line_tokens, weights, groups):
    count, depth = line_tokens.shape
    width = groups * weights[0].shape[1] // 4
    return local_kernel(
        functools.partial(product_kernel, groups),
        jax.ShapeDtypeStruct((4, count, width), jnp.bfloat16),
        (place, line_tokens, *weights),
        2 * count * depth * 4 * width,
    )


def project_kernel(place_ref, *refs):
    attended_refs = refs[:4]
    weight_refs = refs[4:8]
    total_refs = refs[8:-2]
    hi = place_ref[0]
    lo = place_ref[1]
    core = place_ref[2]
    offset = place_ref[3]
    depth = attended_refs[0].shape[1]
    width = weight_refs[0].shape[1]
    span = weight_refs[0].shape[0] // 4
    for side, out_ref in enumerate(refs[-2:]):
        kept = out_ref.shape[0]
        rows = pl.ds(pl.multiple_of(lax.rem(core + side, 2) * kept, kept), kept)
        for r, weight_ref in enumerate(weight_refs):
            columns = pl.ds(pl.multiple_of((lo ^ r) * width, width), width)
            total = total_refs[side][:, columns] if total_refs else 0.0
            for k, attended_ref in enumerate(attended_refs):
                first = lax.rem(hi - k + 4, 4) * span + offset
                total = total + jnp.dot(
                    attended_ref[rows, :],
                    weight_ref[pl.ds(pl.multiple_of(first, depth), depth), :],
                    preferred_element_type=jnp.float32,
                )
            out_ref[:, columns] = total.astype(out_ref.dtype)


def project(place, attended_parts, weights, totals, kind):
    tokens, depth = attended_parts[0].shape
    width = weights[0].shape[1]
    shape = jax.ShapeDtypeStruct((tokens // 2, 4 * width), kind)
    return local_kernel(
        project_kernel,
        (shape, shape),
        (place, *attended_parts, *weights, *totals),
        2 * tokens * 4 * depth * 4 * width,
    )


def normalised(tokens, norm_gain):
    source = tokens.astype(jnp.float32)
    return (
        source * lax.rsqrt(jnp.mean(source * source, axis=1, keepdims=True) + 1e-05) * norm_gain
    ).astype(jnp.bfloat16)


def plain_device(tokens, norm_gain, w_query, w_key, w_value, w_out, doc_starts):
    rows = tokens.shape[0]
    first = lax.axis_index("ctx") * rows
    normed = normalised(tokens, norm_gain)

    def project_with(weight):
        gathered = lax.all_gather(weight, "ctx", axis=0, tiled=True)
        total = jnp.dot(normed, gathered, preferred_element_type=jnp.float32)
        return total.astype(jnp.bfloat16)

    cosine, sine = rotary_tables(first + jnp.arange(rows, dtype=jnp.int32))
    place = jnp.concatenate([jnp.stack([first, jnp.zeros_like(first)]), doc_starts])
    query = project_with(w_query)
    key = project_with(w_key)
    value = project_with(w_value)
    kv_local = w_key.shape[1] // HD
    group = w_query.shape[1] // kv_local
    mixed = []
    for h in range(kv_local):
        lanes = slice(h * HD, (h + 1) * HD)
        pair = jnp.concatenate([key[:, lanes], value[:, lanes]], axis=1)
        pair = lax.all_gather(finish_pair(cosine, sine, pair[None]), "ctx", axis=0, tiled=True)
        part = query[:, h * group : (h + 1) * group]
        mixed.append(attention(place, cosine, sine, part[None], [pair], 1, 0))
    attended = jnp.concatenate(mixed, axis=1)
    wide = lax.all_gather(w_out, "ctx", axis=1, tiled=True)
    partial_out = jnp.dot(attended, wide, preferred_element_type=jnp.float32)
    return lax.psum_scatter(
        partial_out.astype(jnp.bfloat16), "head", scatter_dimension=1, tiled=True
    )


def after(value, *earlier):
    return lax.optimization_barrier((value, *earlier))[0]


def beside(block, r):
    return lax.ppermute(block, "lo", [(i, i ^ r) for i in range(4)])


def sides(block):
    return [block, beside(block, 1), beside(block, 2)]


def corner(blocks):
    half = blocks[0].shape[0] // 2
    return [*blocks, beside(blocks[2][:half], 1), beside(blocks[1][half:], 2)]


def along_line(pieces):
    return lax.all_to_all(pieces, "hi", 0, 0, tiled=True)


def round_line(block):
    return [block] + [
        lax.ppermute(block, "hi", [(i, (i + d) % 4) for i in range(4)]) for d in range(1, 4)
    ]


def line_device(tokens, norm_gain, w_query, w_key, w_value, w_out, doc_starts):
    rows, features = tokens.shape
    hi = lax.axis_index("hi")
    lo = lax.axis_index("lo")
    core = lax.axis_index("head")
    depth = features // 4
    heads = w_query.shape[1] // 4
    half = heads // 2
    place = jnp.stack([hi, lo, core])

    stage = sides(jnp.concatenate([w_key, w_value], axis=0))
    pair_blocks = corner(stage)
    query_blocks = []
    for c in range(2):
        columns = [
            w_query[:, z * heads + c * half : z * heads + (c + 1) * half] for z in range(4)
        ]
        stage = sides(after(jnp.concatenate(columns, axis=1), *stage[1:]))
        query_blocks.append(corner(stage))

    normed = normalised(tokens, norm_gain)
    pieces = jnp.stack([normed[:, d * depth : (d + 1) * depth] for d in range(4)])
    line_tokens = along_line(pieces).reshape(4 * rows, depth)

    row_index = jnp.arange(4 * rows, dtype=jnp.int32)
    cosine, sine = rotary_tables((row_index // rows * 4 + lo) * rows + row_index % rows)
    kv_own = finish_pair(
        cosine, sine, along_line(product(place, line_tokens, pair_blocks, 2))
    )
    kv_parts = [kv_own] + [beside(kv_own, r) for r in range(1, 4)]
    out_blocks = corner(sides(after(w_out, *query_blocks[1][3:], *kv_parts[1:])))
    out_blocks[3:] = [jnp.concatenate(out_blocks[3:], axis=0)]

    firsts = jnp.stack([lo, lo, lo ^ 1, lo ^ 2, lo ^ 3]) * rows
    seen = jnp.concatenate([firsts, doc_starts])
    totals = ()
    kinds = (jnp.float32, jnp.bfloat16)
    for c in range(2):
        query_parts = along_line(product(place, line_tokens, query_blocks[c], 1))
        attended = attention(seen, cosine, sine, query_parts, kv_parts, 4, 4 * rows)
        where = jnp.concatenate([place, jnp.full((1,), c * half, jnp.int32)])
        totals = project(where, round_line(attended), out_blocks, totals, kinds[c])

    mine, theirs = totals
    theirs = lax.ppermute(theirs, "head", [(0, 1), (1, 0)])
    summed = (mine.astype(jnp.float32) + theirs.astype(jnp.float32)).astype(jnp.bfloat16)
    arrived = []
    for e in range(2):
        block = lax.rem(hi + e, 2)
        piece = lax.dynamic_slice_in_dim(summed, block * rows, rows, 0)
        route = [(z * 2 + g, (2 * g + (z + e) % 2) * 2 + z // 2) for z in range(4) for g in range(2)]
        arrived.append(lax.ppermute(piece, ("hi", "head"), route))
    even = lax.rem(hi, 2) == 0
    return jnp.concatenate(
        [jnp.where(even, arrived[0], arrived[1]), jnp.where(even, arrived[1], arrived[0])], axis=1
    )


def solution(mesh):
    ctx = mesh.shape["ctx"]
    heads = mesh.shape["head"]

    def run(tokens, norm_gain, w_query, w_key, w_value, w_out, doc_starts):
        lines = w_key.shape[1] // HD // heads
        if (ctx, heads, lines) == (16, 2, 4):
            both = ("hi", "lo")
            grid = Mesh(mesh.devices.reshape(4, 4, 2), ("hi", "lo", "head"))
            body = line_device
        else:
            both, grid, body = "ctx", mesh, plain_device
        placed = (
            P(both, None),
            P(),
            P(both, "head"),
            P(both, "head"),
            P(both, "head"),
            P("head", both),
            P(),
        )
        return jax.shard_map(
            body, mesh=grid, in_specs=placed, out_specs=P(both, "head"), check_vma=False
        )(tokens, norm_gain, w_query, w_key, w_value, w_out, doc_starts)

    return run
```

```python
import functools

import jax
import jax.numpy as jnp
from jax import lax
from jax.experimental import pallas as pl
from jax.experimental.pallas import tpu as pltpu
from jax.sharding import Mesh
from jax.sharding import PartitionSpec as P

HD = 128
HALF = HD // 2
MIB = 1024 * 1024


def local_kernel(body, out_shape, operands, flops, scratch=(), exps=0):
    size = sum(x.size * x.dtype.itemsize for x in operands)
    return pl.pallas_call(
        body,
        in_specs=[pl.BlockSpec(memory_space=pltpu.SMEM)]
        + [pl.BlockSpec(memory_space=pltpu.VMEM)] * (len(operands) - 1),
        out_shape=out_shape,
        scratch_shapes=scratch,
        compiler_params=pltpu.CompilerParams(vmem_limit_bytes=12 * MIB),
        cost_estimate=pl.CostEstimate(flops=flops, bytes_accessed=size, transcendentals=exps),
    )(*operands)


def rotary_tables(positions):
    freqs = 500000.0 ** (-(jnp.arange(HALF, dtype=jnp.float32) * 2.0 / HD))
    angles = positions.astype(jnp.float32)[:, None] * freqs[None, :]
    cosine = jnp.cos(angles)
    sine = jnp.sin(angles)
    return (
        jnp.concatenate([cosine, cosine], axis=1),
        jnp.concatenate([-sine, sine], axis=1),
    )


def summed_lanes(refs, lanes):
    total = refs[0][:, lanes].astype(jnp.float32)
    for ref in refs[1:]:
        total = total + ref[:, lanes].astype(jnp.float32)
    return total


def rotated(values, cos_ref, sin_ref):
    return values * cos_ref[...] + pltpu.roll(values, HALF, 1) * sin_ref[...]


def pair_kernel(unused_ref, cos_ref, sin_ref, *refs):
    parts, out_ref = refs[:-1], refs[-1]
    key = rotated(summed_lanes(parts, pl.ds(0, HD)), cos_ref, sin_ref)
    out_ref[:, pl.ds(0, HD)] = key.astype(jnp.bfloat16)
    out_ref[:, pl.ds(HD, HD)] = summed_lanes(parts, pl.ds(HD, HD)).astype(jnp.bfloat16)


def finish_pair(cosine, sine, parts):
    operands = (jnp.zeros((1,), jnp.int32), cosine, sine, *parts)
    shape = jax.ShapeDtypeStruct(parts[0].shape, jnp.bfloat16)
    return local_kernel(pair_kernel, shape, operands, 8 * parts[0].size)


def attention_kernel(blocks, stride, n_query, n_kv, place_ref, cos_ref, sin_ref, *refs):
    query_refs = refs[:n_query]
    kv_refs = refs[n_query : n_query + n_kv]
    out_ref, turned, bias = refs[n_query + n_kv :]
    heads, tokens, _ = turned.shape
    for h in range(heads):
        total = summed_lanes(query_refs, pl.ds(h * HD, HD))
        turned[h] = rotated(total, cos_ref, sin_ref).astype(jnp.bfloat16)
    rows = tokens // blocks
    kv_rows = kv_refs[0].shape[0] // blocks
    documents = place_ref.shape[0] - 1 - n_kv
    scale = HD**-0.5
    for j in range(blocks):
        first = j * rows
        length = kv_rows * (j + 1)
        qpos = lax.broadcasted_iota(jnp.int32, (rows, HD), 0) + (place_ref[0] + j * stride)
        qstart = jnp.zeros_like(qpos)
        for i in range(documents):
            start = place_ref[1 + n_kv + i]
            qstart = jnp.where(qpos >= start, start, qstart)
        span = qpos - qstart
        for d in range(n_kv):
            for b in range(j + 1):
                for c in range(0, kv_rows, HD):
                    kpos = lax.broadcasted_iota(jnp.int32, (rows, HD), 1) + (
                        place_ref[1 + d] + (b * stride + c)
                    )
                    back = qpos - kpos
                    visible = (back >= 0) & (back <= span)
                    bias[:, pl.ds(d * length + b * kv_rows + c, HD)] = jnp.where(
                        visible, 0.0, -jnp.inf
                    )

        def one_head(h, unused):
            query = turned[h, pl.ds(first, rows), :]
            scores = []
            for d in range(n_kv):
                part = lax.dot_general(
                    query,
                    kv_refs[d][pl.ds(0, length), pl.ds(0, HD)],
                    (((1,), (1,)), ((), ())),
                    preferred_element_type=jnp.float32,
                )
                scores.append(part + bias[:, pl.ds(d * length, length)])
            highest = functools.reduce(
                jnp.maximum, [jnp.max(s, axis=1, keepdims=True) for s in scores]
            )
            denominator = 0.0
            mixed = 0.0
            for d in range(n_kv):
                probs = jnp.exp((scores[d] - highest) * scale)
                denominator = denominator + jnp.sum(probs, axis=1, keepdims=True)
                mixed = mixed + jnp.dot(
                    probs.astype(jnp.bfloat16),
                    kv_refs[d][pl.ds(0, length), pl.ds(HD, HD)],
                    preferred_element_type=jnp.float32,
                )
            lanes = pl.ds(pl.multiple_of(h * HD, HD), HD)
            out_ref[pl.ds(first, rows), lanes] = (mixed / denominator).astype(jnp.bfloat16)
            return unused

        lax.fori_loop(0, heads, one_head, 0)


def attention(place, cosine, sine, query_parts, kv_parts, blocks, stride):
    tokens, width = query_parts[0].shape
    heads = width // HD
    keys = sum(part.shape[0] for part in kv_parts)
    return local_kernel(
        functools.partial(attention_kernel, blocks, stride, len(query_parts), len(kv_parts)),
        jax.ShapeDtypeStruct((tokens, width), jnp.bfloat16),
        (place, cosine, sine, *query_parts, *kv_parts),
        4 * tokens * width * keys,
        [
            pltpu.VMEM((heads, tokens, HD), jnp.bfloat16),
            pltpu.VMEM((tokens // blocks, keys), jnp.float32),
        ],
        tokens * heads * keys,
    )


def product_kernel(features_of, weights_of, place_ref, *refs):
    token_refs = refs[:4]
    weight_refs = refs[4:-5]
    out_refs = refs[-5:-1]
    gathered = refs[-1]
    hi = place_ref[0]
    lo = place_ref[1]
    rows = token_refs[0].shape[0]
    for d, token_ref in enumerate(token_refs):
        first = pl.multiple_of(lax.rem(hi - d + 4, 4) * rows, rows)
        gathered[pl.ds(first, rows), :] = token_ref[...]
    for d, out_ref in enumerate(out_refs):
        there = lax.rem(hi + d, 4)
        place = 0
        for weights in weights_of(weight_refs, there):
            total = 0.0
            for r, weight in enumerate(weights):
                total = total + jnp.dot(
                    gathered[:, features_of(lo, r)], weight, preferred_element_type=jnp.float32
                )
            width = total.shape[1]
            out_ref[:, pl.ds(place, width)] = total.astype(jnp.bfloat16)
            place += width


def product(features_of, weights_of, place, token_parts, weights, width):
    rows, depth = token_parts[0].shape
    shape = jax.ShapeDtypeStruct((4 * rows, width), jnp.bfloat16)
    return local_kernel(
        functools.partial(product_kernel, features_of, weights_of),
        (shape,) * 4,
        (place, *token_parts, *weights),
        2 * 4 * rows * depth * 4 * width,
        [pltpu.VMEM((4 * rows, depth), jnp.bfloat16)],
    )


def pair_product(place, token_parts, weights):
    share = weights[0].shape[0] // 2

    def features_of(lo, r):
        return pl.ds(pl.multiple_of((lo ^ r) * share, share), share)

    def weights_of(refs, there):
        columns = pl.ds(pl.multiple_of(there * HD, HD), HD)
        return [
            [ref[pl.ds(g * share, share), columns] for ref in refs[:3]] + [refs[3 + g][:, columns]]
            for g in range(2)
        ]

    return product(features_of, weights_of, place, token_parts, weights, 2 * HD)


def query_product(place, token_parts, weight, chunk, chunks):
    share = weight.shape[1]
    width = weight.shape[2] // 4 // chunks

    def features_of(lo, r):
        return pl.ds(r * share, share)

    def weights_of(refs, there):
        columns = pl.ds(pl.multiple_of((there * chunks + chunk) * width, width), width)
        return [[refs[0][r, :, columns] for r in range(4)]]

    return product(features_of, weights_of, place, token_parts, [weight], width)


def project_kernel(place_ref, *refs):
    own, left, right, weight_ref = refs[0], refs[1:4], refs[4:7], refs[7]
    total_refs = refs[8:-2]
    hi = place_ref[0]
    core = place_ref[1]
    offset = place_ref[2]
    depth = own.shape[1]
    blocks, features, width = weight_ref.shape
    span = features // 4
    for side, out_ref in enumerate(refs[-2:]):
        kept = out_ref.shape[0]
        rows = pl.ds(pl.multiple_of(lax.rem(core + side, 2) * kept, kept), kept)
        attended = [own[rows, :]]
        for k in range(1, 4):
            attended.append(jnp.where(hi >= k, left[k - 1][rows, :], right[3 - k][rows, :]))
        for r in range(blocks):
            columns = pl.ds(r * width, width)
            total = total_refs[side][:, columns] if total_refs else 0.0
            for k in range(4):
                first = lax.rem(hi - k + 4, 4) * span + offset
                total = total + jnp.dot(
                    attended[k],
                    weight_ref[r, pl.ds(pl.multiple_of(first, depth), depth), :],
                    preferred_element_type=jnp.float32,
                )
            out_ref[:, columns] = total.astype(out_ref.dtype)


def project(place, attended_parts, weight, totals, kind):
    tokens, depth = attended_parts[0].shape
    blocks, _, width = weight.shape
    shape = jax.ShapeDtypeStruct((tokens // 2, blocks * width), kind)
    return local_kernel(
        project_kernel,
        (shape, shape),
        (place, *attended_parts, weight, *totals),
        2 * tokens * 4 * depth * blocks * width,
    )


def normalised(tokens, norm_gain):
    source = tokens.astype(jnp.float32)
    return (
        source * lax.rsqrt(jnp.mean(source * source, axis=1, keepdims=True) + 1e-05) * norm_gain
    ).astype(jnp.bfloat16)


def plain_device(tokens, norm_gain, w_query, w_key, w_value, w_out, doc_starts):
    rows = tokens.shape[0]
    first = lax.axis_index("ctx") * rows
    normed = normalised(tokens, norm_gain)

    def project_with(weight):
        gathered = lax.all_gather(weight, "ctx", axis=0, tiled=True)
        total = jnp.dot(normed, gathered, preferred_element_type=jnp.float32)
        return total.astype(jnp.bfloat16)

    cosine, sine = rotary_tables(first + jnp.arange(rows, dtype=jnp.int32))
    place = jnp.concatenate([jnp.stack([first, jnp.zeros_like(first)]), doc_starts])
    query = project_with(w_query)
    key = project_with(w_key)
    value = project_with(w_value)
    kv_local = w_key.shape[1] // HD
    group = w_query.shape[1] // kv_local
    mixed = []
    for h in range(kv_local):
        lanes = slice(h * HD, (h + 1) * HD)
        pair = jnp.concatenate([key[:, lanes], value[:, lanes]], axis=1)
        pair = lax.all_gather(finish_pair(cosine, sine, [pair]), "ctx", axis=0, tiled=True)
        part = query[:, h * group : (h + 1) * group]
        mixed.append(attention(place, cosine, sine, [part], [pair], 1, 0))
    attended = jnp.concatenate(mixed, axis=1)
    wide = lax.all_gather(w_out, "ctx", axis=1, tiled=True)
    partial_out = jnp.dot(attended, wide, preferred_element_type=jnp.float32)
    return lax.psum_scatter(
        partial_out.astype(jnp.bfloat16), "head", scatter_dimension=1, tiled=True
    )


def beside(block, r):
    return lax.ppermute(block, "lo", [(i, i ^ r) for i in range(4)])


def sides(block):
    return [block, beside(block, 1), beside(block, 2)]


def corner(blocks):
    half = blocks[0].shape[0] // 2
    return [*blocks, beside(blocks[2][:half], 1), beside(blocks[1][half:], 2)]


def along_line(pieces):
    return [pieces[0]] + [
        lax.ppermute(pieces[d], "hi", [(i, (i + d) % 4) for i in range(4)]) for d in range(1, 4)
    ]


def pass_on(block):
    blocks = [block]
    for step in (1, -1):
        moving = block
        for _ in range(3):
            moving = lax.ppermute(
                moving, "hi", [(i, i + step) for i in range(4) if 0 <= i + step < 4]
            )
            blocks.append(moving)
    return blocks


def line_device(tokens, norm_gain, w_query, w_key, w_value, w_out, doc_starts):
    rows, features = tokens.shape
    hi = lax.axis_index("hi")
    lo = lax.axis_index("lo")
    core = lax.axis_index("head")
    depth = features // 4
    heads = w_query.shape[1] // 4
    half = heads // 2
    place = jnp.stack([hi, lo])

    query_weight = lax.all_gather(w_query, "lo", axis=0)
    out_weight = lax.all_gather(w_out, "lo", axis=0)
    pair_weight = corner(sides(jnp.concatenate([w_key, w_value], axis=0)))

    normed = normalised(tokens, norm_gain)
    token_parts = along_line(
        [lax.dynamic_slice_in_dim(normed, lax.rem(hi + d, 4) * depth, depth, 1) for d in range(4)]
    )

    row_index = jnp.arange(4 * rows, dtype=jnp.int32)
    cosine, sine = rotary_tables((row_index // rows * 4 + lo) * rows + row_index % rows)
    kv_own = finish_pair(
        cosine, sine, along_line(pair_product(place, token_parts, pair_weight))
    )
    kv_parts = [kv_own] + [beside(kv_own, r) for r in range(1, 4)]

    firsts = jnp.stack([lo, lo, lo ^ 1, lo ^ 2, lo ^ 3]) * rows
    seen = jnp.concatenate([firsts, doc_starts])
    totals = ()
    kinds = (jnp.float32, jnp.bfloat16)
    for c in range(2):
        query_parts = along_line(query_product(place, token_parts, query_weight, c, 2))
        attended = attention(seen, cosine, sine, query_parts, kv_parts, 4, 4 * rows)
        where = jnp.stack([hi, core, jnp.full((), c * half, jnp.int32)])
        totals = project(where, pass_on(attended), out_weight, totals, kinds[c])

    mine, theirs = totals
    theirs = lax.ppermute(theirs, "head", [(0, 1), (1, 0)])
    summed = (mine.astype(jnp.float32) + theirs.astype(jnp.float32)).astype(jnp.bfloat16)
    arrived = []
    for e in range(2):
        block = lax.rem(hi + e, 2)
        piece = lax.dynamic_slice_in_dim(summed, block * rows, rows, 0)
        route = [(z * 2 + g, (2 * g + (z + e) % 2) * 2 + z // 2) for z in range(4) for g in range(2)]
        arrived.append(lax.ppermute(piece, ("hi", "head"), route))
    even = lax.rem(hi, 2) == 0
    return jnp.concatenate(
        [jnp.where(even, arrived[0], arrived[1]), jnp.where(even, arrived[1], arrived[0])], axis=1
    )


def solution(mesh):
    ctx = mesh.shape["ctx"]
    heads = mesh.shape["head"]

    def run(tokens, norm_gain, w_query, w_key, w_value, w_out, doc_starts):
        lines = w_key.shape[1] // HD // heads
        if (ctx, heads, lines) == (16, 2, 4):
            both = ("hi", "lo")
            grid = Mesh(mesh.devices.reshape(4, 4, 2), ("hi", "lo", "head"))
            body = line_device
        else:
            both, grid, body = "ctx", mesh, plain_device
        placed = (
            P(both, None),
            P(),
            P(both, "head"),
            P(both, "head"),
            P(both, "head"),
            P("head", both),
            P(),
        )
        return jax.shard_map(
            body, mesh=grid, in_specs=placed, out_specs=P(both, "head"), check_vma=False
        )(tokens, norm_gain, w_query, w_key, w_value, w_out, doc_starts)

    return run
```

```python
import functools

import jax
import jax.numpy as jnp
from jax import lax
from jax.experimental import pallas as pl
from jax.experimental.pallas import tpu as pltpu
from jax.sharding import Mesh
from jax.sharding import PartitionSpec as P

HD = 128
HALF = HD // 2
MIB = 1024 * 1024


def local_kernel(body, out_shape, operands, flops, scratch=(), exps=0):
    size = sum(x.size * x.dtype.itemsize for x in operands)
    return pl.pallas_call(
        body,
        in_specs=[pl.BlockSpec(memory_space=pltpu.SMEM)]
        + [pl.BlockSpec(memory_space=pltpu.VMEM)] * (len(operands) - 1),
        out_shape=out_shape,
        scratch_shapes=scratch,
        compiler_params=pltpu.CompilerParams(vmem_limit_bytes=12 * MIB),
        cost_estimate=pl.CostEstimate(flops=flops, bytes_accessed=size, transcendentals=exps),
    )(*operands)


def rotary_tables(positions):
    freqs = 500000.0 ** (-(jnp.arange(HALF, dtype=jnp.float32) * 2.0 / HD))
    angles = positions.astype(jnp.float32)[:, None] * freqs[None, :]
    cosine = jnp.cos(angles)
    sine = jnp.sin(angles)
    return (
        jnp.concatenate([cosine, cosine], axis=1),
        jnp.concatenate([-sine, sine], axis=1),
    )


def summed_lanes(refs, lanes):
    total = refs[0][:, lanes].astype(jnp.float32)
    for ref in refs[1:]:
        total = total + ref[:, lanes].astype(jnp.float32)
    return total


def rotated(values, cos_ref, sin_ref):
    return values * cos_ref[...] + pltpu.roll(values, HALF, 1) * sin_ref[...]


def pair_kernel(unused_ref, cos_ref, sin_ref, *refs):
    parts, out_ref = refs[:-1], refs[-1]
    key = rotated(summed_lanes(parts, pl.ds(0, HD)), cos_ref, sin_ref)
    out_ref[:, pl.ds(0, HD)] = key.astype(jnp.bfloat16)
    out_ref[:, pl.ds(HD, HD)] = summed_lanes(parts, pl.ds(HD, HD)).astype(jnp.bfloat16)


def finish_pair(cosine, sine, parts):
    operands = (jnp.zeros((1,), jnp.int32), cosine, sine, *parts)
    shape = jax.ShapeDtypeStruct(parts[0].shape, jnp.bfloat16)
    return local_kernel(pair_kernel, shape, operands, 8 * parts[0].size)


def attention_kernel(blocks, stride, n_query, n_kv, place_ref, cos_ref, sin_ref, *refs):
    query_refs = refs[:n_query]
    kv_refs = refs[n_query : n_query + n_kv]
    out_ref, turned, bias = refs[n_query + n_kv :]
    heads, tokens, _ = turned.shape
    for h in range(heads):
        total = summed_lanes(query_refs, pl.ds(h * HD, HD))
        turned[h] = rotated(total, cos_ref, sin_ref).astype(jnp.bfloat16)
    rows = tokens // blocks
    kv_rows = kv_refs[0].shape[0] // blocks
    documents = place_ref.shape[0] - 1 - n_kv
    scale = HD**-0.5
    for j in range(blocks):
        first = j * rows
        length = kv_rows * (j + 1)
        qpos = lax.broadcasted_iota(jnp.int32, (rows, HD), 0) + (place_ref[0] + j * stride)
        qstart = jnp.zeros_like(qpos)
        for i in range(documents):
            start = place_ref[1 + n_kv + i]
            qstart = jnp.where(qpos >= start, start, qstart)
        span = qpos - qstart
        for d in range(n_kv):
            for b in range(j + 1):
                for c in range(0, kv_rows, HD):
                    kpos = lax.broadcasted_iota(jnp.int32, (rows, HD), 1) + (
                        place_ref[1 + d] + (b * stride + c)
                    )
                    back = qpos - kpos
                    visible = (back >= 0) & (back <= span)
                    bias[:, pl.ds(d * length + b * kv_rows + c, HD)] = jnp.where(
                        visible, 0.0, -jnp.inf
                    )

        def one_head(h, unused):
            query = turned[h, pl.ds(first, rows), :]
            scores = []
            for d in range(n_kv):
                part = lax.dot_general(
                    query,
                    kv_refs[d][pl.ds(0, length), pl.ds(0, HD)],
                    (((1,), (1,)), ((), ())),
                    preferred_element_type=jnp.float32,
                )
                scores.append(part + bias[:, pl.ds(d * length, length)])
            highest = functools.reduce(
                jnp.maximum, [jnp.max(s, axis=1, keepdims=True) for s in scores]
            )
            denominator = 0.0
            mixed = 0.0
            for d in range(n_kv):
                probs = jnp.exp((scores[d] - highest) * scale)
                denominator = denominator + jnp.sum(probs, axis=1, keepdims=True)
                mixed = mixed + jnp.dot(
                    probs.astype(jnp.bfloat16),
                    kv_refs[d][pl.ds(0, length), pl.ds(HD, HD)],
                    preferred_element_type=jnp.float32,
                )
            lanes = pl.ds(pl.multiple_of(h * HD, HD), HD)
            out_ref[pl.ds(first, rows), lanes] = (mixed / denominator).astype(jnp.bfloat16)
            return unused

        lax.fori_loop(0, heads, one_head, 0)


def attention(place, cosine, sine, query_parts, kv_parts, blocks, stride):
    tokens, width = query_parts[0].shape
    heads = width // HD
    keys = sum(part.shape[0] for part in kv_parts)
    return local_kernel(
        functools.partial(attention_kernel, blocks, stride, len(query_parts), len(kv_parts)),
        jax.ShapeDtypeStruct((tokens, width), jnp.bfloat16),
        (place, cosine, sine, *query_parts, *kv_parts),
        4 * tokens * width * keys,
        [
            pltpu.VMEM((heads, tokens, HD), jnp.bfloat16),
            pltpu.VMEM((tokens // blocks, keys), jnp.float32),
        ],
        tokens * heads * keys,
    )


def product_kernel(place_ref, *refs):
    token_refs, weight_refs, out_refs, gathered = refs[:4], refs[4:9], refs[9:11], refs[11]
    hi = place_ref[0]
    lo = place_ref[1]
    rows = token_refs[0].shape[0]
    share = weight_refs[3].shape[0]
    for d, token_ref in enumerate(token_refs):
        gathered[pl.ds(pl.multiple_of((hi ^ d) * rows, rows), rows), :] = token_ref[...]
    for side, out_ref in enumerate(out_refs):
        width = out_ref.shape[1]
        columns = pl.ds(pl.multiple_of((lax.div(hi, 2) ^ side) * width, width), width)
        total = 0.0
        for part in range(2):
            for r in range(4):
                if r < 3:
                    weight = weight_refs[r][pl.ds(part * share, share), columns]
                else:
                    weight = weight_refs[3 + part][:, columns]
                block = (lax.rem(hi, 2) ^ part) * 4 + (lo ^ r)
                total = total + jnp.dot(
                    gathered[:, pl.ds(pl.multiple_of(block * share, share), share)],
                    weight,
                    preferred_element_type=jnp.float32,
                )
        out_ref[...] = total.astype(jnp.bfloat16)


def product(place, token_parts, weights):
    rows, depth = token_parts[0].shape
    width = weights[0].shape[1] // 2
    shape = jax.ShapeDtypeStruct((4 * rows, width), jnp.bfloat16)
    return local_kernel(
        product_kernel,
        (shape,) * 2,
        (place, *token_parts, *weights),
        2 * 4 * rows * depth * 2 * width,
        [pltpu.VMEM((4 * rows, depth), jnp.bfloat16)],
    )


def project_kernel(place_ref, *refs):
    attended_refs = refs[:4]
    weight_refs = refs[4:8]
    total_refs = refs[8:-2]
    hi = place_ref[0]
    lo = place_ref[1]
    core = place_ref[2]
    offset = place_ref[3]
    depth = attended_refs[0].shape[1]
    width = weight_refs[0].shape[1]
    span = weight_refs[0].shape[0] // 4
    for side, out_ref in enumerate(refs[-2:]):
        kept = out_ref.shape[0]
        rows = pl.ds(pl.multiple_of(lax.rem(core + side, 2) * kept, kept), kept)
        for r, weight_ref in enumerate(weight_refs):
            columns = pl.ds(pl.multiple_of((lo ^ r) * width, width), width)
            total = total_refs[side][:, columns] if total_refs else 0.0
            for k, attended_ref in enumerate(attended_refs):
                first = lax.rem(hi - k + 4, 4) * span + offset
                total = total + jnp.dot(
                    attended_ref[rows, :],
                    weight_ref[pl.ds(pl.multiple_of(first, depth), depth), :],
                    preferred_element_type=jnp.float32,
                )
            out_ref[:, columns] = total.astype(out_ref.dtype)


def project(place, attended_parts, weights, totals, kind):
    tokens, depth = attended_parts[0].shape
    width = weights[0].shape[1]
    shape = jax.ShapeDtypeStruct((tokens // 2, 4 * width), kind)
    return local_kernel(
        project_kernel,
        (shape, shape),
        (place, *attended_parts, *weights, *totals),
        2 * tokens * 4 * depth * 4 * width,
    )


def normalised(tokens, norm_gain):
    source = tokens.astype(jnp.float32)
    return (
        source * lax.rsqrt(jnp.mean(source * source, axis=1, keepdims=True) + 1e-05) * norm_gain
    ).astype(jnp.bfloat16)


def plain_device(tokens, norm_gain, w_query, w_key, w_value, w_out, doc_starts):
    rows = tokens.shape[0]
    first = lax.axis_index("ctx") * rows
    normed = normalised(tokens, norm_gain)

    def project_with(weight):
        gathered = lax.all_gather(weight, "ctx", axis=0, tiled=True)
        total = jnp.dot(normed, gathered, preferred_element_type=jnp.float32)
        return total.astype(jnp.bfloat16)

    cosine, sine = rotary_tables(first + jnp.arange(rows, dtype=jnp.int32))
    place = jnp.concatenate([jnp.stack([first, jnp.zeros_like(first)]), doc_starts])
    query = project_with(w_query)
    key = project_with(w_key)
    value = project_with(w_value)
    kv_local = w_key.shape[1] // HD
    group = w_query.shape[1] // kv_local
    mixed = []
    for h in range(kv_local):
        lanes = slice(h * HD, (h + 1) * HD)
        pair = jnp.concatenate([key[:, lanes], value[:, lanes]], axis=1)
        pair = lax.all_gather(finish_pair(cosine, sine, [pair]), "ctx", axis=0, tiled=True)
        part = query[:, h * group : (h + 1) * group]
        mixed.append(attention(place, cosine, sine, [part], [pair], 1, 0))
    attended = jnp.concatenate(mixed, axis=1)
    wide = lax.all_gather(w_out, "ctx", axis=1, tiled=True)
    partial_out = jnp.dot(attended, wide, preferred_element_type=jnp.float32)
    return lax.psum_scatter(
        partial_out.astype(jnp.bfloat16), "head", scatter_dimension=1, tiled=True
    )


def after(value, *earlier):
    return lax.optimization_barrier((value, *earlier))[0]


def beside(block, r):
    return lax.ppermute(block, "lo", [(i, i ^ r) for i in range(4)])


def sides(block):
    return [block, beside(block, 1), beside(block, 2)]


def corner(blocks):
    half = blocks[0].shape[0] // 2
    return [*blocks, beside(blocks[2][:half], 1), beside(blocks[1][half:], 2)]


def along(block, d):
    return lax.ppermute(block, "hi", [(i, i ^ d) for i in range(4)])


def round_line(block):
    return [block] + [
        lax.ppermute(block, "hi", [(i, (i + d) % 4) for i in range(4)]) for d in range(1, 4)
    ]


def line_device(tokens, norm_gain, w_query, w_key, w_value, w_out, doc_starts):
    rows, features = tokens.shape
    hi = lax.axis_index("hi")
    lo = lax.axis_index("lo")
    core = lax.axis_index("head")
    which_half = lax.div(hi, 2)
    which = lax.rem(hi, 2)
    depth = features // 2
    heads = w_query.shape[1] // 4
    width = heads // 2
    place = jnp.stack([hi, lo])

    def columns_for(chip, sources, width):
        return jnp.concatenate(
            [
                lax.dynamic_slice_in_dim(w, (2 * z + chip) * step + first, width, 1)
                for z in range(2)
                for w, step, first in sources
            ],
            axis=1,
        )

    stage = ()
    weights = []
    for sources, size in (
        ([(w_key, HD, 0), (w_value, HD, 0)], HD),
        ([(w_query, heads, 0)], width),
        ([(w_query, heads, width)], width),
    ):
        came = along(columns_for(1 - which, sources, size), 1)
        both = jnp.concatenate([columns_for(which, sources, size), came], axis=0)
        stage = sides(after(both, *stage) if stage else both)
        weights.append(corner(stage))
        stage = stage[1:]

    normed = normalised(tokens, norm_gain)
    own = lax.dynamic_slice_in_dim(normed, which_half * depth, depth, 1)
    other = along(lax.dynamic_slice_in_dim(normed, (1 - which_half) * depth, depth, 1), 2)
    token_parts = [own, along(own, 1), other, along(other, 1)]

    row_index = jnp.arange(4 * rows, dtype=jnp.int32)
    cosine, sine = rotary_tables((row_index // rows * 4 + lo) * rows + row_index % rows)

    def summed_parts(weight):
        kept, sent = product(place, token_parts, weight)
        return [kept, along(sent, 2)]

    kv_own = finish_pair(cosine, sine, summed_parts(weights[0]))
    kv_parts = [kv_own] + [beside(kv_own, r) for r in range(1, 4)]

    firsts = jnp.stack([lo, lo, lo ^ 1, lo ^ 2, lo ^ 3]) * rows
    seen = jnp.concatenate([firsts, doc_starts])
    out_sides = sides(after(w_out, *weights[2][3:], *kv_parts[1:]))
    attended = [
        attention(seen, cosine, sine, summed_parts(weight), kv_parts, 4, 4 * rows)
        for weight in weights[1:]
    ]
    out_sides[1:] = lax.optimization_barrier((*out_sides[1:], attended[0]))[:2]
    out_blocks = corner(out_sides)
    out_blocks[3:] = [jnp.concatenate(out_blocks[3:], axis=0)]
    totals = ()
    for c, kind in enumerate((jnp.float32, jnp.bfloat16)):
        where = jnp.stack([hi, lo, core, jnp.full((), c * width, jnp.int32)])
        totals = project(where, round_line(attended[c]), out_blocks, totals, kind)

    mine, theirs = totals
    theirs = lax.ppermute(theirs, "head", [(0, 1), (1, 0)])
    summed = (mine.astype(jnp.float32) + theirs.astype(jnp.float32)).astype(jnp.bfloat16)
    arrived = []
    for e in range(2):
        block = lax.rem(hi + e, 2)
        piece = lax.dynamic_slice_in_dim(summed, block * rows, rows, 0)
        route = [(z * 2 + g, (2 * g + (z + e) % 2) * 2 + z // 2) for z in range(4) for g in range(2)]
        arrived.append(lax.ppermute(piece, ("hi", "head"), route))
    even = lax.rem(hi, 2) == 0
    return jnp.concatenate(
        [jnp.where(even, arrived[0], arrived[1]), jnp.where(even, arrived[1], arrived[0])], axis=1
    )


def solution(mesh):
    ctx = mesh.shape["ctx"]
    heads = mesh.shape["head"]

    def run(tokens, norm_gain, w_query, w_key, w_value, w_out, doc_starts):
        lines = w_key.shape[1] // HD // heads
        if (ctx, heads, lines) == (16, 2, 4):
            both = ("hi", "lo")
            grid = Mesh(mesh.devices.reshape(4, 4, 2), ("hi", "lo", "head"))
            body = line_device
        else:
            both, grid, body = "ctx", mesh, plain_device
        placed = (
            P(both, None),
            P(),
            P(both, "head"),
            P(both, "head"),
            P(both, "head"),
            P("head", both),
            P(),
        )
        return jax.shard_map(
            body, mesh=grid, in_specs=placed, out_specs=P(both, "head"), check_vma=False
        )(tokens, norm_gain, w_query, w_key, w_value, w_out, doc_starts)

    return run
```

```python
import functools

import jax
import jax.numpy as jnp
from jax import lax
from jax.experimental import pallas as pl
from jax.experimental.pallas import tpu as pltpu
from jax.sharding import Mesh
from jax.sharding import PartitionSpec as P

HD = 128
HALF = HD // 2
MIB = 1024 * 1024


def local_kernel(body, out_shape, operands, flops, scratch=(), exps=0):
    size = sum(x.size * x.dtype.itemsize for x in operands)
    return pl.pallas_call(
        body,
        in_specs=[pl.BlockSpec(memory_space=pltpu.SMEM)]
        + [pl.BlockSpec(memory_space=pltpu.VMEM)] * (len(operands) - 1),
        out_shape=out_shape,
        scratch_shapes=scratch,
        compiler_params=pltpu.CompilerParams(vmem_limit_bytes=12 * MIB),
        cost_estimate=pl.CostEstimate(flops=flops, bytes_accessed=size, transcendentals=exps),
    )(*operands)


def rotary_tables(positions):
    freqs = 500000.0 ** (-(jnp.arange(HALF, dtype=jnp.float32) * 2.0 / HD))
    angles = positions.astype(jnp.float32)[:, None] * freqs[None, :]
    cosine = jnp.cos(angles)
    sine = jnp.sin(angles)
    return (
        jnp.concatenate([cosine, cosine], axis=1),
        jnp.concatenate([-sine, sine], axis=1),
    )


def summed_lanes(refs, lanes):
    total = refs[0][:, lanes].astype(jnp.float32)
    for ref in refs[1:]:
        total = total + ref[:, lanes].astype(jnp.float32)
    return total


def rotated(values, cos_ref, sin_ref):
    return values * cos_ref[...] + pltpu.roll(values, HALF, 1) * sin_ref[...]


def pair_kernel(unused_ref, cos_ref, sin_ref, *refs):
    parts, out_ref = refs[:-1], refs[-1]
    key = rotated(summed_lanes(parts, pl.ds(0, HD)), cos_ref, sin_ref)
    out_ref[:, pl.ds(0, HD)] = key.astype(jnp.bfloat16)
    out_ref[:, pl.ds(HD, HD)] = summed_lanes(parts, pl.ds(HD, HD)).astype(jnp.bfloat16)


def finish_pair(cosine, sine, parts):
    operands = (jnp.zeros((1,), jnp.int32), cosine, sine, *parts)
    shape = jax.ShapeDtypeStruct(parts[0].shape, jnp.bfloat16)
    return local_kernel(pair_kernel, shape, operands, 8 * parts[0].size)


def attention_kernel(blocks, stride, n_query, n_kv, place_ref, cos_ref, sin_ref, *refs):
    query_refs = refs[:n_query]
    kv_refs = refs[n_query : n_query + n_kv]
    out_ref, turned, bias = refs[n_query + n_kv :]
    heads, tokens, _ = turned.shape
    for h in range(heads):
        total = summed_lanes(query_refs, pl.ds(h * HD, HD))
        turned[h] = rotated(total, cos_ref, sin_ref).astype(jnp.bfloat16)
    rows = tokens // blocks
    kv_rows = kv_refs[0].shape[0] // blocks
    documents = place_ref.shape[0] - 1 - n_kv
    scale = HD**-0.5
    for j in range(blocks):
        first = j * rows
        length = kv_rows * (j + 1)
        qpos = lax.broadcasted_iota(jnp.int32, (rows, HD), 0) + (place_ref[0] + j * stride)
        qstart = jnp.zeros_like(qpos)
        for i in range(documents):
            start = place_ref[1 + n_kv + i]
            qstart = jnp.where(qpos >= start, start, qstart)
        span = qpos - qstart
        for d in range(n_kv):
            for b in range(j + 1):
                for c in range(0, kv_rows, HD):
                    kpos = lax.broadcasted_iota(jnp.int32, (rows, HD), 1) + (
                        place_ref[1 + d] + (b * stride + c)
                    )
                    back = qpos - kpos
                    visible = (back >= 0) & (back <= span)
                    bias[:, pl.ds(d * length + b * kv_rows + c, HD)] = jnp.where(
                        visible, 0.0, -jnp.inf
                    )

        def one_head(h, unused):
            query = turned[h, pl.ds(first, rows), :]
            scores = []
            for d in range(n_kv):
                part = lax.dot_general(
                    query,
                    kv_refs[d][pl.ds(0, length), pl.ds(0, HD)],
                    (((1,), (1,)), ((), ())),
                    preferred_element_type=jnp.float32,
                )
                scores.append(part + bias[:, pl.ds(d * length, length)])
            highest = functools.reduce(
                jnp.maximum, [jnp.max(s, axis=1, keepdims=True) for s in scores]
            )
            denominator = 0.0
            mixed = 0.0
            for d in range(n_kv):
                probs = jnp.exp((scores[d] - highest) * scale)
                denominator = denominator + jnp.sum(probs, axis=1, keepdims=True)
                mixed = mixed + jnp.dot(
                    probs.astype(jnp.bfloat16),
                    kv_refs[d][pl.ds(0, length), pl.ds(HD, HD)],
                    preferred_element_type=jnp.float32,
                )
            lanes = pl.ds(pl.multiple_of(h * HD, HD), HD)
            out_ref[pl.ds(first, rows), lanes] = (mixed / denominator).astype(jnp.bfloat16)
            return unused

        lax.fori_loop(0, heads, one_head, 0)


def attention(place, cosine, sine, query_parts, kv_parts, blocks, stride):
    tokens, width = query_parts[0].shape
    heads = width // HD
    keys = sum(part.shape[0] for part in kv_parts)
    return local_kernel(
        functools.partial(attention_kernel, blocks, stride, len(query_parts), len(kv_parts)),
        jax.ShapeDtypeStruct((tokens, width), jnp.bfloat16),
        (place, cosine, sine, *query_parts, *kv_parts),
        32 * tokens * width * keys,
        [
            pltpu.VMEM((heads, tokens, HD), jnp.bfloat16),
            pltpu.VMEM((tokens // blocks, keys), jnp.float32),
        ],
        tokens * heads * keys,
    )


def product_kernel(place_ref, *refs):
    token_refs, weight_refs, out_refs, gathered = refs[:4], refs[4:9], refs[9:11], refs[11]
    hi = place_ref[0]
    lo = place_ref[1]
    rows = token_refs[0].shape[0]
    share = weight_refs[3].shape[0]
    for d, token_ref in enumerate(token_refs):
        gathered[pl.ds(pl.multiple_of((hi ^ d) * rows, rows), rows), :] = token_ref[...]
    for side, out_ref in enumerate(out_refs):
        width = out_ref.shape[1]
        first = (lax.div(hi, 2) ^ side) * place_ref[2] + place_ref[3]
        columns = pl.ds(pl.multiple_of(first, width), width)
        total = 0.0
        for part in range(2):
            for r in range(4):
                if r < 3:
                    weight = weight_refs[r][pl.ds(part * share, share), columns]
                else:
                    weight = weight_refs[3 + part][:, columns]
                block = (lax.rem(hi, 2) ^ part) * 4 + (lo ^ r)
                total = total + jnp.dot(
                    gathered[:, pl.ds(pl.multiple_of(block * share, share), share)],
                    weight,
                    preferred_element_type=jnp.float32,
                )
        out_ref[...] = total.astype(jnp.bfloat16)


def product(hi, lo, token_parts, weights, chunk, chunks):
    rows, depth = token_parts[0].shape
    step = weights[0].shape[1] // 2
    width = step // chunks
    place = jnp.stack([hi, lo, jnp.full((), step, jnp.int32), jnp.full((), chunk * width, jnp.int32)])
    shape = jax.ShapeDtypeStruct((4 * rows, width), jnp.bfloat16)
    return local_kernel(
        product_kernel,
        (shape,) * 2,
        (place, *token_parts, *weights),
        2 * 4 * rows * depth * 2 * width,
        [pltpu.VMEM((4 * rows, depth), jnp.bfloat16)],
    )


def project_kernel(place_ref, *refs):
    attended_refs = refs[:4]
    weight_refs = refs[4:8]
    total_refs = refs[8:-2]
    hi = place_ref[0]
    lo = place_ref[1]
    core = place_ref[2]
    offset = place_ref[3]
    depth = attended_refs[0].shape[1]
    width = weight_refs[0].shape[1]
    span = weight_refs[0].shape[0] // 4
    for side, out_ref in enumerate(refs[-2:]):
        kept = out_ref.shape[0]
        rows = pl.ds(pl.multiple_of(lax.rem(core + side, 2) * kept, kept), kept)
        for r, weight_ref in enumerate(weight_refs):
            columns = pl.ds(pl.multiple_of((lo ^ r) * width, width), width)
            total = total_refs[side][:, columns] if total_refs else 0.0
            for k, attended_ref in enumerate(attended_refs):
                first = lax.rem(hi - k + 4, 4) * span + offset
                total = total + jnp.dot(
                    attended_ref[rows, :],
                    weight_ref[pl.ds(pl.multiple_of(first, depth), depth), :],
                    preferred_element_type=jnp.float32,
                )
            out_ref[:, columns] = total.astype(out_ref.dtype)


def project(place, attended_parts, weights, totals, kind):
    tokens, depth = attended_parts[0].shape
    width = weights[0].shape[1]
    shape = jax.ShapeDtypeStruct((tokens // 2, 4 * width), kind)
    return local_kernel(
        project_kernel,
        (shape, shape),
        (place, *attended_parts, *weights, *totals),
        2 * tokens * 4 * depth * 4 * width,
    )


def normalised(tokens, norm_gain):
    source = tokens.astype(jnp.float32)
    return (
        source * lax.rsqrt(jnp.mean(source * source, axis=1, keepdims=True) + 1e-05) * norm_gain
    ).astype(jnp.bfloat16)


def plain_device(tokens, norm_gain, w_query, w_key, w_value, w_out, doc_starts):
    rows = tokens.shape[0]
    first = lax.axis_index("ctx") * rows
    normed = normalised(tokens, norm_gain)

    def project_with(weight):
        gathered = lax.all_gather(weight, "ctx", axis=0, tiled=True)
        total = jnp.dot(normed, gathered, preferred_element_type=jnp.float32)
        return total.astype(jnp.bfloat16)

    cosine, sine = rotary_tables(first + jnp.arange(rows, dtype=jnp.int32))
    place = jnp.concatenate([jnp.stack([first, jnp.zeros_like(first)]), doc_starts])
    query = project_with(w_query)
    key = project_with(w_key)
    value = project_with(w_value)
    kv_local = w_key.shape[1] // HD
    group = w_query.shape[1] // kv_local
    mixed = []
    for h in range(kv_local):
        lanes = slice(h * HD, (h + 1) * HD)
        pair = jnp.concatenate([key[:, lanes], value[:, lanes]], axis=1)
        pair = lax.all_gather(finish_pair(cosine, sine, [pair]), "ctx", axis=0, tiled=True)
        part = query[:, h * group : (h + 1) * group]
        mixed.append(attention(place, cosine, sine, [part], [pair], 1, 0))
    attended = jnp.concatenate(mixed, axis=1)
    wide = lax.all_gather(w_out, "ctx", axis=1, tiled=True)
    partial_out = jnp.dot(attended, wide, preferred_element_type=jnp.float32)
    return lax.psum_scatter(
        partial_out.astype(jnp.bfloat16), "head", scatter_dimension=1, tiled=True
    )


def after(value, *earlier):
    return lax.optimization_barrier((value, *earlier))[0]


def beside(block, r):
    return lax.ppermute(block, "lo", [(i, i ^ r) for i in range(4)])


def sides(block):
    return [block, beside(block, 1), beside(block, 2)]


def corner(blocks):
    half = blocks[0].shape[0] // 2
    return [*blocks, beside(blocks[2][:half], 1), beside(blocks[1][half:], 2)]


def along(block, d):
    return lax.ppermute(block, "hi", [(i, i ^ d) for i in range(4)])


def round_line(block):
    return [block] + [
        lax.ppermute(block, "hi", [(i, (i + d) % 4) for i in range(4)]) for d in range(1, 4)
    ]


def line_device(tokens, norm_gain, w_query, w_key, w_value, w_out, doc_starts):
    rows, features = tokens.shape
    hi = lax.axis_index("hi")
    lo = lax.axis_index("lo")
    core = lax.axis_index("head")
    which_half = lax.div(hi, 2)
    which = lax.rem(hi, 2)
    depth = features // 2
    heads = w_query.shape[1] // 4
    width = heads // 2

    def columns_for(chip, sources, width):
        return jnp.concatenate(
            [
                lax.dynamic_slice_in_dim(w, (2 * z + chip) * width, width, 1)
                for z in range(2)
                for w in sources
            ],
            axis=1,
        )

    stage = ()
    weights = []
    for sources, size in (((w_key, w_value), HD), ((w_query,), heads)):
        came = along(columns_for(1 - which, sources, size), 1)
        both = jnp.concatenate([columns_for(which, sources, size), came], axis=0)
        stage = sides(after(both, *stage) if stage else both)
        weights.append(corner(stage))
        stage = stage[1:]

    normed = normalised(tokens, norm_gain)
    own = lax.dynamic_slice_in_dim(normed, which_half * depth, depth, 1)
    other = along(lax.dynamic_slice_in_dim(normed, (1 - which_half) * depth, depth, 1), 2)
    token_parts = [own, along(own, 1), other, along(other, 1)]

    row_index = jnp.arange(4 * rows, dtype=jnp.int32)
    cosine, sine = rotary_tables((row_index // rows * 4 + lo) * rows + row_index % rows)

    kept, sent = product(hi, lo, token_parts, weights[0], 0, 1)
    kv_own = finish_pair(cosine, sine, [kept, along(sent, 2)])
    kv_parts = [kv_own] + [beside(kv_own, r) for r in range(1, 4)]

    firsts = jnp.stack([lo, lo, lo ^ 1, lo ^ 2, lo ^ 3]) * rows
    seen = jnp.concatenate([firsts, doc_starts])
    out_sides = sides(after(w_out, *weights[1][3:], *kv_parts[1:]))
    products = [product(hi, lo, token_parts, weights[1], c, 2) for c in range(2)]
    products[0] = (after(products[0][0], products[1][0]), products[0][1])
    attended = [
        attention(seen, cosine, sine, [kept, along(sent, 2)], kv_parts, 4, 4 * rows)
        for kept, sent in products
    ]
    out_sides[1:] = lax.optimization_barrier((*out_sides[1:], attended[1]))[:2]
    out_blocks = corner(out_sides)
    out_blocks[3:] = [jnp.concatenate(out_blocks[3:], axis=0)]
    totals = ()
    for c, kind in enumerate((jnp.float32, jnp.bfloat16)):
        where = jnp.stack([hi, lo, core, jnp.full((), c * width, jnp.int32)])
        totals = project(where, round_line(attended[c]), out_blocks, totals, kind)

    mine, theirs = totals
    theirs = lax.ppermute(theirs, "head", [(0, 1), (1, 0)])
    summed = (mine.astype(jnp.float32) + theirs.astype(jnp.float32)).astype(jnp.bfloat16)
    arrived = []
    for e in range(2):
        block = lax.rem(hi + e, 2)
        piece = lax.dynamic_slice_in_dim(summed, block * rows, rows, 0)
        route = [(z * 2 + g, (2 * g + (z + e) % 2) * 2 + z // 2) for z in range(4) for g in range(2)]
        arrived.append(lax.ppermute(piece, ("hi", "head"), route))
    even = lax.rem(hi, 2) == 0
    return jnp.concatenate(
        [jnp.where(even, arrived[0], arrived[1]), jnp.where(even, arrived[1], arrived[0])], axis=1
    )


def solution(mesh):
    ctx = mesh.shape["ctx"]
    heads = mesh.shape["head"]

    def run(tokens, norm_gain, w_query, w_key, w_value, w_out, doc_starts):
        lines = w_key.shape[1] // HD // heads
        if (ctx, heads, lines) == (16, 2, 4):
            both = ("hi", "lo")
            grid = Mesh(mesh.devices.reshape(4, 4, 2), ("hi", "lo", "head"))
            body = line_device
        else:
            both, grid, body = "ctx", mesh, plain_device
        placed = (
            P(both, None),
            P(),
            P(both, "head"),
            P(both, "head"),
            P(both, "head"),
            P("head", both),
            P(),
        )
        return jax.shard_map(
            body, mesh=grid, in_specs=placed, out_specs=P(both, "head"), check_vma=False
        )(tokens, norm_gain, w_query, w_key, w_value, w_out, doc_starts)

    return run
```

```python
import functools

import jax
import jax.numpy as jnp
from jax import lax
from jax.experimental import pallas as pl
from jax.experimental.pallas import tpu as pltpu
from jax.sharding import Mesh
from jax.sharding import PartitionSpec as P

HD = 128
HALF = HD // 2
MIB = 1024 * 1024


def local_kernel(body, out_shape, operands, flops, scratch=(), exps=0):
    size = sum(x.size * x.dtype.itemsize for x in operands)
    return pl.pallas_call(
        body,
        in_specs=[pl.BlockSpec(memory_space=pltpu.SMEM)]
        + [pl.BlockSpec(memory_space=pltpu.VMEM)] * (len(operands) - 1),
        out_shape=out_shape,
        scratch_shapes=scratch,
        compiler_params=pltpu.CompilerParams(vmem_limit_bytes=12 * MIB),
        cost_estimate=pl.CostEstimate(flops=flops, bytes_accessed=size, transcendentals=exps),
    )(*operands)


def rotary_tables(positions):
    freqs = 500000.0 ** (-(jnp.arange(HALF, dtype=jnp.float32) * 2.0 / HD))
    angles = positions.astype(jnp.float32)[:, None] * freqs[None, :]
    cosine = jnp.cos(angles)
    sine = jnp.sin(angles)
    return (
        jnp.concatenate([cosine, cosine], axis=1),
        jnp.concatenate([-sine, sine], axis=1),
    )


def summed_lanes(refs, lanes):
    total = refs[0][:, lanes].astype(jnp.float32)
    for ref in refs[1:]:
        total = total + ref[:, lanes].astype(jnp.float32)
    return total


def rotated(values, cos_ref, sin_ref):
    return values * cos_ref[...] + pltpu.roll(values, HALF, 1) * sin_ref[...]


def pair_kernel(unused_ref, cos_ref, sin_ref, *refs):
    parts, out_ref = refs[:-1], refs[-1]
    key = rotated(summed_lanes(parts, pl.ds(0, HD)), cos_ref, sin_ref)
    out_ref[:, pl.ds(0, HD)] = key.astype(jnp.bfloat16)
    out_ref[:, pl.ds(HD, HD)] = summed_lanes(parts, pl.ds(HD, HD)).astype(jnp.bfloat16)


def finish_pair(cosine, sine, parts):
    operands = (jnp.zeros((1,), jnp.int32), cosine, sine, *parts)
    shape = jax.ShapeDtypeStruct(parts[0].shape, jnp.bfloat16)
    return local_kernel(pair_kernel, shape, operands, 8 * parts[0].size)


def attention_kernel(blocks, stride, n_query, n_kv, place_ref, cos_ref, sin_ref, *refs):
    query_refs = refs[:n_query]
    kv_refs = refs[n_query : n_query + n_kv]
    out_ref, turned, bias = refs[n_query + n_kv :]
    heads, tokens, _ = turned.shape
    for h in range(heads):
        total = summed_lanes(query_refs, pl.ds(h * HD, HD))
        turned[h] = rotated(total, cos_ref, sin_ref).astype(jnp.bfloat16)
    rows = tokens // blocks
    kv_rows = kv_refs[0].shape[0] // blocks
    documents = place_ref.shape[0] - 1 - n_kv
    scale = HD**-0.5
    for j in range(blocks):
        first = j * rows
        length = kv_rows * (j + 1)
        qpos = lax.broadcasted_iota(jnp.int32, (rows, HD), 0) + (place_ref[0] + j * stride)
        qstart = jnp.zeros_like(qpos)
        for i in range(documents):
            start = place_ref[1 + n_kv + i]
            qstart = jnp.where(qpos >= start, start, qstart)
        span = qpos - qstart
        for d in range(n_kv):
            for b in range(j + 1):
                for c in range(0, kv_rows, HD):
                    kpos = lax.broadcasted_iota(jnp.int32, (rows, HD), 1) + (
                        place_ref[1 + d] + (b * stride + c)
                    )
                    back = qpos - kpos
                    visible = (back >= 0) & (back <= span)
                    bias[:, pl.ds(d * length + b * kv_rows + c, HD)] = jnp.where(
                        visible, 0.0, -jnp.inf
                    )

        def one_head(h, unused):
            query = turned[h, pl.ds(first, rows), :]
            scores = []
            for d in range(n_kv):
                part = lax.dot_general(
                    query,
                    kv_refs[d][pl.ds(0, length), pl.ds(0, HD)],
                    (((1,), (1,)), ((), ())),
                    preferred_element_type=jnp.float32,
                )
                scores.append(part + bias[:, pl.ds(d * length, length)])
            highest = functools.reduce(
                jnp.maximum, [jnp.max(s, axis=1, keepdims=True) for s in scores]
            )
            denominator = 0.0
            mixed = 0.0
            for d in range(n_kv):
                probs = jnp.exp((scores[d] - highest) * scale)
                denominator = denominator + jnp.sum(probs, axis=1, keepdims=True)
                mixed = mixed + jnp.dot(
                    probs.astype(jnp.bfloat16),
                    kv_refs[d][pl.ds(0, length), pl.ds(HD, HD)],
                    preferred_element_type=jnp.float32,
                )
            lanes = pl.ds(pl.multiple_of(h * HD, HD), HD)
            out_ref[pl.ds(first, rows), lanes] = (mixed / denominator).astype(jnp.bfloat16)
            return unused

        lax.fori_loop(0, heads, one_head, 0)


def attention(place, cosine, sine, query_parts, kv_parts, blocks, stride):
    tokens, width = query_parts[0].shape
    heads = width // HD
    keys = sum(part.shape[0] for part in kv_parts)
    return local_kernel(
        functools.partial(attention_kernel, blocks, stride, len(query_parts), len(kv_parts)),
        jax.ShapeDtypeStruct((tokens, width), jnp.bfloat16),
        (place, cosine, sine, *query_parts, *kv_parts),
        32 * tokens * width * keys,
        [
            pltpu.VMEM((heads, tokens, HD), jnp.bfloat16),
            pltpu.VMEM((tokens // blocks, keys), jnp.float32),
        ],
        tokens * heads * keys,
    )


def product_kernel(place_ref, *refs):
    own_ref, half_refs = refs[0], refs[1:3]
    weight_refs, out_refs, gathered = refs[3:8], refs[8:10], refs[10]
    hi = place_ref[0]
    lo = place_ref[1]
    rows, depth = own_ref.shape
    share = weight_refs[3].shape[0]
    gathered[pl.ds(pl.multiple_of(hi * rows, rows), rows), :] = own_ref[...]
    for side, half_ref in enumerate(half_refs):
        first = lax.rem(place_ref[2] + side, 2) * (depth // 2)
        features = pl.ds(pl.multiple_of(first, depth // 2), depth // 2)
        for d in range(1, 4):
            gathered[pl.ds(pl.multiple_of((hi ^ d) * rows, rows), rows), features] = half_ref[
                pl.ds((d - 1) * rows, rows), :
            ]
    for side, out_ref in enumerate(out_refs):
        width = out_ref.shape[1]
        first = (lax.div(hi, 2) ^ side) * place_ref[3] + place_ref[4]
        columns = pl.ds(pl.multiple_of(first, width), width)
        total = 0.0
        for part in range(2):
            for r in range(4):
                if r < 3:
                    weight = weight_refs[r][pl.ds(part * share, share), columns]
                else:
                    weight = weight_refs[3 + part][:, columns]
                block = (lax.rem(hi, 2) ^ part) * 4 + (lo ^ r)
                total = total + jnp.dot(
                    gathered[:, pl.ds(pl.multiple_of(block * share, share), share)],
                    weight,
                    preferred_element_type=jnp.float32,
                )
        out_ref[...] = total.astype(jnp.bfloat16)


def product(index, token_parts, weights, chunk, chunks):
    rows, depth = token_parts[0].shape
    step = weights[0].shape[1] // 2
    width = step // chunks
    place = jnp.concatenate([index, jnp.array([step, chunk * width], jnp.int32)])
    shape = jax.ShapeDtypeStruct((4 * rows, width), jnp.bfloat16)
    return local_kernel(
        product_kernel,
        (shape,) * 2,
        (place, *token_parts, *weights),
        2 * 4 * rows * depth * 2 * width,
        [pltpu.VMEM((4 * rows, depth), jnp.bfloat16)],
    )


def project_kernel(place_ref, *refs):
    attended_refs = refs[:4]
    weight_refs = refs[4:8]
    total_refs = refs[8:-2]
    hi = place_ref[0]
    lo = place_ref[1]
    core = place_ref[2]
    offset = place_ref[3]
    depth = attended_refs[0].shape[1]
    width = weight_refs[0].shape[1]
    span = weight_refs[0].shape[0] // 4
    for side, out_ref in enumerate(refs[-2:]):
        kept = out_ref.shape[0]
        rows = pl.ds(pl.multiple_of(lax.rem(core + side, 2) * kept, kept), kept)
        for r, weight_ref in enumerate(weight_refs):
            columns = pl.ds(pl.multiple_of((lo ^ r) * width, width), width)
            total = total_refs[side][:, columns] if total_refs else 0.0
            for k, attended_ref in enumerate(attended_refs):
                first = lax.rem(hi - k + 4, 4) * span + offset
                total = total + jnp.dot(
                    attended_ref[rows, :],
                    weight_ref[pl.ds(pl.multiple_of(first, depth), depth), :],
                    preferred_element_type=jnp.float32,
                )
            out_ref[:, columns] = total.astype(out_ref.dtype)


def project(place, attended_parts, weights, totals, kind):
    tokens, depth = attended_parts[0].shape
    width = weights[0].shape[1]
    shape = jax.ShapeDtypeStruct((tokens // 2, 4 * width), kind)
    return local_kernel(
        project_kernel,
        (shape, shape),
        (place, *attended_parts, *weights, *totals),
        2 * tokens * 4 * depth * 4 * width,
    )


def normalised(tokens, norm_gain):
    source = tokens.astype(jnp.float32)
    return (
        source * lax.rsqrt(jnp.mean(source * source, axis=1, keepdims=True) + 1e-05) * norm_gain
    ).astype(jnp.bfloat16)


def plain_device(tokens, norm_gain, w_query, w_key, w_value, w_out, doc_starts):
    rows = tokens.shape[0]
    first = lax.axis_index("ctx") * rows
    normed = normalised(tokens, norm_gain)

    def project_with(weight):
        gathered = lax.all_gather(weight, "ctx", axis=0, tiled=True)
        total = jnp.dot(normed, gathered, preferred_element_type=jnp.float32)
        return total.astype(jnp.bfloat16)

    cosine, sine = rotary_tables(first + jnp.arange(rows, dtype=jnp.int32))
    place = jnp.concatenate([jnp.stack([first, jnp.zeros_like(first)]), doc_starts])
    query = project_with(w_query)
    key = project_with(w_key)
    value = project_with(w_value)
    kv_local = w_key.shape[1] // HD
    group = w_query.shape[1] // kv_local
    mixed = []
    for h in range(kv_local):
        lanes = slice(h * HD, (h + 1) * HD)
        pair = jnp.concatenate([key[:, lanes], value[:, lanes]], axis=1)
        pair = lax.all_gather(finish_pair(cosine, sine, [pair]), "ctx", axis=0, tiled=True)
        part = query[:, h * group : (h + 1) * group]
        mixed.append(attention(place, cosine, sine, [part], [pair], 1, 0))
    attended = jnp.concatenate(mixed, axis=1)
    wide = lax.all_gather(w_out, "ctx", axis=1, tiled=True)
    partial_out = jnp.dot(attended, wide, preferred_element_type=jnp.float32)
    return lax.psum_scatter(
        partial_out.astype(jnp.bfloat16), "head", scatter_dimension=1, tiled=True
    )


def after(value, *earlier):
    return lax.optimization_barrier((value, *earlier))[0]


def beside(block, r):
    return lax.ppermute(block, "lo", [(i, i ^ r) for i in range(4)])


def sides(block):
    return [block, beside(block, 1), beside(block, 2)]


def corner(blocks):
    half = blocks[0].shape[0] // 2
    return [*blocks, beside(blocks[2][:half], 1), beside(blocks[1][half:], 2)]


def along(block, d):
    return lax.ppermute(block, "hi", [(i, i ^ d) for i in range(4)])


def round_line(block):
    return [block] + [
        lax.ppermute(block, "hi", [(i, (i + d) % 4) for i in range(4)]) for d in range(1, 4)
    ]


def line_device(tokens, norm_gain, w_query, w_key, w_value, w_out, doc_starts):
    rows, features = tokens.shape
    hi = lax.axis_index("hi")
    lo = lax.axis_index("lo")
    core = lax.axis_index("head")
    which_half = lax.div(hi, 2)
    which = lax.rem(hi, 2)
    depth = features // 2
    heads = w_query.shape[1] // 4
    width = heads // 2

    def columns_for(chip, sources, width):
        return jnp.concatenate(
            [
                lax.dynamic_slice_in_dim(w, (2 * z + chip) * width, width, 1)
                for z in range(2)
                for w in sources
            ],
            axis=1,
        )

    stage = ()
    weights = []
    for sources, size in (((w_key, w_value), HD), ((w_query,), heads)):
        came = along(columns_for(1 - which, sources, size), 1)
        both = jnp.concatenate([columns_for(which, sources, size), came], axis=0)
        weights.append(corner(sides(after(both, *stage) if stage else both)))
        stage = weights[-1][3:]

    normed = normalised(tokens, norm_gain)
    own = lax.dynamic_slice_in_dim(normed, which_half * depth, depth, 1)

    def core_half(z):
        return lax.dynamic_slice_in_dim(normed, z * depth + core * (depth // 2), depth // 2, 1)

    near = along(core_half(which_half), 1)
    other = along(core_half(1 - which_half), 2)
    halves = jnp.concatenate([near, other, along(after(other, near), 1)], axis=0)
    token_parts = [own, halves, lax.ppermute(halves, "head", [(0, 1), (1, 0)])]
    index = jnp.stack([hi, lo, core])

    row_index = jnp.arange(4 * rows, dtype=jnp.int32)
    cosine, sine = rotary_tables((row_index // rows * 4 + lo) * rows + row_index % rows)

    kept, sent = product(index, token_parts, weights[0], 0, 1)
    kv_own = finish_pair(cosine, sine, [kept, along(sent, 2)])
    kv_parts = [kv_own] + [beside(kv_own, r) for r in range(1, 4)]

    firsts = jnp.stack([lo, lo, lo ^ 1, lo ^ 2, lo ^ 3]) * rows
    seen = jnp.concatenate([firsts, doc_starts])
    out_sides = sides(after(w_out, *weights[1][3:], *kv_parts[1:]))
    products = [product(index, token_parts, weights[1], c, 2) for c in range(2)]
    products[0] = (after(products[0][0], products[1][0]), products[0][1])
    attended = [
        attention(seen, cosine, sine, [kept, along(sent, 2)], kv_parts, 4, 4 * rows)
        for kept, sent in products
    ]
    out_sides[1:] = lax.optimization_barrier((*out_sides[1:], attended[1]))[:2]
    out_blocks = corner(out_sides)
    out_blocks[3:] = [jnp.concatenate(out_blocks[3:], axis=0)]
    totals = ()
    for c, kind in enumerate((jnp.float32, jnp.bfloat16)):
        where = jnp.concatenate([index, jnp.full((1,), c * width, jnp.int32)])
        totals = project(where, round_line(attended[c]), out_blocks, totals, kind)

    mine, theirs = totals
    theirs = lax.ppermute(theirs, "head", [(0, 1), (1, 0)])
    summed = (mine.astype(jnp.float32) + theirs.astype(jnp.float32)).astype(jnp.bfloat16)
    arrived = []
    for e in range(2):
        block = lax.rem(hi + e, 2)
        piece = lax.dynamic_slice_in_dim(summed, block * rows, rows, 0)
        route = [(z * 2 + g, (2 * g + (z + e) % 2) * 2 + z // 2) for z in range(4) for g in range(2)]
        arrived.append(lax.ppermute(piece, ("hi", "head"), route))
    even = lax.rem(hi, 2) == 0
    return jnp.concatenate(
        [jnp.where(even, arrived[0], arrived[1]), jnp.where(even, arrived[1], arrived[0])], axis=1
    )


def solution(mesh):
    ctx = mesh.shape["ctx"]
    heads = mesh.shape["head"]

    def run(tokens, norm_gain, w_query, w_key, w_value, w_out, doc_starts):
        lines = w_key.shape[1] // HD // heads
        if (ctx, heads, lines) == (16, 2, 4):
            both = ("hi", "lo")
            grid = Mesh(mesh.devices.reshape(4, 4, 2), ("hi", "lo", "head"))
            body = line_device
        else:
            both, grid, body = "ctx", mesh, plain_device
        placed = (
            P(both, None),
            P(),
            P(both, "head"),
            P(both, "head"),
            P(both, "head"),
            P("head", both),
            P(),
        )
        return jax.shard_map(
            body, mesh=grid, in_specs=placed, out_specs=P(both, "head"), check_vma=False
        )(tokens, norm_gain, w_query, w_key, w_value, w_out, doc_starts)

    return run
```

```python
import functools

import jax
import jax.numpy as jnp
from jax import lax
from jax.experimental import pallas as pl
from jax.experimental.pallas import tpu as pltpu
from jax.sharding import Mesh
from jax.sharding import PartitionSpec as P

HD = 128
HALF = HD // 2
MIB = 1024 * 1024


def local_kernel(body, out_shape, operands, flops, scratch=(), exps=0):
    size = sum(x.size * x.dtype.itemsize for x in operands)
    return pl.pallas_call(
        body,
        in_specs=[pl.BlockSpec(memory_space=pltpu.SMEM)]
        + [pl.BlockSpec(memory_space=pltpu.VMEM)] * (len(operands) - 1),
        out_shape=out_shape,
        scratch_shapes=scratch,
        compiler_params=pltpu.CompilerParams(vmem_limit_bytes=12 * MIB),
        cost_estimate=pl.CostEstimate(flops=flops, bytes_accessed=size, transcendentals=exps),
    )(*operands)


def rotary_tables(positions):
    freqs = 500000.0 ** (-(jnp.arange(HALF, dtype=jnp.float32) * 2.0 / HD))
    angles = positions.astype(jnp.float32)[:, None] * freqs[None, :]
    cosine = jnp.cos(angles)
    sine = jnp.sin(angles)
    return (
        jnp.concatenate([cosine, cosine], axis=1),
        jnp.concatenate([-sine, sine], axis=1),
    )


def summed_lanes(refs, lanes):
    total = refs[0][:, lanes].astype(jnp.float32)
    for ref in refs[1:]:
        total = total + ref[:, lanes].astype(jnp.float32)
    return total


def rotated(values, cos_ref, sin_ref):
    return values * cos_ref[...] + pltpu.roll(values, HALF, 1) * sin_ref[...]


def pair_kernel(unused_ref, cos_ref, sin_ref, *refs):
    parts, out_ref = refs[:-1], refs[-1]
    key = rotated(summed_lanes(parts, pl.ds(0, HD)), cos_ref, sin_ref)
    out_ref[:, pl.ds(0, HD)] = key.astype(jnp.bfloat16)
    out_ref[:, pl.ds(HD, HD)] = summed_lanes(parts, pl.ds(HD, HD)).astype(jnp.bfloat16)


def finish_pair(cosine, sine, parts):
    operands = (jnp.zeros((1,), jnp.int32), cosine, sine, *parts)
    shape = jax.ShapeDtypeStruct(parts[0].shape, jnp.bfloat16)
    return local_kernel(pair_kernel, shape, operands, 8 * parts[0].size)


def attention_kernel(blocks, stride, n_query, n_kv, place_ref, cos_ref, sin_ref, *refs):
    query_refs = refs[:n_query]
    kv_refs = refs[n_query : n_query + n_kv]
    out_ref, turned, bias = refs[n_query + n_kv :]
    heads, tokens, _ = turned.shape
    for h in range(heads):
        total = summed_lanes(query_refs, pl.ds(h * HD, HD))
        turned[h] = rotated(total, cos_ref, sin_ref).astype(jnp.bfloat16)
    rows = tokens // blocks
    kv_rows = kv_refs[0].shape[0] // blocks
    documents = place_ref.shape[0] - 1 - n_kv
    scale = HD**-0.5
    for j in range(blocks):
        first = j * rows
        length = kv_rows * (j + 1)
        qpos = lax.broadcasted_iota(jnp.int32, (rows, HD), 0) + (place_ref[0] + j * stride)
        qstart = jnp.zeros_like(qpos)
        for i in range(documents):
            start = place_ref[1 + n_kv + i]
            qstart = jnp.where(qpos >= start, start, qstart)
        span = qpos - qstart
        for d in range(n_kv):
            for b in range(j + 1):
                for c in range(0, kv_rows, HD):
                    kpos = lax.broadcasted_iota(jnp.int32, (rows, HD), 1) + (
                        place_ref[1 + d] + (b * stride + c)
                    )
                    back = qpos - kpos
                    visible = (back >= 0) & (back <= span)
                    bias[:, pl.ds(d * length + b * kv_rows + c, HD)] = jnp.where(
                        visible, 0.0, -jnp.inf
                    )

        def one_head(h, unused):
            query = turned[h, pl.ds(first, rows), :]
            scores = []
            for d in range(n_kv):
                part = lax.dot_general(
                    query,
                    kv_refs[d][pl.ds(0, length), pl.ds(0, HD)],
                    (((1,), (1,)), ((), ())),
                    preferred_element_type=jnp.float32,
                )
                scores.append(part + bias[:, pl.ds(d * length, length)])
            highest = functools.reduce(
                jnp.maximum, [jnp.max(s, axis=1, keepdims=True) for s in scores]
            )
            denominator = 0.0
            mixed = 0.0
            for d in range(n_kv):
                probs = jnp.exp((scores[d] - highest) * scale)
                denominator = denominator + jnp.sum(probs, axis=1, keepdims=True)
                mixed = mixed + jnp.dot(
                    probs.astype(jnp.bfloat16),
                    kv_refs[d][pl.ds(0, length), pl.ds(HD, HD)],
                    preferred_element_type=jnp.float32,
                )
            lanes = pl.ds(pl.multiple_of(h * HD, HD), HD)
            out_ref[pl.ds(first, rows), lanes] = (mixed / denominator).astype(jnp.bfloat16)
            return unused

        lax.fori_loop(0, heads, one_head, 0)


def attention(place, cosine, sine, query_parts, kv_parts, blocks, stride):
    tokens, width = query_parts[0].shape
    heads = width // HD
    keys = sum(part.shape[0] for part in kv_parts)
    return local_kernel(
        functools.partial(attention_kernel, blocks, stride, len(query_parts), len(kv_parts)),
        jax.ShapeDtypeStruct((tokens, width), jnp.bfloat16),
        (place, cosine, sine, *query_parts, *kv_parts),
        32 * tokens * width * keys,
        [
            pltpu.VMEM((heads, tokens, HD), jnp.bfloat16),
            pltpu.VMEM((tokens // blocks, keys), jnp.float32),
        ],
        tokens * heads * keys,
    )


def product_kernel(place_ref, *refs):
    own_ref, half_refs = refs[0], refs[1:3]
    weight_refs, out_refs, gathered = refs[3:8], refs[8:10], refs[10]
    hi = place_ref[0]
    lo = place_ref[1]
    rows, depth = own_ref.shape
    share = weight_refs[3].shape[0]
    gathered[pl.ds(pl.multiple_of(hi * rows, rows), rows), :] = own_ref[...]
    for side, half_ref in enumerate(half_refs):
        first = lax.rem(place_ref[2] + side, 2) * (depth // 2)
        features = pl.ds(pl.multiple_of(first, depth // 2), depth // 2)
        for d in range(1, 4):
            gathered[pl.ds(pl.multiple_of((hi ^ d) * rows, rows), rows), features] = half_ref[
                pl.ds((d - 1) * rows, rows), :
            ]
    for side, out_ref in enumerate(out_refs):
        width = out_ref.shape[1]
        first = (lax.div(hi, 2) ^ side) * place_ref[3] + place_ref[4]
        columns = pl.ds(pl.multiple_of(first, width), width)
        total = 0.0
        for part in range(2):
            for r in range(4):
                if r < 3:
                    weight = weight_refs[r][pl.ds(part * share, share), columns]
                else:
                    weight = weight_refs[3 + part][:, columns]
                block = (lax.rem(hi, 2) ^ part) * 4 + (lo ^ r)
                total = total + jnp.dot(
                    gathered[:, pl.ds(pl.multiple_of(block * share, share), share)],
                    weight,
                    preferred_element_type=jnp.float32,
                )
        out_ref[...] = total.astype(jnp.bfloat16)


def product(index, token_parts, weights, chunk, chunks):
    rows, depth = token_parts[0].shape
    step = weights[0].shape[1] // 2
    width = step // chunks
    place = jnp.concatenate([index, jnp.array([step, chunk * width], jnp.int32)])
    shape = jax.ShapeDtypeStruct((4 * rows, width), jnp.bfloat16)
    return local_kernel(
        product_kernel,
        (shape,) * 2,
        (place, *token_parts, *weights),
        2 * 4 * rows * depth * 2 * width,
        [pltpu.VMEM((4 * rows, depth), jnp.bfloat16)],
    )


def project_kernel(place_ref, *refs):
    attended_refs, weight_refs, out_ref = refs[:4], refs[4:8], refs[8]
    hi = place_ref[0]
    lo = place_ref[1]
    side = lax.div(hi, 2) ^ place_ref[2]
    depth = attended_refs[0].shape[1]
    features, width = weight_refs[0].shape
    span = features // 4
    for r, weight_ref in enumerate(weight_refs):
        total = 0.0
        for k, attended_ref in enumerate(attended_refs):
            first = side * (2 * span) + (lax.rem(hi, 2) ^ (k // 2)) * span + (k % 2) * depth
            total = total + jnp.dot(
                attended_ref[...],
                weight_ref[pl.ds(pl.multiple_of(first, depth), depth), :],
                preferred_element_type=jnp.float32,
            )
        columns = pl.ds(pl.multiple_of((lo ^ r) * width, width), width)
        out_ref[:, columns] = total.astype(out_ref.dtype)


def project(place, attended_parts, weights):
    tokens, depth = attended_parts[0].shape
    width = weights[0].shape[1]
    return local_kernel(
        project_kernel,
        jax.ShapeDtypeStruct((tokens, 4 * width), jnp.bfloat16),
        (place, *attended_parts, *weights),
        2 * tokens * 4 * depth * 4 * width,
    )


def normalised(tokens, norm_gain):
    source = tokens.astype(jnp.float32)
    return (
        source * lax.rsqrt(jnp.mean(source * source, axis=1, keepdims=True) + 1e-05) * norm_gain
    ).astype(jnp.bfloat16)


def plain_device(tokens, norm_gain, w_query, w_key, w_value, w_out, doc_starts):
    rows = tokens.shape[0]
    first = lax.axis_index("ctx") * rows
    normed = normalised(tokens, norm_gain)

    def project_with(weight):
        gathered = lax.all_gather(weight, "ctx", axis=0, tiled=True)
        total = jnp.dot(normed, gathered, preferred_element_type=jnp.float32)
        return total.astype(jnp.bfloat16)

    cosine, sine = rotary_tables(first + jnp.arange(rows, dtype=jnp.int32))
    place = jnp.concatenate([jnp.stack([first, jnp.zeros_like(first)]), doc_starts])
    query = project_with(w_query)
    key = project_with(w_key)
    value = project_with(w_value)
    kv_local = w_key.shape[1] // HD
    group = w_query.shape[1] // kv_local
    mixed = []
    for h in range(kv_local):
        lanes = slice(h * HD, (h + 1) * HD)
        pair = jnp.concatenate([key[:, lanes], value[:, lanes]], axis=1)
        pair = lax.all_gather(finish_pair(cosine, sine, [pair]), "ctx", axis=0, tiled=True)
        part = query[:, h * group : (h + 1) * group]
        mixed.append(attention(place, cosine, sine, [part], [pair], 1, 0))
    attended = jnp.concatenate(mixed, axis=1)
    wide = lax.all_gather(w_out, "ctx", axis=1, tiled=True)
    partial_out = jnp.dot(attended, wide, preferred_element_type=jnp.float32)
    return lax.psum_scatter(
        partial_out.astype(jnp.bfloat16), "head", scatter_dimension=1, tiled=True
    )


def after(value, *earlier):
    return lax.optimization_barrier((value, *earlier))[0]


def beside(block, r):
    return lax.ppermute(block, "lo", [(i, i ^ r) for i in range(4)])


def sides(block):
    return [block, beside(block, 1), beside(block, 2)]


def corner(blocks):
    half = blocks[0].shape[0] // 2
    return [*blocks, beside(blocks[2][:half], 1), beside(blocks[1][half:], 2)]


def along(block, d):
    return lax.ppermute(block, "hi", [(i, i ^ d) for i in range(4)])


def line_device(tokens, norm_gain, w_query, w_key, w_value, w_out, doc_starts):
    rows, features = tokens.shape
    hi = lax.axis_index("hi")
    lo = lax.axis_index("lo")
    core = lax.axis_index("head")
    which_half = lax.div(hi, 2)
    which = lax.rem(hi, 2)
    depth = features // 2
    heads = w_query.shape[1] // 4
    width = heads // 2

    def columns_for(chip, sources, width):
        return jnp.concatenate(
            [
                lax.dynamic_slice_in_dim(w, (2 * z + chip) * width, width, 1)
                for z in range(2)
                for w in sources
            ],
            axis=1,
        )

    stage = ()
    weights = []
    for sources, size in (((w_key, w_value), HD), ((w_query,), heads)):
        came = along(columns_for(1 - which, sources, size), 1)
        both = jnp.concatenate([columns_for(which, sources, size), came], axis=0)
        weights.append(corner(sides(after(both, *stage) if stage else both)))
        stage = weights[-1][3:]

    normed = normalised(tokens, norm_gain)
    own = lax.dynamic_slice_in_dim(normed, which_half * depth, depth, 1)

    def core_half(z):
        return lax.dynamic_slice_in_dim(normed, z * depth + core * (depth // 2), depth // 2, 1)

    near = along(core_half(which_half), 1)
    other = along(core_half(1 - which_half), 2)
    halves = jnp.concatenate([near, other, along(after(other, near), 1)], axis=0)
    token_parts = [own, halves, lax.ppermute(halves, "head", [(0, 1), (1, 0)])]
    index = jnp.stack([hi, lo, core])

    row_index = jnp.arange(4 * rows, dtype=jnp.int32)
    cosine, sine = rotary_tables((row_index // rows * 4 + lo) * rows + row_index % rows)

    kept, sent = product(index, token_parts, weights[0], 0, 1)
    features_here = w_out.shape[0] // 2
    out_own = lax.dynamic_slice_in_dim(w_out, which_half * features_here, features_here, 0)
    out_other = lax.dynamic_slice_in_dim(w_out, (1 - which_half) * features_here, features_here, 0)
    out_other = along(after(out_other, halves), 2)
    kv_own = finish_pair(cosine, sine, [after(kept, out_other), along(sent, 2)])
    kv_going = after(kv_own, *weights[1][3:])
    kv_parts = [kv_own] + [beside(kv_going, r) for r in range(1, 4)]

    firsts = jnp.stack([lo, lo, lo ^ 1, lo ^ 2, lo ^ 3]) * rows
    seen = jnp.concatenate([firsts, doc_starts])
    out_sides = sides(after(jnp.concatenate([out_own, out_other], axis=0), *kv_parts[1:]))
    products = [product(index, token_parts, weights[1], c, 2) for c in range(2)]
    products[0] = (after(products[0][0], products[1][0]), products[0][1])
    attended = [
        attention(seen, cosine, sine, [kept, along(sent, 2)], kv_parts, 4, 4 * rows)
        for kept, sent in products
    ]
    out_sides[1:] = lax.optimization_barrier((*out_sides[1:], attended[1]))[:2]
    out_blocks = corner(out_sides)
    out_blocks[3:] = [jnp.concatenate(out_blocks[3:], axis=0)]
    attended += [along(chunk, 1) for chunk in attended]

    theirs, mine = [
        project(jnp.stack([hi, lo, group]), attended, out_blocks) for group in (1 - core, core)
    ]
    theirs = lax.ppermute(theirs, "head", [(0, 1), (1, 0)])

    def added(one, two):
        return (one.astype(jnp.float32) + two.astype(jnp.float32)).astype(jnp.bfloat16)

    kept = 2 * rows
    shares = [
        added(
            lax.dynamic_slice_in_dim(mine, z * kept, kept, 0),
            lax.dynamic_slice_in_dim(theirs, z * kept, kept, 0),
        )
        for z in (which_half, 1 - which_half)
    ]
    summed = added(shares[0], along(shares[1], 2))
    here = lax.dynamic_slice_in_dim(summed, which * rows, rows, 0)
    there = along(lax.dynamic_slice_in_dim(summed, (1 - which) * rows, rows, 0), 1)
    first = which == 0
    return jnp.concatenate(
        [jnp.where(first, here, there), jnp.where(first, there, here)], axis=1
    )


def solution(mesh):
    ctx = mesh.shape["ctx"]
    heads = mesh.shape["head"]

    def run(tokens, norm_gain, w_query, w_key, w_value, w_out, doc_starts):
        lines = w_key.shape[1] // HD // heads
        if (ctx, heads, lines) == (16, 2, 4):
            both = ("hi", "lo")
            grid = Mesh(mesh.devices.reshape(4, 4, 2), ("hi", "lo", "head"))
            body = line_device
        else:
            both, grid, body = "ctx", mesh, plain_device
        placed = (
            P(both, None),
            P(),
            P(both, "head"),
            P(both, "head"),
            P(both, "head"),
            P("head", both),
            P(),
        )
        return jax.shard_map(
            body, mesh=grid, in_specs=placed, out_specs=P(both, "head"), check_vma=False
        )(tokens, norm_gain, w_query, w_key, w_value, w_out, doc_starts)

    return run
```

```python
import functools

import jax
import jax.numpy as jnp
from jax import lax
from jax.experimental import pallas as pl
from jax.experimental.pallas import tpu as pltpu
from jax.sharding import Mesh
from jax.sharding import PartitionSpec as P

HD = 128
HALF = HD // 2
MIB = 1024 * 1024


def local_kernel(body, out_shape, operands, flops, scratch=(), exps=0):
    size = sum(x.size * x.dtype.itemsize for x in operands)
    return pl.pallas_call(
        body,
        in_specs=[pl.BlockSpec(memory_space=pltpu.SMEM)]
        + [pl.BlockSpec(memory_space=pltpu.VMEM)] * (len(operands) - 1),
        out_shape=out_shape,
        scratch_shapes=scratch,
        compiler_params=pltpu.CompilerParams(vmem_limit_bytes=12 * MIB),
        cost_estimate=pl.CostEstimate(flops=flops, bytes_accessed=size, transcendentals=exps),
    )(*operands)


def rotary_tables(positions):
    freqs = 500000.0 ** (-(jnp.arange(HALF, dtype=jnp.float32) * 2.0 / HD))
    angles = positions.astype(jnp.float32)[:, None] * freqs[None, :]
    cosine = jnp.cos(angles)
    sine = jnp.sin(angles)
    return (
        jnp.concatenate([cosine, cosine], axis=1),
        jnp.concatenate([-sine, sine], axis=1),
    )


def summed_lanes(refs, lanes):
    total = refs[0][:, lanes].astype(jnp.float32)
    for ref in refs[1:]:
        total = total + ref[:, lanes].astype(jnp.float32)
    return total


def rotated(values, cos_ref, sin_ref):
    return values * cos_ref[...] + pltpu.roll(values, HALF, 1) * sin_ref[...]


def pair_kernel(unused_ref, cos_ref, sin_ref, *refs):
    parts, out_ref = refs[:-1], refs[-1]
    key = rotated(summed_lanes(parts, pl.ds(0, HD)), cos_ref, sin_ref)
    out_ref[:, pl.ds(0, HD)] = key.astype(jnp.bfloat16)
    out_ref[:, pl.ds(HD, HD)] = summed_lanes(parts, pl.ds(HD, HD)).astype(jnp.bfloat16)


def finish_pair(cosine, sine, parts):
    operands = (jnp.zeros((1,), jnp.int32), cosine, sine, *parts)
    shape = jax.ShapeDtypeStruct(parts[0].shape, jnp.bfloat16)
    return local_kernel(pair_kernel, shape, operands, 8 * parts[0].size)


def attention_kernel(blocks, stride, n_query, n_kv, place_ref, cos_ref, sin_ref, *refs):
    query_refs = refs[:n_query]
    kv_refs = refs[n_query : n_query + n_kv]
    out_ref, turned, bias = refs[n_query + n_kv :]
    heads, tokens, _ = turned.shape
    for h in range(heads):
        total = summed_lanes(query_refs, pl.ds(h * HD, HD))
        turned[h] = rotated(total, cos_ref, sin_ref).astype(jnp.bfloat16)
    rows = tokens // blocks
    kv_rows = kv_refs[0].shape[0] // blocks
    documents = place_ref.shape[0] - 1 - n_kv
    scale = HD**-0.5
    for j in range(blocks):
        first = j * rows
        length = kv_rows * (j + 1)
        qpos = lax.broadcasted_iota(jnp.int32, (rows, HD), 0) + (place_ref[0] + j * stride)
        qstart = jnp.zeros_like(qpos)
        for i in range(documents):
            start = place_ref[1 + n_kv + i]
            qstart = jnp.where(qpos >= start, start, qstart)
        span = qpos - qstart
        for d in range(n_kv):
            for b in range(j + 1):
                for c in range(0, kv_rows, HD):
                    kpos = lax.broadcasted_iota(jnp.int32, (rows, HD), 1) + (
                        place_ref[1 + d] + (b * stride + c)
                    )
                    back = qpos - kpos
                    visible = (back >= 0) & (back <= span)
                    bias[:, pl.ds(d * length + b * kv_rows + c, HD)] = jnp.where(
                        visible, 0.0, -jnp.inf
                    )

        def one_head(h, unused):
            query = turned[h, pl.ds(first, rows), :]
            scores = []
            for d in range(n_kv):
                part = lax.dot_general(
                    query,
                    kv_refs[d][pl.ds(0, length), pl.ds(0, HD)],
                    (((1,), (1,)), ((), ())),
                    preferred_element_type=jnp.float32,
                )
                scores.append(part + bias[:, pl.ds(d * length, length)])
            highest = functools.reduce(
                jnp.maximum, [jnp.max(s, axis=1, keepdims=True) for s in scores]
            )
            denominator = 0.0
            mixed = 0.0
            for d in range(n_kv):
                probs = jnp.exp((scores[d] - highest) * scale)
                denominator = denominator + jnp.sum(probs, axis=1, keepdims=True)
                mixed = mixed + jnp.dot(
                    probs.astype(jnp.bfloat16),
                    kv_refs[d][pl.ds(0, length), pl.ds(HD, HD)],
                    preferred_element_type=jnp.float32,
                )
            lanes = pl.ds(pl.multiple_of(h * HD, HD), HD)
            out_ref[pl.ds(first, rows), lanes] = (mixed / denominator).astype(jnp.bfloat16)
            return unused

        lax.fori_loop(0, heads, one_head, 0)


def attention(place, cosine, sine, query_parts, kv_parts, blocks, stride):
    tokens, width = query_parts[0].shape
    heads = width // HD
    keys = sum(part.shape[0] for part in kv_parts)
    return local_kernel(
        functools.partial(attention_kernel, blocks, stride, len(query_parts), len(kv_parts)),
        jax.ShapeDtypeStruct((tokens, width), jnp.bfloat16),
        (place, cosine, sine, *query_parts, *kv_parts),
        32 * tokens * width * keys,
        [
            pltpu.VMEM((heads, tokens, HD), jnp.bfloat16),
            pltpu.VMEM((tokens // blocks, keys), jnp.float32),
        ],
        tokens * heads * keys,
    )


def product_kernel(place_ref, *refs):
    own_ref, half_refs = refs[0], refs[1:3]
    weight_refs, out_refs, gathered = refs[3:8], refs[8:10], refs[10]
    hi = place_ref[0]
    lo = place_ref[1]
    rows, depth = own_ref.shape
    share = weight_refs[3].shape[0]
    gathered[pl.ds(pl.multiple_of(hi * rows, rows), rows), :] = own_ref[...]
    for side, half_ref in enumerate(half_refs):
        first = lax.rem(place_ref[2] + side, 2) * (depth // 2)
        features = pl.ds(pl.multiple_of(first, depth // 2), depth // 2)
        for d in range(1, 4):
            gathered[pl.ds(pl.multiple_of((hi ^ d) * rows, rows), rows), features] = half_ref[
                pl.ds((d - 1) * rows, rows), :
            ]
    for side, out_ref in enumerate(out_refs):
        width = out_ref.shape[1]
        first = (lax.div(hi, 2) ^ side) * place_ref[3] + place_ref[4]
        columns = pl.ds(pl.multiple_of(first, width), width)
        total = 0.0
        for part in range(2):
            for r in range(4):
                if r < 3:
                    weight = weight_refs[r][pl.ds(part * share, share), columns]
                else:
                    weight = weight_refs[3 + part][:, columns]
                block = (lax.rem(hi, 2) ^ part) * 4 + (lo ^ r)
                total = total + jnp.dot(
                    gathered[:, pl.ds(pl.multiple_of(block * share, share), share)],
                    weight,
                    preferred_element_type=jnp.float32,
                )
        out_ref[...] = total.astype(jnp.bfloat16)


def product(index, token_parts, weights, chunk, chunks):
    rows, depth = token_parts[0].shape
    step = weights[0].shape[1] // 2
    width = step // chunks
    place = jnp.concatenate([index, jnp.array([step, chunk * width], jnp.int32)])
    shape = jax.ShapeDtypeStruct((4 * rows, width), jnp.bfloat16)
    return local_kernel(
        product_kernel,
        (shape,) * 2,
        (place, *token_parts, *weights),
        2 * 4 * rows * depth * 2 * width,
        [pltpu.VMEM((4 * rows, depth), jnp.bfloat16)],
    )


def project_kernel(place_ref, *refs):
    attended_refs, weight_refs, out_ref = refs[:4], refs[4:-1], refs[-1]
    hi = place_ref[0]
    side = lax.div(hi, 2) ^ place_ref[1]
    depth = attended_refs[0].shape[1]
    features, width = weight_refs[0].shape
    span = features // 4
    for r, weight_ref in enumerate(weight_refs):
        total = 0.0
        for k, attended_ref in enumerate(attended_refs):
            first = side * (2 * span) + (lax.rem(hi, 2) ^ (k // 2)) * span + (k % 2) * depth
            total = total + jnp.dot(
                attended_ref[...],
                weight_ref[pl.ds(pl.multiple_of(first, depth), depth), :],
                preferred_element_type=jnp.float32,
            )
        out_ref[:, pl.ds(r * width, width)] = total.astype(out_ref.dtype)


def project(place, attended_parts, weights):
    tokens, depth = attended_parts[0].shape
    width = weights[0].shape[1]
    return local_kernel(
        project_kernel,
        jax.ShapeDtypeStruct((tokens, len(weights) * width), jnp.bfloat16),
        (place, *attended_parts, *weights),
        2 * tokens * 4 * depth * len(weights) * width,
    )


def assemble_kernel(place_ref, *refs):
    piece_refs, out_ref = refs[:-1], refs[-1]
    which = lax.rem(place_ref[0], 2)
    lo = place_ref[1]
    width = out_ref.shape[1] // 8
    chunks = len(piece_refs) // 2
    for d in range(2):
        for r in range(4):
            piece_ref = piece_refs[d * chunks + r * chunks // 4]
            block = (which ^ d) * 4 + (lo ^ r)
            out_ref[:, pl.ds(pl.multiple_of(block * width, width), width)] = piece_ref[
                :, pl.ds(r % (4 // chunks) * width, width)
            ]


def assemble(place, pieces):
    rows = pieces[0].shape[0]
    width = sum(piece.shape[1] for piece in pieces)
    shape = jax.ShapeDtypeStruct((rows, width), jnp.bfloat16)
    return local_kernel(assemble_kernel, shape, (place, *pieces), rows * width)


def normalised(tokens, norm_gain):
    source = tokens.astype(jnp.float32)
    return (
        source * lax.rsqrt(jnp.mean(source * source, axis=1, keepdims=True) + 1e-05) * norm_gain
    ).astype(jnp.bfloat16)


def plain_device(tokens, norm_gain, w_query, w_key, w_value, w_out, doc_starts):
    rows = tokens.shape[0]
    first = lax.axis_index("ctx") * rows
    normed = normalised(tokens, norm_gain)

    def project_with(weight):
        gathered = lax.all_gather(weight, "ctx", axis=0, tiled=True)
        total = jnp.dot(normed, gathered, preferred_element_type=jnp.float32)
        return total.astype(jnp.bfloat16)

    cosine, sine = rotary_tables(first + jnp.arange(rows, dtype=jnp.int32))
    place = jnp.concatenate([jnp.stack([first, jnp.zeros_like(first)]), doc_starts])
    query = project_with(w_query)
    key = project_with(w_key)
    value = project_with(w_value)
    kv_local = w_key.shape[1] // HD
    group = w_query.shape[1] // kv_local
    mixed = []
    for h in range(kv_local):
        lanes = slice(h * HD, (h + 1) * HD)
        pair = jnp.concatenate([key[:, lanes], value[:, lanes]], axis=1)
        pair = lax.all_gather(finish_pair(cosine, sine, [pair]), "ctx", axis=0, tiled=True)
        part = query[:, h * group : (h + 1) * group]
        mixed.append(attention(place, cosine, sine, [part], [pair], 1, 0))
    attended = jnp.concatenate(mixed, axis=1)
    wide = lax.all_gather(w_out, "ctx", axis=1, tiled=True)
    partial_out = jnp.dot(attended, wide, preferred_element_type=jnp.float32)
    return lax.psum_scatter(
        partial_out.astype(jnp.bfloat16), "head", scatter_dimension=1, tiled=True
    )


def after(value, *earlier):
    return lax.optimization_barrier((value, *earlier))[0]


def corner_after(blocks, *earlier):
    return corner([blocks[0], *lax.optimization_barrier((*blocks[1:], *earlier))[:2]])


def beside(block, r):
    return lax.ppermute(block, "lo", [(i, i ^ r) for i in range(4)])


def sides(block):
    return [block, beside(block, 1), beside(block, 2)]


def corner(blocks):
    half = blocks[0].shape[0] // 2
    return [*blocks, beside(blocks[2][:half], 1), beside(blocks[1][half:], 2)]


def along(block, d):
    return lax.ppermute(block, "hi", [(i, i ^ d) for i in range(4)])


def line_device(tokens, norm_gain, w_query, w_key, w_value, w_out, doc_starts):
    rows, features = tokens.shape
    hi = lax.axis_index("hi")
    lo = lax.axis_index("lo")
    core = lax.axis_index("head")
    which_half = lax.div(hi, 2)
    which = lax.rem(hi, 2)
    depth = features // 2
    heads = w_query.shape[1] // 4
    width = heads // 2

    def columns_for(chip, sources, width):
        return jnp.concatenate(
            [
                lax.dynamic_slice_in_dim(w, (2 * z + chip) * width, width, 1)
                for z in range(2)
                for w in sources
            ],
            axis=1,
        )

    def exchanged(sources, width):
        came = along(columns_for(1 - which, sources, width), 1)
        return jnp.concatenate([columns_for(which, sources, width), came], axis=0)

    pair_weight = corner(sides(exchanged((w_key, w_value), HD)))
    query_sides = sides(after(exchanged((w_query,), heads), *pair_weight[3:]))

    normed = normalised(tokens, norm_gain)
    own = lax.dynamic_slice_in_dim(normed, which_half * depth, depth, 1)

    def core_half(z):
        return lax.dynamic_slice_in_dim(normed, z * depth + core * (depth // 2), depth // 2, 1)

    near = along(core_half(which_half), 1)
    other = along(core_half(1 - which_half), 2)
    halves = jnp.concatenate([near, other, along(after(other, near), 1)], axis=0)
    token_parts = [own, halves, lax.ppermute(halves, "head", [(0, 1), (1, 0)])]
    index = jnp.stack([hi, lo, core])

    row_index = jnp.arange(4 * rows, dtype=jnp.int32)
    cosine, sine = rotary_tables((row_index // rows * 4 + lo) * rows + row_index % rows)

    kept, sent = product(index, token_parts, pair_weight, 0, 1)
    query_weight = corner_after(query_sides, sent)

    features_here = w_out.shape[0] // 2
    out_own = lax.dynamic_slice_in_dim(w_out, which_half * features_here, features_here, 0)
    out_other = lax.dynamic_slice_in_dim(w_out, (1 - which_half) * features_here, features_here, 0)
    out_other = along(after(out_other, sent), 2)
    kv_own = finish_pair(cosine, sine, [after(kept, out_other), along(sent, 2)])
    kv_going = after(kv_own, *query_weight[3:])
    kv_parts = [kv_own] + [beside(kv_going, r) for r in range(1, 4)]

    firsts = jnp.stack([lo, lo, lo ^ 1, lo ^ 2, lo ^ 3]) * rows
    seen = jnp.concatenate([firsts, doc_starts])
    out_sides = sides(after(jnp.concatenate([out_own, out_other], axis=0), *kv_parts[1:]))
    products = [product(index, token_parts, query_weight, c, 2) for c in range(2)]
    products[0] = (after(products[0][0], products[1][0]), products[0][1])
    attended = [
        attention(seen, cosine, sine, [kept, along(sent, 2)], kv_parts, 4, 4 * rows)
        for kept, sent in products
    ]
    out_blocks = corner_after(out_sides, *attended)
    out_blocks[3:] = [jnp.concatenate(out_blocks[3:], axis=0)]
    attended += [along(chunk, 1) for chunk in attended]

    def added(one, two):
        return (one.astype(jnp.float32) + two.astype(jnp.float32)).astype(jnp.bfloat16)

    kept = 2 * rows
    here, there, shares = [], [], []
    for blocks in (out_blocks[:2], out_blocks[2:]):
        blocks = [after(blocks[0], *shares[1:]), *blocks[1:]]
        theirs, mine = [
            project(jnp.stack([hi, group]), attended, blocks) for group in (1 - core, core)
        ]
        theirs = lax.ppermute(theirs, "head", [(0, 1), (1, 0)])
        shares = [
            added(
                lax.dynamic_slice_in_dim(mine, z * kept, kept, 0),
                lax.dynamic_slice_in_dim(theirs, z * kept, kept, 0),
            )
            for z in (which_half, 1 - which_half)
        ]
        summed = added(shares[0], along(shares[1], 2))
        here.append(lax.dynamic_slice_in_dim(summed, which * rows, rows, 0))
        there.append(along(lax.dynamic_slice_in_dim(summed, (1 - which) * rows, rows, 0), 1))
    return assemble(index, here + there)


def solution(mesh):
    ctx = mesh.shape["ctx"]
    heads = mesh.shape["head"]

    def run(tokens, norm_gain, w_query, w_key, w_value, w_out, doc_starts):
        lines = w_key.shape[1] // HD // heads
        if (ctx, heads, lines) == (16, 2, 4):
            both = ("hi", "lo")
            grid = Mesh(mesh.devices.reshape(4, 4, 2), ("hi", "lo", "head"))
            body = line_device
        else:
            both, grid, body = "ctx", mesh, plain_device
        placed = (
            P(both, None),
            P(),
            P(both, "head"),
            P(both, "head"),
            P(both, "head"),
            P("head", both),
            P(),
        )
        return jax.shard_map(
            body, mesh=grid, in_specs=placed, out_specs=P(both, "head"), check_vma=False
        )(tokens, norm_gain, w_query, w_key, w_value, w_out, doc_starts)

    return run
```

```python
import functools

import jax
import jax.numpy as jnp
from jax import lax
from jax.experimental import pallas as pl
from jax.experimental.pallas import tpu as pltpu
from jax.sharding import Mesh
from jax.sharding import PartitionSpec as P

HD = 128
HALF = HD // 2
MIB = 1024 * 1024


def local_kernel(body, out_shape, operands, flops, scratch=(), exps=0):
    size = sum(x.size * x.dtype.itemsize for x in operands)
    return pl.pallas_call(
        body,
        in_specs=[pl.BlockSpec(memory_space=pltpu.SMEM)]
        + [pl.BlockSpec(memory_space=pltpu.VMEM)] * (len(operands) - 1),
        out_shape=out_shape,
        scratch_shapes=scratch,
        compiler_params=pltpu.CompilerParams(vmem_limit_bytes=12 * MIB),
        cost_estimate=pl.CostEstimate(flops=flops, bytes_accessed=size, transcendentals=exps),
    )(*operands)


def rotary_tables(positions):
    freqs = 500000.0 ** (-(jnp.arange(HALF, dtype=jnp.float32) * 2.0 / HD))
    angles = positions.astype(jnp.float32)[:, None] * freqs[None, :]
    cosine = jnp.cos(angles)
    sine = jnp.sin(angles)
    return (
        jnp.concatenate([cosine, cosine], axis=1),
        jnp.concatenate([-sine, sine], axis=1),
    )


def summed_lanes(refs, lanes):
    total = refs[0][:, lanes].astype(jnp.float32)
    for ref in refs[1:]:
        total = total + ref[:, lanes].astype(jnp.float32)
    return total


def rotated(values, cos_ref, sin_ref):
    return values * cos_ref[...] + pltpu.roll(values, HALF, 1) * sin_ref[...]


def pair_kernel(unused_ref, cos_ref, sin_ref, *refs):
    parts, out_ref = refs[:-1], refs[-1]
    key = rotated(summed_lanes(parts, pl.ds(0, HD)), cos_ref, sin_ref)
    out_ref[:, pl.ds(0, HD)] = key.astype(jnp.bfloat16)
    out_ref[:, pl.ds(HD, HD)] = summed_lanes(parts, pl.ds(HD, HD)).astype(jnp.bfloat16)


def finish_pair(cosine, sine, parts):
    operands = (jnp.zeros((1,), jnp.int32), cosine, sine, *parts)
    shape = jax.ShapeDtypeStruct(parts[0].shape, jnp.bfloat16)
    return local_kernel(pair_kernel, shape, operands, 8 * parts[0].size)


def attention_kernel(blocks, stride, n_query, n_kv, place_ref, cos_ref, sin_ref, *refs):
    query_refs = refs[:n_query]
    kv_refs = refs[n_query : n_query + n_kv]
    out_ref, turned, bias = refs[n_query + n_kv :]
    heads, tokens, _ = turned.shape
    for h in range(heads):
        total = summed_lanes(query_refs, pl.ds(h * HD, HD))
        turned[h] = rotated(total, cos_ref, sin_ref).astype(jnp.bfloat16)
    rows = tokens // blocks
    kv_rows = kv_refs[0].shape[0] // blocks
    documents = place_ref.shape[0] - 1 - n_kv
    scale = HD**-0.5
    for j in range(blocks):
        first = j * rows
        length = kv_rows * (j + 1)
        qpos = lax.broadcasted_iota(jnp.int32, (rows, HD), 0) + (place_ref[0] + j * stride)
        qstart = jnp.zeros_like(qpos)
        for i in range(documents):
            start = place_ref[1 + n_kv + i]
            qstart = jnp.where(qpos >= start, start, qstart)
        span = qpos - qstart
        for d in range(n_kv):
            for b in range(j + 1):
                for c in range(0, kv_rows, HD):
                    kpos = lax.broadcasted_iota(jnp.int32, (rows, HD), 1) + (
                        place_ref[1 + d] + (b * stride + c)
                    )
                    back = qpos - kpos
                    visible = (back >= 0) & (back <= span)
                    bias[:, pl.ds(d * length + b * kv_rows + c, HD)] = jnp.where(
                        visible, 0.0, -jnp.inf
                    )

        def one_head(h, unused):
            query = turned[h, pl.ds(first, rows), :]
            scores = []
            for d in range(n_kv):
                part = lax.dot_general(
                    query,
                    kv_refs[d][pl.ds(0, length), pl.ds(0, HD)],
                    (((1,), (1,)), ((), ())),
                    preferred_element_type=jnp.float32,
                )
                scores.append(part + bias[:, pl.ds(d * length, length)])
            highest = functools.reduce(
                jnp.maximum, [jnp.max(s, axis=1, keepdims=True) for s in scores]
            )
            denominator = 0.0
            mixed = 0.0
            for d in range(n_kv):
                probs = jnp.exp((scores[d] - highest) * scale)
                denominator = denominator + jnp.sum(probs, axis=1, keepdims=True)
                mixed = mixed + jnp.dot(
                    probs.astype(jnp.bfloat16),
                    kv_refs[d][pl.ds(0, length), pl.ds(HD, HD)],
                    preferred_element_type=jnp.float32,
                )
            lanes = pl.ds(pl.multiple_of(h * HD, HD), HD)
            out_ref[pl.ds(first, rows), lanes] = (mixed / denominator).astype(jnp.bfloat16)
            return unused

        lax.fori_loop(0, heads, one_head, 0)


def attention(place, cosine, sine, query_parts, kv_parts, blocks, stride):
    tokens, width = query_parts[0].shape
    heads = width // HD
    keys = sum(part.shape[0] for part in kv_parts)
    return local_kernel(
        functools.partial(attention_kernel, blocks, stride, len(query_parts), len(kv_parts)),
        jax.ShapeDtypeStruct((tokens, width), jnp.bfloat16),
        (place, cosine, sine, *query_parts, *kv_parts),
        32 * tokens * width * keys,
        [
            pltpu.VMEM((heads, tokens, HD), jnp.bfloat16),
            pltpu.VMEM((tokens // blocks, keys), jnp.float32),
        ],
        tokens * heads * keys,
    )


def product_kernel(place_ref, *refs):
    own_ref, half_refs = refs[0], refs[1:3]
    weight_refs, out_refs, gathered = refs[3:8], refs[8:10], refs[10]
    hi = place_ref[0]
    lo = place_ref[1]
    rows, depth = own_ref.shape
    share = weight_refs[3].shape[0]
    gathered[pl.ds(pl.multiple_of(hi * rows, rows), rows), :] = own_ref[...]
    for side, half_ref in enumerate(half_refs):
        first = lax.rem(place_ref[2] + side, 2) * (depth // 2)
        features = pl.ds(pl.multiple_of(first, depth // 2), depth // 2)
        for d in range(1, 4):
            gathered[pl.ds(pl.multiple_of((hi ^ d) * rows, rows), rows), features] = half_ref[
                pl.ds((d - 1) * rows, rows), :
            ]
    for side, out_ref in enumerate(out_refs):
        width = out_ref.shape[1]
        first = (lax.div(hi, 2) ^ side) * place_ref[3] + place_ref[4]
        columns = pl.ds(pl.multiple_of(first, width), width)
        total = 0.0
        for part in range(2):
            for r in range(4):
                if r < 3:
                    weight = weight_refs[r][pl.ds(part * share, share), columns]
                else:
                    weight = weight_refs[3 + part][:, columns]
                block = (lax.rem(hi, 2) ^ part) * 4 + (lo ^ r)
                total = total + jnp.dot(
                    gathered[:, pl.ds(pl.multiple_of(block * share, share), share)],
                    weight,
                    preferred_element_type=jnp.float32,
                )
        out_ref[...] = total.astype(jnp.bfloat16)


def product(index, token_parts, weights, chunk, chunks):
    rows, depth = token_parts[0].shape
    step = weights[0].shape[1] // 2
    width = step // chunks
    place = jnp.concatenate([index, jnp.array([step, chunk * width], jnp.int32)])
    shape = jax.ShapeDtypeStruct((4 * rows, width), jnp.bfloat16)
    return local_kernel(
        product_kernel,
        (shape,) * 2,
        (place, *token_parts, *weights),
        2 * 4 * rows * depth * 2 * width,
        [pltpu.VMEM((4 * rows, depth), jnp.bfloat16)],
    )


def project_kernel(place_ref, *refs):
    attended_refs, weight_refs, out_ref = refs[:4], refs[4:-1], refs[-1]
    hi = place_ref[0]
    side = lax.div(hi, 2) ^ place_ref[1]
    depth = attended_refs[0].shape[1]
    features, width = weight_refs[0].shape
    span = features // 4
    for r, weight_ref in enumerate(weight_refs):
        total = 0.0
        for k, attended_ref in enumerate(attended_refs):
            first = side * (2 * span) + (lax.rem(hi, 2) ^ (k // 2)) * span + (k % 2) * depth
            total = total + jnp.dot(
                attended_ref[...],
                weight_ref[pl.ds(pl.multiple_of(first, depth), depth), :],
                preferred_element_type=jnp.float32,
            )
        out_ref[:, pl.ds(r * width, width)] = total.astype(out_ref.dtype)


def project(place, attended_parts, weights):
    tokens, depth = attended_parts[0].shape
    width = weights[0].shape[1]
    return local_kernel(
        project_kernel,
        jax.ShapeDtypeStruct((tokens, len(weights) * width), jnp.bfloat16),
        (place, *attended_parts, *weights),
        2 * tokens * 4 * depth * len(weights) * width,
    )


def assemble_kernel(place_ref, *refs):
    piece_refs, out_ref = refs[:-1], refs[-1]
    which = lax.rem(place_ref[0], 2)
    lo = place_ref[1]
    width = out_ref.shape[1] // 8
    chunks = len(piece_refs) // 2
    for d in range(2):
        for r in range(4):
            piece_ref = piece_refs[d * chunks + r * chunks // 4]
            block = (which ^ d) * 4 + (lo ^ r)
            out_ref[:, pl.ds(pl.multiple_of(block * width, width), width)] = piece_ref[
                :, pl.ds(r % (4 // chunks) * width, width)
            ]


def assemble(place, pieces):
    rows = pieces[0].shape[0]
    width = sum(piece.shape[1] for piece in pieces)
    shape = jax.ShapeDtypeStruct((rows, width), jnp.bfloat16)
    return local_kernel(assemble_kernel, shape, (place, *pieces), rows * width)


def normalised(tokens, norm_gain):
    source = tokens.astype(jnp.float32)
    return (
        source * lax.rsqrt(jnp.mean(source * source, axis=1, keepdims=True) + 1e-05) * norm_gain
    ).astype(jnp.bfloat16)


def plain_device(tokens, norm_gain, w_query, w_key, w_value, w_out, doc_starts):
    rows = tokens.shape[0]
    first = lax.axis_index("ctx") * rows
    normed = normalised(tokens, norm_gain)

    def project_with(weight):
        gathered = lax.all_gather(weight, "ctx", axis=0, tiled=True)
        total = jnp.dot(normed, gathered, preferred_element_type=jnp.float32)
        return total.astype(jnp.bfloat16)

    cosine, sine = rotary_tables(first + jnp.arange(rows, dtype=jnp.int32))
    place = jnp.concatenate([jnp.stack([first, jnp.zeros_like(first)]), doc_starts])
    query = project_with(w_query)
    key = project_with(w_key)
    value = project_with(w_value)
    kv_local = w_key.shape[1] // HD
    group = w_query.shape[1] // kv_local
    mixed = []
    for h in range(kv_local):
        lanes = slice(h * HD, (h + 1) * HD)
        pair = jnp.concatenate([key[:, lanes], value[:, lanes]], axis=1)
        pair = lax.all_gather(finish_pair(cosine, sine, [pair]), "ctx", axis=0, tiled=True)
        part = query[:, h * group : (h + 1) * group]
        mixed.append(attention(place, cosine, sine, [part], [pair], 1, 0))
    attended = jnp.concatenate(mixed, axis=1)
    wide = lax.all_gather(w_out, "ctx", axis=1, tiled=True)
    partial_out = jnp.dot(attended, wide, preferred_element_type=jnp.float32)
    return lax.psum_scatter(
        partial_out.astype(jnp.bfloat16), "head", scatter_dimension=1, tiled=True
    )


def after(value, *earlier):
    return lax.optimization_barrier((value, *earlier))[0]


def corner_after(blocks, *earlier):
    return corner([blocks[0], *lax.optimization_barrier((*blocks[1:], *earlier))[:2]])


def beside(block, r):
    return lax.ppermute(block, "lo", [(i, i ^ r) for i in range(4)])


def sides(block):
    return [block, beside(block, 1), beside(block, 2)]


def corner(blocks):
    half = blocks[0].shape[0] // 2
    return [*blocks, beside(blocks[2][:half], 1), beside(blocks[1][half:], 2)]


def along(block, d):
    return lax.ppermute(block, "hi", [(i, i ^ d) for i in range(4)])


def line_device(tokens, norm_gain, w_query, w_key, w_value, w_out, doc_starts):
    rows, features = tokens.shape
    hi = lax.axis_index("hi")
    lo = lax.axis_index("lo")
    core = lax.axis_index("head")
    which_half = lax.div(hi, 2)
    which = lax.rem(hi, 2)
    depth = features // 2
    heads = w_query.shape[1] // 4
    width = heads // 2

    def columns_for(chip, sources, width):
        return jnp.concatenate(
            [
                lax.dynamic_slice_in_dim(w, (2 * z + chip) * width, width, 1)
                for z in range(2)
                for w in sources
            ],
            axis=1,
        )

    def exchanged(sources, width, *earlier):
        came = along(after(columns_for(1 - which, sources, width), *earlier), 1)
        return jnp.concatenate([columns_for(which, sources, width), came], axis=0)

    pair_both = exchanged((w_key, w_value), HD)
    pair_weight = corner(sides(pair_both))
    query_both = exchanged((w_query,), heads, pair_both)
    query_sides = sides(after(query_both, *pair_weight[3:]))

    normed = normalised(tokens, norm_gain)
    own = lax.dynamic_slice_in_dim(normed, which_half * depth, depth, 1)

    def core_half(z):
        return lax.dynamic_slice_in_dim(normed, z * depth + core * (depth // 2), depth // 2, 1)

    near = along(core_half(which_half), 1)
    other = along(core_half(1 - which_half), 2)
    halves = jnp.concatenate([near, other, along(after(other, near), 1)], axis=0)
    features_here = w_out.shape[0] // 2
    out_own = lax.dynamic_slice_in_dim(w_out, which_half * features_here, features_here, 0)
    out_other = lax.dynamic_slice_in_dim(w_out, (1 - which_half) * features_here, features_here, 0)
    out_other = along(after(out_other, near, other), 2)
    own = after(own, out_other)
    token_parts = [own, halves, lax.ppermute(halves, "head", [(0, 1), (1, 0)])]
    index = jnp.stack([hi, lo, core])

    row_index = jnp.arange(4 * rows, dtype=jnp.int32)
    cosine, sine = rotary_tables((row_index // rows * 4 + lo) * rows + row_index % rows)

    kept, sent = product(index, token_parts, pair_weight, 0, 1)
    query_weight = corner_after(query_sides, sent)

    kv_own = finish_pair(cosine, sine, [kept, along(sent, 2)])
    kv_going = after(kv_own, *query_weight[3:])
    kv_parts = [kv_own] + [beside(kv_going, r) for r in range(1, 4)]

    firsts = jnp.stack([lo, lo, lo ^ 1, lo ^ 2, lo ^ 3]) * rows
    seen = jnp.concatenate([firsts, doc_starts])
    out_sides = sides(after(jnp.concatenate([out_own, out_other], axis=0), *kv_parts[1:]))
    products = [product(index, token_parts, query_weight, c, 2) for c in range(2)]
    products[0] = (after(products[0][0], products[1][0]), products[0][1])
    attended = [
        attention(seen, cosine, sine, [kept, along(sent, 2)], kv_parts, 4, 4 * rows)
        for kept, sent in products
    ]
    out_blocks = corner_after(out_sides, *attended)
    out_blocks[3:] = [jnp.concatenate(out_blocks[3:], axis=0)]
    attended += [along(chunk, 1) for chunk in attended]

    def added(one, two):
        return (one.astype(jnp.float32) + two.astype(jnp.float32)).astype(jnp.bfloat16)

    kept = 2 * rows
    here, there, shares, summed = [], [], [], None
    for blocks in (out_blocks[:2], out_blocks[2:]):
        first = [after(blocks[0], *shares[1:]), *blocks[1:]]
        theirs = project(jnp.stack([hi, 1 - core]), attended, first)
        last = first if summed is None else [after(first[0], summed), *first[1:]]
        mine = project(jnp.stack([hi, core]), attended, last)
        theirs = lax.ppermute(theirs, "head", [(0, 1), (1, 0)])
        shares = [
            added(
                lax.dynamic_slice_in_dim(mine, z * kept, kept, 0),
                lax.dynamic_slice_in_dim(theirs, z * kept, kept, 0),
            )
            for z in (which_half, 1 - which_half)
        ]
        summed = added(shares[0], along(shares[1], 2))
        here.append(lax.dynamic_slice_in_dim(summed, which * rows, rows, 0))
        there.append(along(lax.dynamic_slice_in_dim(summed, (1 - which) * rows, rows, 0), 1))
    return assemble(index, here + there)


def solution(mesh):
    ctx = mesh.shape["ctx"]
    heads = mesh.shape["head"]

    def run(tokens, norm_gain, w_query, w_key, w_value, w_out, doc_starts):
        lines = w_key.shape[1] // HD // heads
        if (ctx, heads, lines) == (16, 2, 4):
            both = ("hi", "lo")
            grid = Mesh(mesh.devices.reshape(4, 4, 2), ("hi", "lo", "head"))
            body = line_device
        else:
            both, grid, body = "ctx", mesh, plain_device
        placed = (
            P(both, None),
            P(),
            P(both, "head"),
            P(both, "head"),
            P(both, "head"),
            P("head", both),
            P(),
        )
        return jax.shard_map(
            body, mesh=grid, in_specs=placed, out_specs=P(both, "head"), check_vma=False
        )(tokens, norm_gain, w_query, w_key, w_value, w_out, doc_starts)

    return run
```

```python
import functools

import jax
import jax.numpy as jnp
from jax import lax
from jax.experimental import pallas as pl
from jax.experimental.pallas import tpu as pltpu
from jax.sharding import Mesh
from jax.sharding import PartitionSpec as P

HD = 128
HALF = HD // 2
MIB = 1024 * 1024


def local_kernel(body, out_shape, operands, flops, scratch=(), exps=0):
    size = sum(x.size * x.dtype.itemsize for x in operands)
    return pl.pallas_call(
        body,
        in_specs=[pl.BlockSpec(memory_space=pltpu.SMEM)]
        + [pl.BlockSpec(memory_space=pltpu.VMEM)] * (len(operands) - 1),
        out_shape=out_shape,
        scratch_shapes=scratch,
        compiler_params=pltpu.CompilerParams(vmem_limit_bytes=12 * MIB),
        cost_estimate=pl.CostEstimate(flops=flops, bytes_accessed=size, transcendentals=exps),
    )(*operands)


def rotary_tables(positions):
    freqs = 500000.0 ** (-(jnp.arange(HALF, dtype=jnp.float32) * 2.0 / HD))
    angles = positions.astype(jnp.float32)[:, None] * freqs[None, :]
    cosine = jnp.cos(angles)
    sine = jnp.sin(angles)
    return (
        jnp.concatenate([cosine, cosine], axis=1),
        jnp.concatenate([-sine, sine], axis=1),
    )


def summed_lanes(refs, lanes):
    total = refs[0][:, lanes].astype(jnp.float32)
    for ref in refs[1:]:
        total = total + ref[:, lanes].astype(jnp.float32)
    return total


def rotated(values, cos_ref, sin_ref):
    return values * cos_ref[...] + pltpu.roll(values, HALF, 1) * sin_ref[...]


def pair_kernel(unused_ref, cos_ref, sin_ref, *refs):
    parts, out_ref = refs[:-1], refs[-1]
    key = rotated(summed_lanes(parts, pl.ds(0, HD)), cos_ref, sin_ref)
    out_ref[:, pl.ds(0, HD)] = key.astype(jnp.bfloat16)
    out_ref[:, pl.ds(HD, HD)] = summed_lanes(parts, pl.ds(HD, HD)).astype(jnp.bfloat16)


def finish_pair(cosine, sine, parts):
    operands = (jnp.zeros((1,), jnp.int32), cosine, sine, *parts)
    shape = jax.ShapeDtypeStruct(parts[0].shape, jnp.bfloat16)
    return local_kernel(pair_kernel, shape, operands, 8 * parts[0].size)


def attention_kernel(blocks, stride, n_query, n_kv, place_ref, cos_ref, sin_ref, *refs):
    query_refs = refs[:n_query]
    kv_refs = refs[n_query : n_query + n_kv]
    out_ref, turned, bias = refs[n_query + n_kv :]
    heads, tokens, _ = turned.shape
    for h in range(heads):
        total = summed_lanes(query_refs, pl.ds(h * HD, HD))
        turned[h] = rotated(total, cos_ref, sin_ref).astype(jnp.bfloat16)
    rows = tokens // blocks
    kv_rows = kv_refs[0].shape[0] // blocks
    documents = place_ref.shape[0] - 1 - n_kv
    scale = HD**-0.5
    for j in range(blocks):
        first = j * rows
        length = kv_rows * (j + 1)
        qpos = lax.broadcasted_iota(jnp.int32, (rows, HD), 0) + (place_ref[0] + j * stride)
        qstart = jnp.zeros_like(qpos)
        for i in range(documents):
            start = place_ref[1 + n_kv + i]
            qstart = jnp.where(qpos >= start, start, qstart)
        span = qpos - qstart
        for d in range(n_kv):
            for b in range(j + 1):
                for c in range(0, kv_rows, HD):
                    kpos = lax.broadcasted_iota(jnp.int32, (rows, HD), 1) + (
                        place_ref[1 + d] + (b * stride + c)
                    )
                    back = qpos - kpos
                    visible = (back >= 0) & (back <= span)
                    bias[:, pl.ds(d * length + b * kv_rows + c, HD)] = jnp.where(
                        visible, 0.0, -jnp.inf
                    )

        def one_head(h, unused):
            query = turned[h, pl.ds(first, rows), :]
            scores = []
            for d in range(n_kv):
                part = lax.dot_general(
                    query,
                    kv_refs[d][pl.ds(0, length), pl.ds(0, HD)],
                    (((1,), (1,)), ((), ())),
                    preferred_element_type=jnp.float32,
                )
                scores.append(part + bias[:, pl.ds(d * length, length)])
            highest = functools.reduce(
                jnp.maximum, [jnp.max(s, axis=1, keepdims=True) for s in scores]
            )
            denominator = 0.0
            mixed = 0.0
            for d in range(n_kv):
                probs = jnp.exp((scores[d] - highest) * scale)
                denominator = denominator + jnp.sum(probs, axis=1, keepdims=True)
                mixed = mixed + jnp.dot(
                    probs.astype(jnp.bfloat16),
                    kv_refs[d][pl.ds(0, length), pl.ds(HD, HD)],
                    preferred_element_type=jnp.float32,
                )
            lanes = pl.ds(pl.multiple_of(h * HD, HD), HD)
            out_ref[pl.ds(first, rows), lanes] = (mixed / denominator).astype(jnp.bfloat16)
            return unused

        lax.fori_loop(0, heads, one_head, 0)


def attention(place, cosine, sine, query_parts, kv_parts, blocks, stride):
    tokens, width = query_parts[0].shape
    heads = width // HD
    keys = sum(part.shape[0] for part in kv_parts)
    return local_kernel(
        functools.partial(attention_kernel, blocks, stride, len(query_parts), len(kv_parts)),
        jax.ShapeDtypeStruct((tokens, width), jnp.bfloat16),
        (place, cosine, sine, *query_parts, *kv_parts),
        32 * tokens * width * keys,
        [
            pltpu.VMEM((heads, tokens, HD), jnp.bfloat16),
            pltpu.VMEM((tokens // blocks, keys), jnp.float32),
        ],
        tokens * heads * keys,
    )


def product_kernel(place_ref, *refs):
    own_ref, half_refs = refs[0], refs[1:3]
    weight_refs, out_refs, gathered = refs[3:8], refs[8:10], refs[10]
    hi = place_ref[0]
    lo = place_ref[1]
    rows, depth = own_ref.shape
    share = weight_refs[3].shape[0]
    gathered[pl.ds(pl.multiple_of(hi * rows, rows), rows), :] = own_ref[...]
    for side, half_ref in enumerate(half_refs):
        first = lax.rem(place_ref[2] + side, 2) * (depth // 2)
        features = pl.ds(pl.multiple_of(first, depth // 2), depth // 2)
        for d in range(1, 4):
            gathered[pl.ds(pl.multiple_of((hi ^ d) * rows, rows), rows), features] = half_ref[
                pl.ds((d - 1) * rows, rows), :
            ]
    for side, out_ref in enumerate(out_refs):
        width = out_ref.shape[1]
        first = (lax.div(hi, 2) ^ side) * place_ref[3] + place_ref[4]
        columns = pl.ds(pl.multiple_of(first, width), width)
        total = 0.0
        for part in range(2):
            for r in range(4):
                if r < 3:
                    weight = weight_refs[r][pl.ds(part * share, share), columns]
                else:
                    weight = weight_refs[3 + part][:, columns]
                block = (lax.rem(hi, 2) ^ part) * 4 + (lo ^ r)
                total = total + jnp.dot(
                    gathered[:, pl.ds(pl.multiple_of(block * share, share), share)],
                    weight,
                    preferred_element_type=jnp.float32,
                )
        out_ref[...] = total.astype(jnp.bfloat16)


def product(index, token_parts, weights, chunk, chunks):
    rows, depth = token_parts[0].shape
    step = weights[0].shape[1] // 2
    width = step // chunks
    place = jnp.concatenate([index, jnp.array([step, chunk * width], jnp.int32)])
    shape = jax.ShapeDtypeStruct((4 * rows, width), jnp.bfloat16)
    return local_kernel(
        product_kernel,
        (shape,) * 2,
        (place, *token_parts, *weights),
        2 * 4 * rows * depth * 2 * width,
        [pltpu.VMEM((4 * rows, depth), jnp.bfloat16)],
    )


def project_kernel(place_ref, *refs):
    attended_refs, weight_refs, out_ref = refs[:4], refs[4:-1], refs[-1]
    hi = place_ref[0]
    kept, columns = out_ref.shape
    rows = pl.ds(pl.multiple_of(place_ref[1] * kept, kept), kept)
    depth = attended_refs[0].shape[1]
    features, width = weight_refs[0].shape
    span = features // 4
    for chip in range(2):
        side = lax.rem(hi, 2) ^ chip
        for r, weight_ref in enumerate(weight_refs):
            total = 0.0
            for k, attended_ref in enumerate(attended_refs):
                first = side * (2 * span) + (lax.div(hi, 2) ^ (k // 2)) * span + (k % 2) * depth
                total = total + jnp.dot(
                    attended_ref[rows, :],
                    weight_ref[pl.ds(pl.multiple_of(first, depth), depth), :],
                    preferred_element_type=jnp.float32,
                )
            place = chip * (columns // 2) + r * width
            out_ref[:, pl.ds(place, width)] = total.astype(out_ref.dtype)


def project(place, attended_parts, weights):
    tokens, depth = attended_parts[0].shape
    width = 2 * len(weights) * weights[0].shape[1]
    return local_kernel(
        project_kernel,
        jax.ShapeDtypeStruct((tokens // 2, width), jnp.bfloat16),
        (place, *attended_parts, *weights),
        2 * (tokens // 2) * 4 * depth * width,
    )


def assemble_kernel(place_ref, *refs):
    piece_refs, out_ref = refs[:-1], refs[-1]
    lo = place_ref[1]
    width = out_ref.shape[1] // 8
    each = 4 // len(piece_refs)
    for chip in range(2):
        for r in range(4):
            out_ref[:, pl.ds(pl.multiple_of((chip * 4 + (lo ^ r)) * width, width), width)] = (
                piece_refs[r // each][:, pl.ds((chip * each + r % each) * width, width)]
            )


def assemble(place, pieces):
    rows = pieces[0].shape[0]
    width = sum(piece.shape[1] for piece in pieces)
    shape = jax.ShapeDtypeStruct((rows, width), jnp.bfloat16)
    return local_kernel(assemble_kernel, shape, (place, *pieces), rows * width)


def normalised(tokens, norm_gain):
    source = tokens.astype(jnp.float32)
    return (
        source * lax.rsqrt(jnp.mean(source * source, axis=1, keepdims=True) + 1e-05) * norm_gain
    ).astype(jnp.bfloat16)


def plain_device(tokens, norm_gain, w_query, w_key, w_value, w_out, doc_starts):
    rows = tokens.shape[0]
    first = lax.axis_index("ctx") * rows
    normed = normalised(tokens, norm_gain)

    def project_with(weight):
        gathered = lax.all_gather(weight, "ctx", axis=0, tiled=True)
        total = jnp.dot(normed, gathered, preferred_element_type=jnp.float32)
        return total.astype(jnp.bfloat16)

    cosine, sine = rotary_tables(first + jnp.arange(rows, dtype=jnp.int32))
    place = jnp.concatenate([jnp.stack([first, jnp.zeros_like(first)]), doc_starts])
    query = project_with(w_query)
    key = project_with(w_key)
    value = project_with(w_value)
    kv_local = w_key.shape[1] // HD
    group = w_query.shape[1] // kv_local
    mixed = []
    for h in range(kv_local):
        lanes = slice(h * HD, (h + 1) * HD)
        pair = jnp.concatenate([key[:, lanes], value[:, lanes]], axis=1)
        pair = lax.all_gather(finish_pair(cosine, sine, [pair]), "ctx", axis=0, tiled=True)
        part = query[:, h * group : (h + 1) * group]
        mixed.append(attention(place, cosine, sine, [part], [pair], 1, 0))
    attended = jnp.concatenate(mixed, axis=1)
    wide = lax.all_gather(w_out, "ctx", axis=1, tiled=True)
    partial_out = jnp.dot(attended, wide, preferred_element_type=jnp.float32)
    return lax.psum_scatter(
        partial_out.astype(jnp.bfloat16), "head", scatter_dimension=1, tiled=True
    )


def after(value, *earlier):
    return lax.optimization_barrier((value, *earlier))[0]


def corner_after(blocks, *earlier):
    return corner([blocks[0], *lax.optimization_barrier((*blocks[1:], *earlier))[:2]])


def beside(block, r):
    return lax.ppermute(block, "lo", [(i, i ^ r) for i in range(4)])


def sides(block):
    return [block, beside(block, 1), beside(block, 2)]


def corner(blocks):
    half = blocks[0].shape[0] // 2
    return [*blocks, beside(blocks[2][:half], 1), beside(blocks[1][half:], 2)]


def along(block, d):
    return lax.ppermute(block, "hi", [(i, i ^ d) for i in range(4)])


def line_device(tokens, norm_gain, w_query, w_key, w_value, w_out, doc_starts):
    rows, features = tokens.shape
    hi = lax.axis_index("hi")
    lo = lax.axis_index("lo")
    core = lax.axis_index("head")
    which_half = lax.div(hi, 2)
    which = lax.rem(hi, 2)
    depth = features // 2
    heads = w_query.shape[1] // 4
    width = heads // 2

    def columns_for(chip, sources, width):
        return jnp.concatenate(
            [
                lax.dynamic_slice_in_dim(w, (2 * z + chip) * width, width, 1)
                for z in range(2)
                for w in sources
            ],
            axis=1,
        )

    def exchanged(sources, width, *earlier):
        came = along(after(columns_for(1 - which, sources, width), *earlier), 1)
        return jnp.concatenate([columns_for(which, sources, width), came], axis=0)

    pair_both = exchanged((w_key, w_value), HD)
    pair_weight = corner(sides(pair_both))
    query_both = exchanged((w_query,), heads, pair_both)
    query_sides = sides(after(query_both, *pair_weight[3:]))

    normed = normalised(tokens, norm_gain)
    own = lax.dynamic_slice_in_dim(normed, which_half * depth, depth, 1)

    def core_half(z):
        return lax.dynamic_slice_in_dim(normed, z * depth + core * (depth // 2), depth // 2, 1)

    near = along(core_half(which_half), 1)
    other = along(core_half(1 - which_half), 2)
    halves = jnp.concatenate([near, other, along(after(other, near), 1)], axis=0)
    token_parts = [own, halves, lax.ppermute(halves, "head", [(0, 1), (1, 0)])]
    index = jnp.stack([hi, lo, core])

    row_index = jnp.arange(4 * rows, dtype=jnp.int32)
    cosine, sine = rotary_tables((row_index // rows * 4 + lo) * rows + row_index % rows)

    kept, sent = product(index, token_parts, pair_weight, 0, 1)
    query_weight = corner_after(query_sides, sent)

    def rows_for(chip):
        return jnp.concatenate(
            [lax.dynamic_slice_in_dim(w_out, (2 * z + chip) * heads, heads, 0) for z in range(2)],
            axis=0,
        )

    out_both = jnp.concatenate(
        [rows_for(which), along(after(rows_for(1 - which), sent), 1)], axis=0
    )

    kv_own = finish_pair(cosine, sine, [kept, along(sent, 2)])
    kv_going = after(kv_own, *query_weight[3:])
    kv_parts = [kv_own] + [beside(kv_going, r) for r in range(1, 4)]

    firsts = jnp.stack([lo, lo, lo ^ 1, lo ^ 2, lo ^ 3]) * rows
    seen = jnp.concatenate([firsts, doc_starts])
    out_sides = sides(after(out_both, *kv_parts[1:]))
    products = [product(index, token_parts, query_weight, c, 2) for c in range(2)]
    products[0] = (after(products[0][0], products[1][0]), products[0][1])
    attended = [
        attention(seen, cosine, sine, [kept, along(sent, 2)], kv_parts, 4, 4 * rows)
        for kept, sent in products
    ]
    out_blocks = corner_after(out_sides, *attended)
    out_blocks[3:] = [jnp.concatenate(out_blocks[3:], axis=0)]
    attended += [along(chunk, 2) for chunk in attended]

    def added(one, two):
        return (one.astype(jnp.float32) + two.astype(jnp.float32)).astype(jnp.bfloat16)

    home = [
        ((2 * half + chip) * 2 + group, (2 * group + chip) * 2 + half)
        for half in range(2)
        for chip in range(2)
        for group in range(2)
    ]
    pieces, shares, summed = [], [], None
    for blocks in (out_blocks[:2], out_blocks[2:]):
        first = [after(blocks[0], *shares[1:]), *blocks[1:]]
        theirs = project(jnp.stack([hi, 1 - core]), attended, first)
        last = first if summed is None else [after(first[0], summed), *first[1:]]
        mine = project(jnp.stack([hi, core]), attended, last)
        theirs = lax.ppermute(theirs, "head", [(0, 1), (1, 0)])
        shares = [
            added(
                lax.dynamic_slice_in_dim(mine, chip * rows, rows, 0),
                lax.dynamic_slice_in_dim(theirs, chip * rows, rows, 0),
            )
            for chip in (which, 1 - which)
        ]
        summed = added(shares[0], along(shares[1], 1))
        pieces.append(lax.ppermute(summed, ("hi", "head"), home))
    return assemble(index, pieces)


def solution(mesh):
    ctx = mesh.shape["ctx"]
    heads = mesh.shape["head"]

    def run(tokens, norm_gain, w_query, w_key, w_value, w_out, doc_starts):
        lines = w_key.shape[1] // HD // heads
        if (ctx, heads, lines) == (16, 2, 4):
            both = ("hi", "lo")
            grid = Mesh(mesh.devices.reshape(4, 4, 2), ("hi", "lo", "head"))
            body = line_device
        else:
            both, grid, body = "ctx", mesh, plain_device
        placed = (
            P(both, None),
            P(),
            P(both, "head"),
            P(both, "head"),
            P(both, "head"),
            P("head", both),
            P(),
        )
        return jax.shard_map(
            body, mesh=grid, in_specs=placed, out_specs=P(both, "head"), check_vma=False
        )(tokens, norm_gain, w_query, w_key, w_value, w_out, doc_starts)

    return run
```

```python
import functools

import jax
import jax.numpy as jnp
from jax import lax
from jax.experimental import pallas as pl
from jax.experimental.pallas import tpu as pltpu
from jax.sharding import Mesh
from jax.sharding import PartitionSpec as P

HD = 128
HALF = HD // 2
MIB = 1024 * 1024


def local_kernel(body, out_shape, operands, flops, scratch=(), exps=0):
    size = sum(x.size * x.dtype.itemsize for x in operands)
    return pl.pallas_call(
        body,
        in_specs=[pl.BlockSpec(memory_space=pltpu.SMEM)]
        + [pl.BlockSpec(memory_space=pltpu.VMEM)] * (len(operands) - 1),
        out_shape=out_shape,
        scratch_shapes=scratch,
        compiler_params=pltpu.CompilerParams(vmem_limit_bytes=12 * MIB),
        cost_estimate=pl.CostEstimate(flops=flops, bytes_accessed=size, transcendentals=exps),
    )(*operands)


def rotary_tables(positions):
    freqs = 500000.0 ** (-(jnp.arange(HALF, dtype=jnp.float32) * 2.0 / HD))
    angles = positions.astype(jnp.float32)[:, None] * freqs[None, :]
    cosine = jnp.cos(angles)
    sine = jnp.sin(angles)
    return (
        jnp.concatenate([cosine, cosine], axis=1),
        jnp.concatenate([-sine, sine], axis=1),
    )


def summed_lanes(refs, lanes):
    total = refs[0][:, lanes].astype(jnp.float32)
    for ref in refs[1:]:
        total = total + ref[:, lanes].astype(jnp.float32)
    return total


def rotated(values, cos_ref, sin_ref):
    return values * cos_ref[...] + pltpu.roll(values, HALF, 1) * sin_ref[...]


def pair_kernel(unused_ref, cos_ref, sin_ref, *refs):
    parts, out_ref = refs[:-1], refs[-1]
    key = rotated(summed_lanes(parts, pl.ds(0, HD)), cos_ref, sin_ref)
    out_ref[:, pl.ds(0, HD)] = key.astype(jnp.bfloat16)
    out_ref[:, pl.ds(HD, HD)] = summed_lanes(parts, pl.ds(HD, HD)).astype(jnp.bfloat16)


def finish_pair(cosine, sine, parts):
    operands = (jnp.zeros((1,), jnp.int32), cosine, sine, *parts)
    shape = jax.ShapeDtypeStruct(parts[0].shape, jnp.bfloat16)
    return local_kernel(pair_kernel, shape, operands, 8 * parts[0].size)


def attention_kernel(blocks, stride, n_query, n_kv, place_ref, cos_ref, sin_ref, *refs):
    query_refs = refs[:n_query]
    kv_refs = refs[n_query : n_query + n_kv]
    out_ref, turned, bias = refs[n_query + n_kv :]
    heads, tokens, _ = turned.shape
    for h in range(heads):
        total = summed_lanes(query_refs, pl.ds(h * HD, HD))
        turned[h] = rotated(total, cos_ref, sin_ref).astype(jnp.bfloat16)
    rows = tokens // blocks
    kv_rows = kv_refs[0].shape[0] // blocks
    documents = place_ref.shape[0] - 1 - n_kv
    scale = HD**-0.5
    for j in range(blocks):
        first = j * rows
        length = kv_rows * (j + 1)
        qpos = lax.broadcasted_iota(jnp.int32, (rows, HD), 0) + (place_ref[0] + j * stride)
        qstart = jnp.zeros_like(qpos)
        for i in range(documents):
            start = place_ref[1 + n_kv + i]
            qstart = jnp.where(qpos >= start, start, qstart)
        span = qpos - qstart
        for d in range(n_kv):
            for b in range(j + 1):
                for c in range(0, kv_rows, HD):
                    kpos = lax.broadcasted_iota(jnp.int32, (rows, HD), 1) + (
                        place_ref[1 + d] + (b * stride + c)
                    )
                    back = qpos - kpos
                    visible = (back >= 0) & (back <= span)
                    bias[:, pl.ds(d * length + b * kv_rows + c, HD)] = jnp.where(
                        visible, 0.0, -jnp.inf
                    )

        def one_head(h, unused):
            query = turned[h, pl.ds(first, rows), :]
            scores = []
            for d in range(n_kv):
                part = lax.dot_general(
                    query,
                    kv_refs[d][pl.ds(0, length), pl.ds(0, HD)],
                    (((1,), (1,)), ((), ())),
                    preferred_element_type=jnp.float32,
                )
                scores.append(part + bias[:, pl.ds(d * length, length)])
            highest = functools.reduce(
                jnp.maximum, [jnp.max(s, axis=1, keepdims=True) for s in scores]
            )
            denominator = 0.0
            mixed = 0.0
            for d in range(n_kv):
                probs = jnp.exp((scores[d] - highest) * scale)
                denominator = denominator + jnp.sum(probs, axis=1, keepdims=True)
                mixed = mixed + jnp.dot(
                    probs.astype(jnp.bfloat16),
                    kv_refs[d][pl.ds(0, length), pl.ds(HD, HD)],
                    preferred_element_type=jnp.float32,
                )
            lanes = pl.ds(pl.multiple_of(h * HD, HD), HD)
            out_ref[pl.ds(first, rows), lanes] = (mixed / denominator).astype(jnp.bfloat16)
            return unused

        lax.fori_loop(0, heads, one_head, 0)


def attention(place, cosine, sine, query_parts, kv_parts, blocks, stride):
    tokens, width = query_parts[0].shape
    heads = width // HD
    keys = sum(part.shape[0] for part in kv_parts)
    return local_kernel(
        functools.partial(attention_kernel, blocks, stride, len(query_parts), len(kv_parts)),
        jax.ShapeDtypeStruct((tokens, width), jnp.bfloat16),
        (place, cosine, sine, *query_parts, *kv_parts),
        32 * tokens * width * keys,
        [
            pltpu.VMEM((heads, tokens, HD), jnp.bfloat16),
            pltpu.VMEM((tokens // blocks, keys), jnp.float32),
        ],
        tokens * heads * keys,
    )


def product_kernel(place_ref, *refs):
    own_ref, half_refs = refs[0], refs[1:3]
    weight_refs, out_refs, gathered = refs[3:8], refs[8:10], refs[10]
    hi = place_ref[0]
    lo = place_ref[1]
    rows, depth = own_ref.shape
    share = weight_refs[3].shape[0]
    gathered[pl.ds(pl.multiple_of(hi * rows, rows), rows), :] = own_ref[...]
    for side, half_ref in enumerate(half_refs):
        first = lax.rem(place_ref[2] + side, 2) * (depth // 2)
        features = pl.ds(pl.multiple_of(first, depth // 2), depth // 2)
        for d in range(1, 4):
            gathered[pl.ds(pl.multiple_of((hi ^ d) * rows, rows), rows), features] = half_ref[
                pl.ds((d - 1) * rows, rows), :
            ]
    for side, out_ref in enumerate(out_refs):
        width = out_ref.shape[1]
        first = (lax.div(hi, 2) ^ side) * place_ref[3] + place_ref[4]
        columns = pl.ds(pl.multiple_of(first, width), width)
        total = 0.0
        for part in range(2):
            for r in range(4):
                if r < 3:
                    weight = weight_refs[r][pl.ds(part * share, share), columns]
                else:
                    weight = weight_refs[3 + part][:, columns]
                block = (lax.rem(hi, 2) ^ part) * 4 + (lo ^ r)
                total = total + jnp.dot(
                    gathered[:, pl.ds(pl.multiple_of(block * share, share), share)],
                    weight,
                    preferred_element_type=jnp.float32,
                )
        out_ref[...] = total.astype(jnp.bfloat16)


def product(index, token_parts, weights, chunk, chunks):
    rows, depth = token_parts[0].shape
    step = weights[0].shape[1] // 2
    width = step // chunks
    place = jnp.concatenate([index, jnp.array([step, chunk * width], jnp.int32)])
    shape = jax.ShapeDtypeStruct((4 * rows, width), jnp.bfloat16)
    return local_kernel(
        product_kernel,
        (shape,) * 2,
        (place, *token_parts, *weights),
        2 * 4 * rows * depth * 2 * width,
        [pltpu.VMEM((4 * rows, depth), jnp.bfloat16)],
    )


def project_kernel(place_ref, *refs):
    attended_refs, weight_refs, out_ref = refs[:4], refs[4:-1], refs[-1]
    hi = place_ref[0]
    kept, columns = out_ref.shape
    rows = pl.ds(pl.multiple_of(place_ref[1] * kept, kept), kept)
    depth = attended_refs[0].shape[1]
    features, width = weight_refs[0].shape
    span = features // 4
    for chip in range(2):
        side = lax.rem(hi, 2) ^ chip
        for r, weight_ref in enumerate(weight_refs):
            total = 0.0
            for k, attended_ref in enumerate(attended_refs):
                first = side * (2 * span) + (lax.div(hi, 2) ^ (k // 2)) * span + (k % 2) * depth
                total = total + jnp.dot(
                    attended_ref[rows, :],
                    weight_ref[pl.ds(pl.multiple_of(first, depth), depth), :],
                    preferred_element_type=jnp.float32,
                )
            place = chip * (columns // 2) + r * width
            out_ref[:, pl.ds(place, width)] = total.astype(out_ref.dtype)


def project(place, attended_parts, weights):
    tokens, depth = attended_parts[0].shape
    width = 2 * len(weights) * weights[0].shape[1]
    return local_kernel(
        project_kernel,
        jax.ShapeDtypeStruct((tokens // 2, width), jnp.bfloat16),
        (place, *attended_parts, *weights),
        2 * (tokens // 2) * 4 * depth * width,
    )


def assemble_kernel(place_ref, *refs):
    piece_refs, out_ref = refs[:-1], refs[-1]
    lo = place_ref[1]
    width = out_ref.shape[1] // 8
    each = 4 // len(piece_refs)
    for chip in range(2):
        for r in range(4):
            out_ref[:, pl.ds(pl.multiple_of((chip * 4 + (lo ^ r)) * width, width), width)] = (
                piece_refs[r // each][:, pl.ds((chip * each + r % each) * width, width)]
            )


def assemble(place, pieces):
    rows = pieces[0].shape[0]
    width = sum(piece.shape[1] for piece in pieces)
    shape = jax.ShapeDtypeStruct((rows, width), jnp.bfloat16)
    return local_kernel(assemble_kernel, shape, (place, *pieces), rows * width)


def normalised(tokens, norm_gain):
    source = tokens.astype(jnp.float32)
    return (
        source * lax.rsqrt(jnp.mean(source * source, axis=1, keepdims=True) + 1e-05) * norm_gain
    ).astype(jnp.bfloat16)


def plain_device(tokens, norm_gain, w_query, w_key, w_value, w_out, doc_starts):
    rows = tokens.shape[0]
    first = lax.axis_index("ctx") * rows
    normed = normalised(tokens, norm_gain)

    def project_with(weight):
        gathered = lax.all_gather(weight, "ctx", axis=0, tiled=True)
        total = jnp.dot(normed, gathered, preferred_element_type=jnp.float32)
        return total.astype(jnp.bfloat16)

    cosine, sine = rotary_tables(first + jnp.arange(rows, dtype=jnp.int32))
    place = jnp.concatenate([jnp.stack([first, jnp.zeros_like(first)]), doc_starts])
    query = project_with(w_query)
    key = project_with(w_key)
    value = project_with(w_value)
    kv_local = w_key.shape[1] // HD
    group = w_query.shape[1] // kv_local
    mixed = []
    for h in range(kv_local):
        lanes = slice(h * HD, (h + 1) * HD)
        pair = jnp.concatenate([key[:, lanes], value[:, lanes]], axis=1)
        pair = lax.all_gather(finish_pair(cosine, sine, [pair]), "ctx", axis=0, tiled=True)
        part = query[:, h * group : (h + 1) * group]
        mixed.append(attention(place, cosine, sine, [part], [pair], 1, 0))
    attended = jnp.concatenate(mixed, axis=1)
    wide = lax.all_gather(w_out, "ctx", axis=1, tiled=True)
    partial_out = jnp.dot(attended, wide, preferred_element_type=jnp.float32)
    return lax.psum_scatter(
        partial_out.astype(jnp.bfloat16), "head", scatter_dimension=1, tiled=True
    )


def after(value, *earlier):
    return lax.optimization_barrier((value, *earlier))[0]


def corner_after(blocks, *earlier):
    return corner([blocks[0], *lax.optimization_barrier((*blocks[1:], *earlier))[:2]])


def beside(block, r):
    return lax.ppermute(block, "lo", [(i, i ^ r) for i in range(4)])


def sides(block):
    return [block, beside(block, 1), beside(block, 2)]


def corner(blocks):
    half = blocks[0].shape[0] // 2
    return [*blocks, beside(blocks[2][:half], 1), beside(blocks[1][half:], 2)]


def along(block, d):
    return lax.ppermute(block, "hi", [(i, i ^ d) for i in range(4)])


def line_device(tokens, norm_gain, w_query, w_key, w_value, w_out, doc_starts):
    rows, features = tokens.shape
    hi = lax.axis_index("hi")
    lo = lax.axis_index("lo")
    core = lax.axis_index("head")
    which_half = lax.div(hi, 2)
    which = lax.rem(hi, 2)
    depth = features // 2
    heads = w_query.shape[1] // 4
    width = heads // 2

    def columns_for(chip, sources, width):
        return jnp.concatenate(
            [
                lax.dynamic_slice_in_dim(w, (2 * z + chip) * width, width, 1)
                for z in range(2)
                for w in sources
            ],
            axis=1,
        )

    def exchanged(sources, width, *earlier):
        came = along(after(columns_for(1 - which, sources, width), *earlier), 1)
        return jnp.concatenate([columns_for(which, sources, width), came], axis=0)

    normed = normalised(tokens, norm_gain)
    own = lax.dynamic_slice_in_dim(normed, which_half * depth, depth, 1)

    def core_half(z):
        return lax.dynamic_slice_in_dim(normed, z * depth + core * (depth // 2), depth // 2, 1)

    near = along(core_half(which_half), 1)
    other = along(core_half(1 - which_half), 2)
    halves = jnp.concatenate([near, other, along(after(other, near), 1)], axis=0)
    token_parts = [own, halves, lax.ppermute(halves, "head", [(0, 1), (1, 0)])]
    index = jnp.stack([hi, lo, core])

    pair_both = exchanged((w_key, w_value), HD)
    pair_weight = corner(sides(pair_both))
    query_both = exchanged((w_query,), heads, pair_both, near)
    query_sides = sides(after(query_both, *pair_weight[3:]))

    row_index = jnp.arange(4 * rows, dtype=jnp.int32)
    cosine, sine = rotary_tables((row_index // rows * 4 + lo) * rows + row_index % rows)

    kept, sent = product(index, token_parts, pair_weight, 0, 1)
    query_weight = corner_after(query_sides, sent)

    def rows_for(chip):
        return jnp.concatenate(
            [lax.dynamic_slice_in_dim(w_out, (2 * z + chip) * heads, heads, 0) for z in range(2)],
            axis=0,
        )

    out_both = jnp.concatenate(
        [rows_for(which), along(after(rows_for(1 - which), sent), 1)], axis=0
    )

    kv_own = finish_pair(cosine, sine, [kept, along(sent, 2)])
    kv_going = after(kv_own, *query_weight[3:])
    kv_parts = [kv_own] + [beside(kv_going, r) for r in range(1, 4)]

    firsts = jnp.stack([lo, lo, lo ^ 1, lo ^ 2, lo ^ 3]) * rows
    seen = jnp.concatenate([firsts, doc_starts])
    out_sides = sides(after(out_both, *kv_parts[1:]))
    one = product(index, token_parts, query_weight, 0, 2)
    two = product(index, token_parts, [after(query_weight[0], *one), *query_weight[1:]], 1, 2)
    attended = []
    for kept, sent in ((after(one[0], two[0]), one[1]), two):
        query_parts = [after(kept, *attended[1:]), along(sent, 2)]
        attended.append(attention(seen, cosine, sine, query_parts, kv_parts, 4, 4 * rows))
        attended.append(along(attended[-1], 2))
    attended = [attended[0], attended[2], attended[1], attended[3]]
    out_blocks = corner_after(out_sides, *attended[:2])
    out_blocks[3:] = [jnp.concatenate(out_blocks[3:], axis=0)]
    out_blocks[0] = after(out_blocks[0], out_blocks[3])

    def added(one, two):
        return (one.astype(jnp.float32) + two.astype(jnp.float32)).astype(jnp.bfloat16)

    home = [
        ((2 * half + chip) * 2 + group, (2 * group + chip) * 2 + half)
        for half in range(2)
        for chip in range(2)
        for group in range(2)
    ]
    pieces, shares, summed = [], [], None
    for blocks in (out_blocks[:2], out_blocks[2:]):
        first = [after(blocks[0], *shares[1:]), *blocks[1:]]
        theirs = project(jnp.stack([hi, 1 - core]), attended, first)
        last = first if summed is None else [after(first[0], summed), *first[1:]]
        mine = project(jnp.stack([hi, core]), attended, last)
        theirs = lax.ppermute(theirs, "head", [(0, 1), (1, 0)])
        shares = [
            added(
                lax.dynamic_slice_in_dim(mine, chip * rows, rows, 0),
                lax.dynamic_slice_in_dim(theirs, chip * rows, rows, 0),
            )
            for chip in (which, 1 - which)
        ]
        summed = added(shares[0], along(shares[1], 1))
        pieces.append(lax.ppermute(summed, ("hi", "head"), home))
    return assemble(index, pieces)


def solution(mesh):
    ctx = mesh.shape["ctx"]
    heads = mesh.shape["head"]

    def run(tokens, norm_gain, w_query, w_key, w_value, w_out, doc_starts):
        lines = w_key.shape[1] // HD // heads
        if (ctx, heads, lines) == (16, 2, 4):
            both = ("hi", "lo")
            grid = Mesh(mesh.devices.reshape(4, 4, 2), ("hi", "lo", "head"))
            body = line_device
        else:
            both, grid, body = "ctx", mesh, plain_device
        placed = (
            P(both, None),
            P(),
            P(both, "head"),
            P(both, "head"),
            P(both, "head"),
            P("head", both),
            P(),
        )
        return jax.shard_map(
            body, mesh=grid, in_specs=placed, out_specs=P(both, "head"), check_vma=False
        )(tokens, norm_gain, w_query, w_key, w_value, w_out, doc_starts)

    return run
```

```python
import functools

import jax
import jax.numpy as jnp
from jax import lax
from jax.experimental import pallas as pl
from jax.experimental.pallas import tpu as pltpu
from jax.sharding import Mesh
from jax.sharding import PartitionSpec as P

HD = 128
HALF = HD // 2
MIB = 1024 * 1024


def local_kernel(body, out_shape, operands, flops, scratch=(), exps=0):
    size = sum(x.size * x.dtype.itemsize for x in operands)
    return pl.pallas_call(
        body,
        in_specs=[pl.BlockSpec(memory_space=pltpu.SMEM)]
        + [pl.BlockSpec(memory_space=pltpu.VMEM)] * (len(operands) - 1),
        out_shape=out_shape,
        scratch_shapes=scratch,
        compiler_params=pltpu.CompilerParams(vmem_limit_bytes=12 * MIB),
        cost_estimate=pl.CostEstimate(flops=flops, bytes_accessed=size, transcendentals=exps),
    )(*operands)


def rotary_tables(positions):
    freqs = 500000.0 ** (-(jnp.arange(HALF, dtype=jnp.float32) * 2.0 / HD))
    angles = positions.astype(jnp.float32)[:, None] * freqs[None, :]
    cosine = jnp.cos(angles)
    sine = jnp.sin(angles)
    return (
        jnp.concatenate([cosine, cosine], axis=1),
        jnp.concatenate([-sine, sine], axis=1),
    )


def summed_lanes(refs, lanes):
    total = refs[0][:, lanes].astype(jnp.float32)
    for ref in refs[1:]:
        total = total + ref[:, lanes].astype(jnp.float32)
    return total


def rotated(values, cos_ref, sin_ref):
    return values * cos_ref[...] + pltpu.roll(values, HALF, 1) * sin_ref[...]


def pair_kernel(unused_ref, cos_ref, sin_ref, *refs):
    parts, out_ref = refs[:-1], refs[-1]
    key = rotated(summed_lanes(parts, pl.ds(0, HD)), cos_ref, sin_ref)
    out_ref[:, pl.ds(0, HD)] = key.astype(jnp.bfloat16)
    out_ref[:, pl.ds(HD, HD)] = summed_lanes(parts, pl.ds(HD, HD)).astype(jnp.bfloat16)


def finish_pair(cosine, sine, parts):
    operands = (jnp.zeros((1,), jnp.int32), cosine, sine, *parts)
    shape = jax.ShapeDtypeStruct(parts[0].shape, jnp.bfloat16)
    return local_kernel(pair_kernel, shape, operands, 8 * parts[0].size)


def attention_kernel(blocks, stride, n_query, n_kv, place_ref, cos_ref, sin_ref, *refs):
    query_refs = refs[:n_query]
    kv_refs = refs[n_query : n_query + n_kv]
    out_ref, turned, bias = refs[n_query + n_kv :]
    heads, tokens, _ = turned.shape
    for h in range(heads):
        total = summed_lanes(query_refs, pl.ds(h * HD, HD))
        turned[h] = rotated(total, cos_ref, sin_ref).astype(jnp.bfloat16)
    rows = tokens // blocks
    kv_rows = kv_refs[0].shape[0] // blocks
    documents = place_ref.shape[0] - 1 - n_kv
    scale = HD**-0.5
    for j in range(blocks):
        first = j * rows
        length = kv_rows * (j + 1)
        qpos = lax.broadcasted_iota(jnp.int32, (rows, HD), 0) + (place_ref[0] + j * stride)
        qstart = jnp.zeros_like(qpos)
        for i in range(documents):
            start = place_ref[1 + n_kv + i]
            qstart = jnp.where(qpos >= start, start, qstart)
        span = qpos - qstart
        for d in range(n_kv):
            for b in range(j + 1):
                for c in range(0, kv_rows, HD):
                    kpos = lax.broadcasted_iota(jnp.int32, (rows, HD), 1) + (
                        place_ref[1 + d] + (b * stride + c)
                    )
                    back = qpos - kpos
                    visible = (back >= 0) & (back <= span)
                    bias[:, pl.ds(d * length + b * kv_rows + c, HD)] = jnp.where(
                        visible, 0.0, -jnp.inf
                    )

        def one_head(h, unused):
            query = turned[h, pl.ds(first, rows), :]
            scores = []
            for d in range(n_kv):
                part = lax.dot_general(
                    query,
                    kv_refs[d][pl.ds(0, length), pl.ds(0, HD)],
                    (((1,), (1,)), ((), ())),
                    preferred_element_type=jnp.float32,
                )
                scores.append(part + bias[:, pl.ds(d * length, length)])
            highest = functools.reduce(
                jnp.maximum, [jnp.max(s, axis=1, keepdims=True) for s in scores]
            )
            denominator = 0.0
            mixed = 0.0
            for d in range(n_kv):
                probs = jnp.exp((scores[d] - highest) * scale)
                denominator = denominator + jnp.sum(probs, axis=1, keepdims=True)
                mixed = mixed + jnp.dot(
                    probs.astype(jnp.bfloat16),
                    kv_refs[d][pl.ds(0, length), pl.ds(HD, HD)],
                    preferred_element_type=jnp.float32,
                )
            lanes = pl.ds(pl.multiple_of(h * HD, HD), HD)
            out_ref[pl.ds(first, rows), lanes] = (mixed / denominator).astype(jnp.bfloat16)
            return unused

        lax.fori_loop(0, heads, one_head, 0)


def attention(place, cosine, sine, query_parts, kv_parts, blocks, stride):
    tokens, width = query_parts[0].shape
    heads = width // HD
    keys = sum(part.shape[0] for part in kv_parts)
    return local_kernel(
        functools.partial(attention_kernel, blocks, stride, len(query_parts), len(kv_parts)),
        jax.ShapeDtypeStruct((tokens, width), jnp.bfloat16),
        (place, cosine, sine, *query_parts, *kv_parts),
        32 * tokens * width * keys,
        [
            pltpu.VMEM((heads, tokens, HD), jnp.bfloat16),
            pltpu.VMEM((tokens // blocks, keys), jnp.float32),
        ],
        tokens * heads * keys,
    )


def product_kernel(place_ref, *refs):
    own_ref, half_refs = refs[0], refs[1:3]
    weight_refs, out_refs, gathered = refs[3:8], refs[8:10], refs[10]
    hi = place_ref[0]
    lo = place_ref[1]
    rows, depth = own_ref.shape
    share = weight_refs[3].shape[0]
    gathered[pl.ds(pl.multiple_of(hi * rows, rows), rows), :] = own_ref[...]
    for side, half_ref in enumerate(half_refs):
        first = lax.rem(place_ref[2] + side, 2) * (depth // 2)
        features = pl.ds(pl.multiple_of(first, depth // 2), depth // 2)
        for d in range(1, 4):
            gathered[pl.ds(pl.multiple_of((hi ^ d) * rows, rows), rows), features] = half_ref[
                pl.ds((d - 1) * rows, rows), :
            ]
    for side, out_ref in enumerate(out_refs):
        width = out_ref.shape[1]
        first = (lax.div(hi, 2) ^ side) * place_ref[3] + place_ref[4]
        columns = pl.ds(pl.multiple_of(first, width), width)
        total = 0.0
        for part in range(2):
            for r in range(4):
                if r < 3:
                    weight = weight_refs[r][pl.ds(part * share, share), columns]
                else:
                    weight = weight_refs[3 + part][:, columns]
                block = (lax.rem(hi, 2) ^ part) * 4 + (lo ^ r)
                total = total + jnp.dot(
                    gathered[:, pl.ds(pl.multiple_of(block * share, share), share)],
                    weight,
                    preferred_element_type=jnp.float32,
                )
        out_ref[...] = total.astype(jnp.bfloat16)


def product(index, token_parts, weights, chunk, chunks):
    rows, depth = token_parts[0].shape
    step = weights[0].shape[1] // 2
    width = step // chunks
    place = jnp.concatenate([index, jnp.array([step, chunk * width], jnp.int32)])
    shape = jax.ShapeDtypeStruct((4 * rows, width), jnp.bfloat16)
    return local_kernel(
        product_kernel,
        (shape,) * 2,
        (place, *token_parts, *weights),
        2 * 4 * rows * depth * 2 * width,
        [pltpu.VMEM((4 * rows, depth), jnp.bfloat16)],
    )


def project_kernel(place_ref, *refs):
    attended_refs, weight_refs, out_ref = refs[:4], refs[4:-1], refs[-1]
    hi = place_ref[0]
    kept, columns = out_ref.shape
    rows = pl.ds(pl.multiple_of(place_ref[1] * kept, kept), kept)
    depth = attended_refs[0].shape[1]
    features, width = weight_refs[0].shape
    span = features // 4
    for chip in range(2):
        side = lax.rem(hi, 2) ^ chip
        for r, weight_ref in enumerate(weight_refs):
            total = 0.0
            for k, attended_ref in enumerate(attended_refs):
                first = side * (2 * span) + (lax.div(hi, 2) ^ (k // 2)) * span + (k % 2) * depth
                total = total + jnp.dot(
                    attended_ref[rows, :],
                    weight_ref[pl.ds(pl.multiple_of(first, depth), depth), :],
                    preferred_element_type=jnp.float32,
                )
            place = chip * (columns // 2) + r * width
            out_ref[:, pl.ds(place, width)] = total.astype(out_ref.dtype)


def project(place, attended_parts, weights):
    tokens, depth = attended_parts[0].shape
    width = 2 * len(weights) * weights[0].shape[1]
    return local_kernel(
        project_kernel,
        jax.ShapeDtypeStruct((tokens // 2, width), jnp.bfloat16),
        (place, *attended_parts, *weights),
        2 * (tokens // 2) * 4 * depth * width,
    )


def assemble_kernel(place_ref, *refs):
    piece_refs, out_ref = refs[:-1], refs[-1]
    lo = place_ref[1]
    width = out_ref.shape[1] // 8
    each = 4 // len(piece_refs)
    for chip in range(2):
        for r in range(4):
            out_ref[:, pl.ds(pl.multiple_of((chip * 4 + (lo ^ r)) * width, width), width)] = (
                piece_refs[r // each][:, pl.ds((chip * each + r % each) * width, width)]
            )


def assemble(place, pieces):
    rows = pieces[0].shape[0]
    width = sum(piece.shape[1] for piece in pieces)
    shape = jax.ShapeDtypeStruct((rows, width), jnp.bfloat16)
    return local_kernel(assemble_kernel, shape, (place, *pieces), rows * width)


def normalised(tokens, norm_gain):
    source = tokens.astype(jnp.float32)
    return (
        source * lax.rsqrt(jnp.mean(source * source, axis=1, keepdims=True) + 1e-05) * norm_gain
    ).astype(jnp.bfloat16)


def plain_device(tokens, norm_gain, w_query, w_key, w_value, w_out, doc_starts):
    rows = tokens.shape[0]
    first = lax.axis_index("ctx") * rows
    normed = normalised(tokens, norm_gain)

    def project_with(weight):
        gathered = lax.all_gather(weight, "ctx", axis=0, tiled=True)
        total = jnp.dot(normed, gathered, preferred_element_type=jnp.float32)
        return total.astype(jnp.bfloat16)

    cosine, sine = rotary_tables(first + jnp.arange(rows, dtype=jnp.int32))
    place = jnp.concatenate([jnp.stack([first, jnp.zeros_like(first)]), doc_starts])
    query = project_with(w_query)
    key = project_with(w_key)
    value = project_with(w_value)
    kv_local = w_key.shape[1] // HD
    group = w_query.shape[1] // kv_local
    mixed = []
    for h in range(kv_local):
        lanes = slice(h * HD, (h + 1) * HD)
        pair = jnp.concatenate([key[:, lanes], value[:, lanes]], axis=1)
        pair = lax.all_gather(finish_pair(cosine, sine, [pair]), "ctx", axis=0, tiled=True)
        part = query[:, h * group : (h + 1) * group]
        mixed.append(attention(place, cosine, sine, [part], [pair], 1, 0))
    attended = jnp.concatenate(mixed, axis=1)
    wide = lax.all_gather(w_out, "ctx", axis=1, tiled=True)
    partial_out = jnp.dot(attended, wide, preferred_element_type=jnp.float32)
    return lax.psum_scatter(
        partial_out.astype(jnp.bfloat16), "head", scatter_dimension=1, tiled=True
    )


def after(value, *earlier):
    return lax.optimization_barrier((value, *earlier))[0]


def corner_after(blocks, *earlier):
    return corner([blocks[0], *lax.optimization_barrier((*blocks[1:], *earlier))[:2]])


def beside(block, r):
    return lax.ppermute(block, "lo", [(i, i ^ r) for i in range(4)])


def sides(block):
    return [block, beside(block, 1), beside(block, 2)]


def corner(blocks):
    half = blocks[0].shape[0] // 2
    return [*blocks, beside(blocks[2][:half], 1), beside(blocks[1][half:], 2)]


def along(block, d):
    return lax.ppermute(block, "hi", [(i, i ^ d) for i in range(4)])


def line_device(tokens, norm_gain, w_query, w_key, w_value, w_out, doc_starts):
    rows, features = tokens.shape
    hi = lax.axis_index("hi")
    lo = lax.axis_index("lo")
    core = lax.axis_index("head")
    which_half = lax.div(hi, 2)
    which = lax.rem(hi, 2)
    depth = features // 2
    heads = w_query.shape[1] // 4
    width = heads // 2

    def columns_for(chip, sources, width):
        return jnp.concatenate(
            [
                lax.dynamic_slice_in_dim(w, (2 * z + chip) * width, width, 1)
                for z in range(2)
                for w in sources
            ],
            axis=1,
        )

    def exchanged(sources, width, *earlier):
        came = along(after(columns_for(1 - which, sources, width), *earlier), 1)
        return jnp.concatenate([columns_for(which, sources, width), came], axis=0)

    pair_both = exchanged((w_key, w_value), HD)
    pair_weight = corner(sides(pair_both))
    query_both = exchanged((w_query,), heads, pair_both)
    query_sides = sides(after(query_both, *pair_weight[3:]))

    normed = normalised(tokens, norm_gain)
    own = lax.dynamic_slice_in_dim(normed, which_half * depth, depth, 1)

    def core_half(z):
        return lax.dynamic_slice_in_dim(normed, z * depth + core * (depth // 2), depth // 2, 1)

    near = along(core_half(which_half), 1)
    other = along(core_half(1 - which_half), 2)
    halves = jnp.concatenate([near, other, along(after(other, near), 1)], axis=0)
    token_parts = [own, halves, lax.ppermute(halves, "head", [(0, 1), (1, 0)])]
    index = jnp.stack([hi, lo, core])

    row_index = jnp.arange(4 * rows, dtype=jnp.int32)
    cosine, sine = rotary_tables((row_index // rows * 4 + lo) * rows + row_index % rows)

    kept, sent = product(index, token_parts, pair_weight, 0, 1)
    query_weight = corner_after(query_sides, sent)

    def rows_for(chip):
        return jnp.concatenate(
            [lax.dynamic_slice_in_dim(w_out, (2 * z + chip) * heads, heads, 0) for z in range(2)],
            axis=0,
        )

    out_both = jnp.concatenate(
        [rows_for(which), along(after(rows_for(1 - which), sent), 1)], axis=0
    )

    kv_own = finish_pair(cosine, sine, [kept, along(sent, 2)])
    kv_going = after(kv_own, *query_weight[3:])
    kv_parts = [kv_own] + [beside(kv_going, r) for r in range(1, 4)]

    firsts = jnp.stack([lo, lo, lo ^ 1, lo ^ 2, lo ^ 3]) * rows
    seen = jnp.concatenate([firsts, doc_starts])
    out_sides = sides(after(out_both, *kv_parts[1:]))
    products = [product(index, token_parts, query_weight, c, 2) for c in range(2)]
    products[0] = (after(products[0][0], products[1][0]), products[0][1])
    attended = [
        attention(seen, cosine, sine, [kept, along(sent, 2)], kv_parts, 4, 4 * rows)
        for kept, sent in products
    ]
    out_blocks = corner_after(out_sides, *attended)
    out_blocks[3:] = [jnp.concatenate(out_blocks[3:], axis=0)]
    out_blocks[0] = after(out_blocks[0], out_blocks[3])
    attended += [along(chunk, 2) for chunk in attended]

    def added(one, two):
        return (one.astype(jnp.float32) + two.astype(jnp.float32)).astype(jnp.bfloat16)

    home = [
        ((2 * half + chip) * 2 + group, (2 * group + chip) * 2 + half)
        for half in range(2)
        for chip in range(2)
        for group in range(2)
    ]
    pieces, shares = [], []
    for blocks in (out_blocks[:2], out_blocks[2:]):
        blocks = [after(blocks[0], *shares[1:]), *blocks[1:]]
        theirs = project(jnp.stack([hi, 1 - core]), attended, blocks)
        mine = project(jnp.stack([hi, core]), attended, blocks)
        theirs = lax.ppermute(theirs, "head", [(0, 1), (1, 0)])
        shares = [
            added(
                lax.dynamic_slice_in_dim(mine, chip * rows, rows, 0),
                lax.dynamic_slice_in_dim(theirs, chip * rows, rows, 0),
            )
            for chip in (which, 1 - which)
        ]
        summed = added(shares[0], along(shares[1], 1))
        pieces.append(lax.ppermute(summed, ("hi", "head"), home))
    return assemble(index, pieces)


def solution(mesh):
    ctx = mesh.shape["ctx"]
    heads = mesh.shape["head"]

    def run(tokens, norm_gain, w_query, w_key, w_value, w_out, doc_starts):
        lines = w_key.shape[1] // HD // heads
        if (ctx, heads, lines) == (16, 2, 4):
            both = ("hi", "lo")
            grid = Mesh(mesh.devices.reshape(4, 4, 2), ("hi", "lo", "head"))
            body = line_device
        else:
            both, grid, body = "ctx", mesh, plain_device
        placed = (
            P(both, None),
            P(),
            P(both, "head"),
            P(both, "head"),
            P(both, "head"),
            P("head", both),
            P(),
        )
        return jax.shard_map(
            body, mesh=grid, in_specs=placed, out_specs=P(both, "head"), check_vma=False
        )(tokens, norm_gain, w_query, w_key, w_value, w_out, doc_starts)

    return run
```

```python
import functools

import jax
import jax.numpy as jnp
from jax import lax
from jax.experimental import pallas as pl
from jax.experimental.pallas import tpu as pltpu
from jax.sharding import Mesh
from jax.sharding import PartitionSpec as P

HD = 128
HALF = HD // 2
MIB = 1024 * 1024


def local_kernel(body, out_shape, operands, flops, scratch=(), exps=0, limit=12):
    size = sum(x.size * x.dtype.itemsize for x in operands)
    return pl.pallas_call(
        body,
        in_specs=[pl.BlockSpec(memory_space=pltpu.SMEM)]
        + [pl.BlockSpec(memory_space=pltpu.VMEM)] * (len(operands) - 1),
        out_shape=out_shape,
        scratch_shapes=scratch,
        compiler_params=pltpu.CompilerParams(vmem_limit_bytes=limit * MIB),
        cost_estimate=pl.CostEstimate(flops=flops, bytes_accessed=size, transcendentals=exps),
    )(*operands)


def rotary_tables(positions):
    freqs = 500000.0 ** (-(jnp.arange(HALF, dtype=jnp.float32) * 2.0 / HD))
    angles = positions.astype(jnp.float32)[:, None] * freqs[None, :]
    cosine = jnp.cos(angles)
    sine = jnp.sin(angles)
    return (
        jnp.concatenate([cosine, cosine], axis=1),
        jnp.concatenate([-sine, sine], axis=1),
    )


def summed_lanes(refs, lanes):
    total = refs[0][:, lanes].astype(jnp.float32)
    for ref in refs[1:]:
        total = total + ref[:, lanes].astype(jnp.float32)
    return total


def rotated(values, cos_ref, sin_ref):
    return values * cos_ref[...] + pltpu.roll(values, HALF, 1) * sin_ref[...]


def pair_kernel(unused_ref, cos_ref, sin_ref, *refs):
    parts, out_ref = refs[:-1], refs[-1]
    key = rotated(summed_lanes(parts, pl.ds(0, HD)), cos_ref, sin_ref)
    out_ref[:, pl.ds(0, HD)] = key.astype(jnp.bfloat16)
    out_ref[:, pl.ds(HD, HD)] = summed_lanes(parts, pl.ds(HD, HD)).astype(jnp.bfloat16)


def finish_pair(cosine, sine, parts):
    operands = (jnp.zeros((1,), jnp.int32), cosine, sine, *parts)
    shape = jax.ShapeDtypeStruct(parts[0].shape, jnp.bfloat16)
    return local_kernel(pair_kernel, shape, operands, 8 * parts[0].size)


def attention_kernel(blocks, stride, n_query, n_kv, place_ref, cos_ref, sin_ref, *refs):
    query_refs = refs[:n_query]
    kv_refs = refs[n_query : n_query + n_kv]
    out_ref, turned, bias = refs[n_query + n_kv :]
    heads, tokens, _ = turned.shape
    for h in range(heads):
        total = summed_lanes(query_refs, pl.ds(h * HD, HD))
        turned[h] = rotated(total, cos_ref, sin_ref).astype(jnp.bfloat16)
    rows = tokens // blocks
    kv_rows = kv_refs[0].shape[0] // blocks
    documents = place_ref.shape[0] - 1 - n_kv
    scale = HD**-0.5
    for j in range(blocks):
        first = j * rows
        length = kv_rows * (j + 1)
        qpos = lax.broadcasted_iota(jnp.int32, (rows, HD), 0) + (place_ref[0] + j * stride)
        qstart = jnp.zeros_like(qpos)
        for i in range(documents):
            start = place_ref[1 + n_kv + i]
            qstart = jnp.where(qpos >= start, start, qstart)
        span = qpos - qstart
        for d in range(n_kv):
            for b in range(j + 1):
                for c in range(0, kv_rows, HD):
                    kpos = lax.broadcasted_iota(jnp.int32, (rows, HD), 1) + (
                        place_ref[1 + d] + (b * stride + c)
                    )
                    back = qpos - kpos
                    visible = (back >= 0) & (back <= span)
                    bias[:, pl.ds(d * length + b * kv_rows + c, HD)] = jnp.where(
                        visible, 0.0, -jnp.inf
                    )

        def one_head(h, unused):
            query = turned[h, pl.ds(first, rows), :]
            scores = []
            for d in range(n_kv):
                part = lax.dot_general(
                    query,
                    kv_refs[d][pl.ds(0, length), pl.ds(0, HD)],
                    (((1,), (1,)), ((), ())),
                    preferred_element_type=jnp.float32,
                )
                scores.append(part + bias[:, pl.ds(d * length, length)])
            highest = functools.reduce(
                jnp.maximum, [jnp.max(s, axis=1, keepdims=True) for s in scores]
            )
            denominator = 0.0
            mixed = 0.0
            for d in range(n_kv):
                probs = jnp.exp((scores[d] - highest) * scale)
                denominator = denominator + jnp.sum(probs, axis=1, keepdims=True)
                mixed = mixed + jnp.dot(
                    probs.astype(jnp.bfloat16),
                    kv_refs[d][pl.ds(0, length), pl.ds(HD, HD)],
                    preferred_element_type=jnp.float32,
                )
            lanes = pl.ds(pl.multiple_of(h * HD, HD), HD)
            out_ref[pl.ds(first, rows), lanes] = (mixed / denominator).astype(jnp.bfloat16)
            return unused

        lax.fori_loop(0, heads, one_head, 0)


def attention(place, cosine, sine, query_parts, kv_parts, blocks, stride):
    tokens, width = query_parts[0].shape
    heads = width // HD
    keys = sum(part.shape[0] for part in kv_parts)
    return local_kernel(
        functools.partial(attention_kernel, blocks, stride, len(query_parts), len(kv_parts)),
        jax.ShapeDtypeStruct((tokens, width), jnp.bfloat16),
        (place, cosine, sine, *query_parts, *kv_parts),
        32 * tokens * width * keys,
        [
            pltpu.VMEM((heads, tokens, HD), jnp.bfloat16),
            pltpu.VMEM((tokens // blocks, keys), jnp.float32),
        ],
        tokens * heads * keys,
        limit=8 if len(kv_parts) > 1 else 12,
    )


def product_kernel(place_ref, *refs):
    own_ref, half_refs = refs[0], refs[1:3]
    weight_refs, out_refs, gathered = refs[3:8], refs[8:10], refs[10]
    hi = place_ref[0]
    lo = place_ref[1]
    rows, depth = own_ref.shape
    share = weight_refs[3].shape[0]
    gathered[pl.ds(pl.multiple_of(hi * rows, rows), rows), :] = own_ref[...]
    for side, half_ref in enumerate(half_refs):
        first = lax.rem(place_ref[2] + side, 2) * (depth // 2)
        features = pl.ds(pl.multiple_of(first, depth // 2), depth // 2)
        for d in range(1, 4):
            gathered[pl.ds(pl.multiple_of((hi ^ d) * rows, rows), rows), features] = half_ref[
                pl.ds((d - 1) * rows, rows), :
            ]
    for side, out_ref in enumerate(out_refs):
        width = out_ref.shape[1]
        first = (lax.div(hi, 2) ^ side) * place_ref[3] + place_ref[4]
        columns = pl.ds(pl.multiple_of(first, width), width)
        total = 0.0
        for part in range(2):
            for r in range(4):
                if r < 3:
                    weight = weight_refs[r][pl.ds(part * share, share), columns]
                else:
                    weight = weight_refs[3 + part][:, columns]
                block = (lax.rem(hi, 2) ^ part) * 4 + (lo ^ r)
                total = total + jnp.dot(
                    gathered[:, pl.ds(pl.multiple_of(block * share, share), share)],
                    weight,
                    preferred_element_type=jnp.float32,
                )
        out_ref[...] = total.astype(jnp.bfloat16)


def product(index, token_parts, weights, chunk, chunks):
    rows, depth = token_parts[0].shape
    step = weights[0].shape[1] // 2
    width = step // chunks
    place = jnp.concatenate([index, jnp.array([step, chunk * width], jnp.int32)])
    shape = jax.ShapeDtypeStruct((4 * rows, width), jnp.bfloat16)
    return local_kernel(
        product_kernel,
        (shape,) * 2,
        (place, *token_parts, *weights),
        2 * 4 * rows * depth * 2 * width,
        [pltpu.VMEM((4 * rows, depth), jnp.bfloat16)],
    )


def project_kernel(place_ref, *refs):
    attended_refs, weight_refs, out_ref = refs[:4], refs[4:-1], refs[-1]
    hi = place_ref[0]
    kept, columns = out_ref.shape
    rows = pl.ds(pl.multiple_of(place_ref[1] * kept, kept), kept)
    depth = attended_refs[0].shape[1]
    features, width = weight_refs[0].shape
    span = features // 4
    for chip in range(2):
        side = lax.rem(hi, 2) ^ chip
        for r, weight_ref in enumerate(weight_refs):
            total = 0.0
            for k, attended_ref in enumerate(attended_refs):
                first = side * (2 * span) + (lax.div(hi, 2) ^ (k // 2)) * span + (k % 2) * depth
                total = total + jnp.dot(
                    attended_ref[rows, :],
                    weight_ref[pl.ds(pl.multiple_of(first, depth), depth), :],
                    preferred_element_type=jnp.float32,
                )
            place = chip * (columns // 2) + r * width
            out_ref[:, pl.ds(place, width)] = total.astype(out_ref.dtype)


def project(place, attended_parts, weights):
    tokens, depth = attended_parts[0].shape
    width = 2 * len(weights) * weights[0].shape[1]
    return local_kernel(
        project_kernel,
        jax.ShapeDtypeStruct((tokens // 2, width), jnp.bfloat16),
        (place, *attended_parts, *weights),
        2 * (tokens // 2) * 4 * depth * width,
        limit=6,
    )


def assemble_kernel(place_ref, *refs):
    piece_refs, out_ref = refs[:-1], refs[-1]
    lo = place_ref[1]
    width = out_ref.shape[1] // 8
    each = 4 // len(piece_refs)
    for chip in range(2):
        for r in range(4):
            out_ref[:, pl.ds(pl.multiple_of((chip * 4 + (lo ^ r)) * width, width), width)] = (
                piece_refs[r // each][:, pl.ds((chip * each + r % each) * width, width)]
            )


def assemble(place, pieces):
    rows = pieces[0].shape[0]
    width = sum(piece.shape[1] for piece in pieces)
    shape = jax.ShapeDtypeStruct((rows, width), jnp.bfloat16)
    return local_kernel(assemble_kernel, shape, (place, *pieces), rows * width)


def normalised(tokens, norm_gain):
    source = tokens.astype(jnp.float32)
    return (
        source * lax.rsqrt(jnp.mean(source * source, axis=1, keepdims=True) + 1e-05) * norm_gain
    ).astype(jnp.bfloat16)


def plain_device(tokens, norm_gain, w_query, w_key, w_value, w_out, doc_starts):
    rows = tokens.shape[0]
    first = lax.axis_index("ctx") * rows
    normed = normalised(tokens, norm_gain)

    def project_with(weight):
        gathered = lax.all_gather(weight, "ctx", axis=0, tiled=True)
        total = jnp.dot(normed, gathered, preferred_element_type=jnp.float32)
        return total.astype(jnp.bfloat16)

    cosine, sine = rotary_tables(first + jnp.arange(rows, dtype=jnp.int32))
    place = jnp.concatenate([jnp.stack([first, jnp.zeros_like(first)]), doc_starts])
    query = project_with(w_query)
    key = project_with(w_key)
    value = project_with(w_value)
    kv_local = w_key.shape[1] // HD
    group = w_query.shape[1] // kv_local
    mixed = []
    for h in range(kv_local):
        lanes = slice(h * HD, (h + 1) * HD)
        pair = jnp.concatenate([key[:, lanes], value[:, lanes]], axis=1)
        pair = lax.all_gather(finish_pair(cosine, sine, [pair]), "ctx", axis=0, tiled=True)
        part = query[:, h * group : (h + 1) * group]
        mixed.append(attention(place, cosine, sine, [part], [pair], 1, 0))
    attended = jnp.concatenate(mixed, axis=1)
    wide = lax.all_gather(w_out, "ctx", axis=1, tiled=True)
    partial_out = jnp.dot(attended, wide, preferred_element_type=jnp.float32)
    return lax.psum_scatter(
        partial_out.astype(jnp.bfloat16), "head", scatter_dimension=1, tiled=True
    )


def after(value, *earlier):
    return lax.optimization_barrier((value, *earlier))[0]


def corner_after(blocks, *earlier):
    return corner([blocks[0], *lax.optimization_barrier((*blocks[1:], *earlier))[:2]])


def beside(block, r):
    return lax.ppermute(block, "lo", [(i, i ^ r) for i in range(4)])


def sides(block):
    return [block, beside(block, 1), beside(block, 2)]


def corner(blocks):
    half = blocks[0].shape[0] // 2
    return [*blocks, beside(blocks[2][:half], 1), beside(blocks[1][half:], 2)]


def along(block, d):
    return lax.ppermute(block, "hi", [(i, i ^ d) for i in range(4)])


def line_device(tokens, norm_gain, w_query, w_key, w_value, w_out, doc_starts):
    rows, features = tokens.shape
    hi = lax.axis_index("hi")
    lo = lax.axis_index("lo")
    core = lax.axis_index("head")
    which_half = lax.div(hi, 2)
    which = lax.rem(hi, 2)
    depth = features // 2
    heads = w_query.shape[1] // 4
    width = heads // 2

    def columns_for(chip, sources, width):
        return jnp.concatenate(
            [
                lax.dynamic_slice_in_dim(w, (2 * z + chip) * width, width, 1)
                for z in range(2)
                for w in sources
            ],
            axis=1,
        )

    def exchanged(sources, width, *earlier):
        came = along(after(columns_for(1 - which, sources, width), *earlier), 1)
        return jnp.concatenate([columns_for(which, sources, width), came], axis=0)

    pair_both = exchanged((w_key, w_value), HD)
    pair_weight = corner(sides(pair_both))
    query_both = exchanged((w_query,), heads, pair_both)
    query_sides = sides(after(query_both, *pair_weight[3:]))

    normed = normalised(tokens, norm_gain)
    own = lax.dynamic_slice_in_dim(normed, which_half * depth, depth, 1)

    def core_half(z):
        return lax.dynamic_slice_in_dim(normed, z * depth + core * (depth // 2), depth // 2, 1)

    near = along(core_half(which_half), 1)
    other = along(core_half(1 - which_half), 2)
    halves = jnp.concatenate([near, other, along(after(other, near), 1)], axis=0)
    token_parts = [own, halves, lax.ppermute(halves, "head", [(0, 1), (1, 0)])]
    index = jnp.stack([hi, lo, core])

    row_index = jnp.arange(4 * rows, dtype=jnp.int32)
    cosine, sine = rotary_tables((row_index // rows * 4 + lo) * rows + row_index % rows)

    kept, sent = product(index, token_parts, pair_weight, 0, 1)
    query_weight = corner_after(query_sides, sent)

    def rows_for(chip):
        return jnp.concatenate(
            [lax.dynamic_slice_in_dim(w_out, (2 * z + chip) * heads, heads, 0) for z in range(2)],
            axis=0,
        )

    out_both = jnp.concatenate(
        [rows_for(which), along(after(rows_for(1 - which), sent), 1)], axis=0
    )

    kv_own = finish_pair(cosine, sine, [kept, along(sent, 2)])
    kv_going = after(kv_own, *query_weight[3:])
    kv_parts = [kv_own] + [beside(kv_going, r) for r in range(1, 4)]

    firsts = jnp.stack([lo, lo, lo ^ 1, lo ^ 2, lo ^ 3]) * rows
    seen = jnp.concatenate([firsts, doc_starts])
    out_sides = sides(after(out_both, *kv_parts[1:]))
    products = [product(index, token_parts, query_weight, c, 2) for c in range(2)]
    products[0] = (after(products[0][0], products[1][0]), products[0][1])
    attended = [
        attention(seen, cosine, sine, [kept, along(sent, 2)], kv_parts, 4, 4 * rows)
        for kept, sent in products
    ]
    out_blocks = corner_after(out_sides, *attended)
    out_blocks[3:] = [jnp.concatenate(out_blocks[3:], axis=0)]
    out_blocks[0] = after(out_blocks[0], out_blocks[3])
    attended += [along(chunk, 2) for chunk in attended]

    def added(one, two):
        return (one.astype(jnp.float32) + two.astype(jnp.float32)).astype(jnp.bfloat16)

    home = [
        ((2 * half + chip) * 2 + group, (2 * group + chip) * 2 + half)
        for half in range(2)
        for chip in range(2)
        for group in range(2)
    ]
    pieces, shares = [], []
    for blocks in (out_blocks[:2], out_blocks[2:]):
        blocks = [after(blocks[0], *shares[1:]), *blocks[1:]]
        theirs = project(jnp.stack([hi, 1 - core]), attended, blocks)
        mine = project(jnp.stack([hi, core]), attended, blocks)
        theirs = lax.ppermute(theirs, "head", [(0, 1), (1, 0)])
        shares = [
            added(
                lax.dynamic_slice_in_dim(mine, chip * rows, rows, 0),
                lax.dynamic_slice_in_dim(theirs, chip * rows, rows, 0),
            )
            for chip in (which, 1 - which)
        ]
        summed = added(shares[0], along(shares[1], 1))
        pieces.append(lax.ppermute(summed, ("hi", "head"), home))
    return assemble(index, pieces)


def solution(mesh):
    ctx = mesh.shape["ctx"]
    heads = mesh.shape["head"]

    def run(tokens, norm_gain, w_query, w_key, w_value, w_out, doc_starts):
        lines = w_key.shape[1] // HD // heads
        if (ctx, heads, lines) == (16, 2, 4):
            both = ("hi", "lo")
            grid = Mesh(mesh.devices.reshape(4, 4, 2), ("hi", "lo", "head"))
            body = line_device
        else:
            both, grid, body = "ctx", mesh, plain_device
        placed = (
            P(both, None),
            P(),
            P(both, "head"),
            P(both, "head"),
            P(both, "head"),
            P("head", both),
            P(),
        )
        return jax.shard_map(
            body, mesh=grid, in_specs=placed, out_specs=P(both, "head"), check_vma=False
        )(tokens, norm_gain, w_query, w_key, w_value, w_out, doc_starts)

    return run
```
